32 devices in a mesh: parts: 2 (over y), expert: 16 (over z, x, core), dp: 1.
Axes of the slice: x: 2, y: 2, z: 4, core: 2. Of those that a mesh axis runs over, the one named last changes fastest.
Arguments:
- tokens: bfloat16 [2048, 2048], P(('parts', 'expert', 'dp')), parts along dimension 0, may hold values from -6 to 6
- expert_ids: int32 [2048, 8], P(('parts', 'expert', 'dp')), parts along dimension 0, may hold values from 0 to 15, all different within a row; in each aligned block of 64 rows (0 to 63, 64 to 127, ...) at most 64 rows name the same one
- router_weights: float32 [2048, 8], P(('parts', 'expert', 'dp')), parts along dimension 0, may hold values from 0.1 to 1
- w_gate: bfloat16 [16, 2048, 768], P('expert', None, 'dp'), may hold values from -0.125 to 0.125
- w_up: bfloat16 [16, 2048, 768], P('expert', None, 'dp'), may hold values from -0.125 to 0.125
- w_down: bfloat16 [16, 2048, 768], P('expert', None, 'dp'), may hold values from -0.21875 to 0.21875
Outputs:
- mixed: bfloat16 [2048, 2048], P(('parts', 'expert', 'dp')), parts along dimension 0
The draws below stay inside these ranges and needn't reach their ends.
There are 2 independent parts, one for each index of `parts`. The reference program is written for one: setup_inputs(seed, part) draws one part's arguments, and reference() takes and returns one part's arrays. A program takes and returns all parts, laid end to end along the dimension named above; an argument that names none is the same for every part. Nothing has to cross between parts.
Inputs may be any that keep to these rules, and one draw needn't show every extreme that they name: `expert_ids`: each token names 8 different experts. Among the 64 tokens of one device no expert is named more than 64 times, and in every draw some expert is named exactly 64 times by the tokens of some device.
All inputs are finite; a program needn't handle non-finite values.
Results may differ from the reference program's by a relative error of at most 0.008.
Values may be sent and summed in bfloat16 or wider, within the bound.
No kernel may reach another device: no remote copies, remote signals or barrier semaphores. Data moves between devices by JAX's collectives and lax.ppermute only.
A program may use at most 128 MiB of HBM per device.

```python
import math
import jax
import jax.numpy as jnp
import numpy as np
from jax import lax

D = 2048
FF = 768
TOP = 8
TOK_DEV = 64
EXPERTS = 16
TOKENS = 1024
CAP = 64
N_EXPERT = 16
N_DP = 1


def block_scale(key, dims, shards, low, high):
    factor_of, own = 1.0, jax.random.fold_in(key, 6)
    for position, shards_of in shards:
        draws = jnp.exp(jax.random.uniform(jax.random.fold_in(own, position), (shards_of,), jnp.float32, low / len(shards), high / len(shards)))
        factor_of = factor_of * jnp.repeat(draws, dims[position] // shards_of).reshape([-1 if axis == position else 1 for axis in range(len(dims))])
    return factor_of


def deal_out(rng, own, number, rows, number_of, top, limit, skew):
    order = jax.random.permutation(rng, number_of)
    packed, ordinary = portions_of(number_of, rows * top, limit, skew, True), portions_of(number_of, rows * top, limit, skew, False)
    places = jnp.arange(number_of)

    def named(sizes, turn):
        used = int((sizes > 0).sum())
        fixed = max(1, used // 4)
        shifted = fixed + (places - fixed + turn * (used - fixed)) % max(1, number_of - fixed)
        return jnp.zeros((number_of,), jnp.int32).at[order[jnp.where(places < fixed, places, shifted)]].set(jnp.asarray(sizes, jnp.int32))

    sizes = jnp.where(number % 4 == 0, named(packed, number // 4), named(ordinary, number - number // 4 - 1))
    mixed = jax.random.permutation(jax.random.fold_in(own, 3), number_of)
    source_of, sink = mixed[0:number_of // 2 * 2:2], mixed[1:number_of // 2 * 2:2]
    room = jnp.minimum(sizes[source_of] - 1, limit - sizes[sink]) // 2
    room = jnp.where((source_of == order[0]) | (sink == order[0]) | (sizes[sink] == 0), 0, jnp.maximum(room, 0))
    shifted = jax.random.randint(jax.random.fold_in(own, 4), (number_of // 2,), 0, 1 << 20) % (room + 1)
    sizes = sizes.at[source_of].add(-shifted).at[sink].add(shifted)
    items = jnp.searchsorted(jnp.cumsum(sizes), jnp.arange(rows * top), side="right").astype(jnp.int32)
    grid = items.reshape(top, rows).T
    grid = grid[jax.random.permutation(jax.random.fold_in(own, 1), rows)]
    turn = jax.random.randint(jax.random.fold_in(own, 2), (rows, 1), 0, top)
    return jnp.take_along_axis(grid, (jnp.arange(top)[None, :] + turn) % top, axis=1)


def portions_of(number_of, total, bound, slope, full):
    portions = [(1 << 20) // math.isqrt(rank ** slope) + 1 for rank in range(1, number_of + 1)]
    largest = bound if full else min(bound, max(-(-total // number_of), total * portions[0] // sum(portions)))
    least = 1 if total - largest >= number_of - 1 else 0
    counts, surplus = [largest] + [least] * (number_of - 1), total - largest - least * (number_of - 1)
    while surplus > 0:
        free = [i for i in range(1, number_of) if counts[i] < largest] or [i for i in range(1, number_of) if counts[i] < bound]
        mass, remaining = sum([portions[i] for i in free]), surplus
        for i in free:
            more = min(bound - counts[i], max(1, remaining * portions[i] // mass), surplus)
            counts[i] = counts[i] + more
            surplus = surplus - more
    return np.array(counts)


def noise(stream_key, shape, scale, reach, cuts=(), kind=jnp.bfloat16):
    gain = block_scale(stream_key, shape, cuts, -0.22, 0.18) if cuts else 1.0
    values = jax.random.normal(stream_key, shape, jnp.float32) * scale * gain
    return jnp.minimum(jnp.maximum(values, -reach), reach).astype(kind)


def setup_inputs(seed: int = 0, part: int = 0) -> dict:
    streams_of = jax.random.split(jax.random.key(seed), 7)
    own_keys = jax.random.split(jax.random.fold_in(streams_of[6], part), 7)
    tokens = noise(own_keys[0], (TOKENS, D), 1.0, 6.0, ((0, 16),))
    expert_ids_keys = jax.random.split(jax.random.fold_in(own_keys[1], 1), TOKENS // TOK_DEV)
    expert_ids_turns = jax.random.permutation(jax.random.fold_in(own_keys[1], 3), TOKENS // TOK_DEV)
    expert_ids = jax.vmap(lambda own, number: deal_out(jax.random.fold_in(own_keys[1], 2), own, number, TOK_DEV, EXPERTS, TOP, CAP, 2))(expert_ids_keys, expert_ids_turns).reshape((TOKENS, TOP))
    router_weights = jnp.clip(jnp.exp(math.log(1.0) - 2.3025851 * jax.random.uniform(own_keys[2], (TOKENS, TOP), jnp.float32) ** block_scale(own_keys[2], (TOKENS, TOP), ((0, 16),), -0.2, 0.2)), 0.1, 1.0)
    w_gate = noise(streams_of[3], (EXPERTS, D, FF), D ** -0.5, 0.125, ((0, 16),))
    w_up = noise(streams_of[4], (EXPERTS, D, FF), D ** -0.5, 0.125, ((0, 16),))
    w_down = noise(streams_of[5], (EXPERTS, D, FF), FF ** -0.5, 0.21875, ((0, 16),))
    return {"tokens": tokens, "expert_ids": expert_ids, "router_weights": router_weights, "w_gate": w_gate, "w_up": w_up, "w_down": w_down}


def reference(tokens, expert_ids, router_weights, w_gate, w_up, w_down):
    maxrows = CAP * N_EXPERT * N_DP
    block = math.gcd(maxrows, 128)
    padded = jnp.concatenate([tokens, jnp.zeros((1, D), jnp.bfloat16)], 0)

    def step(accum, inputs):
        expert, gate_w, up_w, down_w = inputs
        chosen = expert_ids == expert
        weight = jnp.sum(jnp.where(chosen, router_weights, jnp.zeros_like(router_weights)), 1)
        member = jnp.any(chosen, 1)
        count = jnp.sum(member.astype(jnp.int32))
        where_rows = jnp.nonzero(member, size=maxrows, fill_value=TOKENS)[0].astype(jnp.int32)
        rows = padded[where_rows]

        def run(block_rows):
            gate_val = jnp.dot(block_rows, gate_w, preferred_element_type=jnp.float32)
            up_val = jnp.dot(block_rows, up_w, preferred_element_type=jnp.float32)
            hidden = (jax.nn.silu(gate_val) * up_val).astype(jnp.bfloat16)
            return jnp.dot(hidden, down_w.T, preferred_element_type=jnp.float32)

        def empty(block_rows):
            return jnp.zeros((block_rows.shape[0], D), jnp.float32)

        pieces = []
        for index in range(maxrows // block):
            block_rows = rows[index * block:(index + 1) * block]
            pieces.append(lax.cond(index * block < count, run, empty, block_rows))
        expert_out = lax.optimization_barrier(jnp.concatenate(pieces, 0).astype(jnp.bfloat16))
        weights_pad = jnp.concatenate([weight, jnp.zeros((1,), weight.dtype)], 0)[where_rows]
        accum = accum.at[where_rows].add(weights_pad[:, None] * expert_out.astype(jnp.float32))
        return accum, None

    start = jnp.zeros((TOKENS + 1, D), jnp.float32)
    total, unused = lax.scan(step, start, (jnp.arange(EXPERTS, dtype=jnp.int32), w_gate, w_up, w_down))
    return total[:TOKENS].astype(jnp.bfloat16)
```

```python
import math

import jax
import jax.numpy as jnp
from jax import lax
from jax.sharding import PartitionSpec as P


def expert_rows(rows, gate_w, up_w, down_w):
    total = rows.shape[0]
    block = math.gcd(total, 128)
    pieces = []
    for index in range(total // block):
        block_rows = rows[index * block : (index + 1) * block]
        gate_val = jnp.dot(block_rows, gate_w, preferred_element_type=jnp.float32)
        up_val = jnp.dot(block_rows, up_w, preferred_element_type=jnp.float32)
        hidden = (jax.nn.silu(gate_val) * up_val).astype(jnp.bfloat16)
        pieces.append(
            lax.dot_general(
                hidden, down_w, (((1,), (1,)), ((), ())), preferred_element_type=jnp.float32
            )
        )
    return jnp.concatenate(pieces, 0)


def routed_body(tokens, expert_ids, router_weights, w_gate, w_up, w_down):
    tok_count, top = expert_ids.shape
    width = tokens.shape[1]
    experts = lax.axis_size("expert")
    cap = max(2, min(tok_count, 2 * tok_count * top // experts))
    slots_all = experts * cap
    flat_ids = expert_ids.reshape(-1)
    onehot = (flat_ids[:, None] == jnp.arange(experts, dtype=jnp.int32)[None, :]).astype(jnp.int32)
    before = jnp.cumsum(onehot, 0) - onehot
    position = jnp.sum(before * onehot, 1)
    slot = flat_ids * cap + position
    send = jnp.zeros((slots_all, width), jnp.bfloat16).at[slot].set(jnp.repeat(tokens, top, 0))
    send = send.reshape(experts, cap, width)
    arrived = lax.all_to_all(send, "expert", split_axis=0, concat_axis=0, tiled=True)
    packed = arrived.reshape(slots_all, width)
    result = expert_rows(
        packed,
        lax.all_gather(w_gate, "dp", axis=2, tiled=True)[0],
        lax.all_gather(w_up, "dp", axis=2, tiled=True)[0],
        lax.all_gather(w_down, "dp", axis=2, tiled=True)[0],
    )
    expert_out = result.astype(jnp.bfloat16)
    back = lax.all_to_all(
        expert_out.reshape(experts, cap, width), "expert", split_axis=0, concat_axis=0, tiled=True
    )
    picked = back.reshape(slots_all, width)[slot].reshape(tok_count, top, width)
    mixed = jnp.einsum("tk,tkd->td", router_weights, picked.astype(jnp.float32))
    return mixed.astype(jnp.bfloat16)


def dense_body(tokens, expert_ids, router_weights, w_gate, w_up, w_down):
    experts = lax.axis_size("expert")
    numbers = jnp.arange(experts, dtype=jnp.int32)
    chosen = expert_ids[None, :, :] == numbers[:, None, None]
    weight = jnp.sum(jnp.where(chosen, router_weights[None, :, :], 0.0), 2)
    weight = lax.all_to_all(weight, "expert", split_axis=0, concat_axis=0, tiled=True).reshape(-1)
    rows = lax.all_gather(tokens, "expert", axis=0, tiled=True)
    gate_val = jnp.dot(rows, w_gate[0], preferred_element_type=jnp.float32)
    up_val = jnp.dot(rows, w_up[0], preferred_element_type=jnp.float32)
    hidden = (jax.nn.silu(gate_val) * up_val).astype(jnp.bfloat16)
    out = lax.dot_general(
        hidden, w_down[0], (((1,), (1,)), ((), ())), preferred_element_type=jnp.float32
    )
    out = (out * weight[:, None]).astype(jnp.bfloat16)
    return lax.psum_scatter(out, "expert", scatter_dimension=0, tiled=True)


def solution(mesh):
    in_specs = (
        P(("parts", "expert", "dp"), None),
        P(("parts", "expert", "dp"), None),
        P(("parts", "expert", "dp"), None),
        P("expert", None, "dp"),
        P("expert", None, "dp"),
        P("expert", None, "dp"),
    )
    out_specs = P(("parts", "expert", "dp"), None)

    def whole(tokens, expert_ids, router_weights, w_gate, w_up, w_down):
        few = mesh.shape["dp"] == 1 and 2 * expert_ids.shape[1] >= mesh.shape["expert"]
        body = dense_body if few else routed_body
        return jax.shard_map(
            body, mesh=mesh, in_specs=in_specs, out_specs=out_specs, check_vma=False
        )(tokens, expert_ids, router_weights, w_gate, w_up, w_down)

    return whole
```

```python
import functools
import math

import jax
import jax.numpy as jnp
from jax import lax
from jax.experimental import pallas as pl
from jax.experimental.pallas import tpu as pltpu
from jax.sharding import PartitionSpec as P


def expert_rows(rows, gate_w, up_w, down_w):
    total = rows.shape[0]
    block = math.gcd(total, 128)
    pieces = []
    for index in range(total // block):
        block_rows = rows[index * block : (index + 1) * block]
        gate_val = jnp.dot(block_rows, gate_w, preferred_element_type=jnp.float32)
        up_val = jnp.dot(block_rows, up_w, preferred_element_type=jnp.float32)
        hidden = (jax.nn.silu(gate_val) * up_val).astype(jnp.bfloat16)
        pieces.append(
            lax.dot_general(
                hidden, down_w, (((1,), (1,)), ((), ())), preferred_element_type=jnp.float32
            )
        )
    return jnp.concatenate(pieces, 0)


def routed_body(tokens, expert_ids, router_weights, w_gate, w_up, w_down):
    tok_count, top = expert_ids.shape
    width = tokens.shape[1]
    experts = lax.axis_size("expert")
    cap = max(2, min(tok_count, 2 * tok_count * top // experts))
    slots_all = experts * cap
    flat_ids = expert_ids.reshape(-1)
    onehot = (flat_ids[:, None] == jnp.arange(experts, dtype=jnp.int32)[None, :]).astype(jnp.int32)
    before = jnp.cumsum(onehot, 0) - onehot
    position = jnp.sum(before * onehot, 1)
    slot = flat_ids * cap + position
    send = jnp.zeros((slots_all, width), jnp.bfloat16).at[slot].set(jnp.repeat(tokens, top, 0))
    send = send.reshape(experts, cap, width)
    arrived = lax.all_to_all(send, "expert", split_axis=0, concat_axis=0, tiled=True)
    packed = arrived.reshape(slots_all, width)
    result = expert_rows(
        packed,
        lax.all_gather(w_gate, "dp", axis=2, tiled=True)[0],
        lax.all_gather(w_up, "dp", axis=2, tiled=True)[0],
        lax.all_gather(w_down, "dp", axis=2, tiled=True)[0],
    )
    expert_out = result.astype(jnp.bfloat16)
    back = lax.all_to_all(
        expert_out.reshape(experts, cap, width), "expert", split_axis=0, concat_axis=0, tiled=True
    )
    picked = back.reshape(slots_all, width)[slot].reshape(tok_count, top, width)
    mixed = jnp.einsum("tk,tkd->td", router_weights, picked.astype(jnp.float32))
    return mixed.astype(jnp.bfloat16)


def ring_order(chips):
    half = chips // 2
    return [2 * row for row in range(half)] + [2 * row + 1 for row in reversed(range(half))]


def swap_pairs(experts):
    return [(index, index ^ 1) for index in range(experts)]


def ring_pairs(experts):
    order = ring_order(experts // 2)
    count = len(order)
    pairs = []
    for place, chip in enumerate(order):
        pairs.append((2 * chip, 2 * order[(place + 1) % count]))
        pairs.append((2 * chip + 1, 2 * order[(place - 1) % count] + 1))
    return pairs


def expert_kernel(width, experts, own_ref, first_ref, second_ref, gate_ref, up_ref, down_ref,
                  first_out, second_out, rows_ref, hidden_ref):
    half = first_ref.shape[0]
    ff = gate_ref.shape[2]
    rows_ref[:half, :] = first_ref[...]
    rows_ref[half:, :] = second_ref[...]
    tail = rows_ref[:, width:].astype(jnp.float32)
    lane = lax.broadcasted_iota(jnp.int32, tail.shape, 1)
    own = own_ref[0]
    mine = (lane == own) | (lane == own + experts)
    weight = jnp.sum(jnp.where(mine, tail, 0.0), axis=1, keepdims=True)
    step = math.gcd(ff, 256)
    for at in range(0, ff, step):
        part = slice(at, at + step)
        rows = rows_ref[:, :width]
        gate = jnp.dot(rows, gate_ref[0, :, part], preferred_element_type=jnp.float32)
        up = jnp.dot(rows, up_ref[0, :, part], preferred_element_type=jnp.float32)
        hidden_ref[:, part] = (gate / (1.0 + jnp.exp(-gate)) * up).astype(jnp.bfloat16)
    step = math.gcd(width, 512)
    for at in range(0, width, step):
        part = slice(at, at + step)
        out = lax.dot_general(
            hidden_ref[...], down_ref[0, part, :], (((1,), (1,)), ((), ())),
            preferred_element_type=jnp.float32,
        )
        out = (out * weight).astype(jnp.bfloat16)
        first_out[:, part] = out[:half]
        second_out[:, part] = out[half:]


def run_expert(own, first, second, gate_w, up_w, down_w, experts):
    half, wide = first.shape
    width, ff = gate_w.shape[1:]
    vmem = pl.BlockSpec(memory_space=pltpu.VMEM)
    return pl.pallas_call(
        functools.partial(expert_kernel, width, experts),
        out_shape=[jax.ShapeDtypeStruct((half, width), jnp.bfloat16)] * 2,
        in_specs=[pl.BlockSpec(memory_space=pltpu.SMEM)] + [vmem] * 5,
        out_specs=[vmem] * 2,
        scratch_shapes=[
            pltpu.VMEM((2 * half, wide), jnp.bfloat16),
            pltpu.VMEM((2 * half, ff), jnp.bfloat16),
        ],
        compiler_params=pltpu.CompilerParams(vmem_limit_bytes=30 << 20),
        cost_estimate=pl.CostEstimate(
            flops=2 * 2 * half * 3 * width * ff, bytes_accessed=8 * half * width,
            transcendentals=2 * half * ff,
        ),
    )(own, first, second, gate_w, up_w, down_w)


def added(*terms):
    total = terms[0].astype(jnp.float32)
    for term in terms[1:]:
        total = total + term.astype(jnp.float32)
    return total.astype(jnp.bfloat16)


def dense_body(tokens, expert_ids, router_weights, w_gate, w_up, w_down):
    experts = lax.axis_size("expert")
    count = tokens.shape[0]
    rounds = experts // 4
    swap = functools.partial(lax.ppermute, axis_name="expert", perm=swap_pairs(experts))
    ring = functools.partial(lax.ppermute, axis_name="expert", perm=ring_pairs(experts))
    own = lax.axis_index("expert").reshape(1)

    numbers = jnp.arange(experts, dtype=jnp.int32)
    chosen = expert_ids[:, :, None] == numbers[None, None, :]
    weight = jnp.sum(jnp.where(chosen, router_weights[:, :, None], 0.0), 1)
    high = weight.astype(jnp.bfloat16)
    low = (weight - high.astype(jnp.float32)).astype(jnp.bfloat16)
    empty = jnp.zeros((count, 128 - 2 * experts), jnp.bfloat16)
    mine = jnp.concatenate([tokens, high, low, empty], 1)

    weights = [pltpu.with_memory_space_constraint(w, pltpu.VMEM) for w in (w_gate, w_up, w_down)]
    run = lambda first, second: run_expert(own, first, second, *weights, experts)

    sibling = swap(mine)
    held = jnp.concatenate([mine, sibling], 0)
    kept, other = run(mine, sibling)
    pairs = []
    for step in range(1, rounds + 1):
        held = ring(held if step < rounds else held[:count])
        first, second = run(held, swap(held))
        pairs.append((second, swap(first)))
    moving = None
    for second, first in reversed(pairs):
        terms = added(second, first) if moving is None else None
        if moving is not None:
            if moving.shape[0] < second.shape[0]:
                moving = jnp.pad(moving, ((0, second.shape[0] - moving.shape[0]), (0, 0)))
            terms = added(second, first, moving)
        moving = ring(terms)
    last = swap(added(moving[:count], other))
    return added(moving[count:], kept, last)


def solution(mesh):
    in_specs = (
        P(("parts", "expert", "dp"), None),
        P(("parts", "expert", "dp"), None),
        P(("parts", "expert", "dp"), None),
        P("expert", None, "dp"),
        P("expert", None, "dp"),
        P("expert", None, "dp"),
    )
    out_specs = P(("parts", "expert", "dp"), None)

    def whole(tokens, expert_ids, router_weights, w_gate, w_up, w_down):
        few = mesh.shape["dp"] == 1 and 2 * expert_ids.shape[1] >= mesh.shape["expert"]
        body = dense_body if few else routed_body
        return jax.shard_map(
            body, mesh=mesh, in_specs=in_specs, out_specs=out_specs, check_vma=False
        )(tokens, expert_ids, router_weights, w_gate, w_up, w_down)

    return whole
```

```python
import functools
import math

import jax
import jax.numpy as jnp
from jax import lax
from jax.experimental import pallas as pl
from jax.experimental.pallas import tpu as pltpu
from jax.sharding import PartitionSpec as P


def expert_rows(rows, gate_w, up_w, down_w):
    total = rows.shape[0]
    block = math.gcd(total, 128)
    pieces = []
    for index in range(total // block):
        block_rows = rows[index * block : (index + 1) * block]
        gate_val = jnp.dot(block_rows, gate_w, preferred_element_type=jnp.float32)
        up_val = jnp.dot(block_rows, up_w, preferred_element_type=jnp.float32)
        hidden = (jax.nn.silu(gate_val) * up_val).astype(jnp.bfloat16)
        pieces.append(
            lax.dot_general(
                hidden, down_w, (((1,), (1,)), ((), ())), preferred_element_type=jnp.float32
            )
        )
    return jnp.concatenate(pieces, 0)


def routed_body(tokens, expert_ids, router_weights, w_gate, w_up, w_down):
    tok_count, top = expert_ids.shape
    width = tokens.shape[1]
    experts = lax.axis_size("expert")
    cap = max(2, min(tok_count, 2 * tok_count * top // experts))
    slots_all = experts * cap
    flat_ids = expert_ids.reshape(-1)
    onehot = (flat_ids[:, None] == jnp.arange(experts, dtype=jnp.int32)[None, :]).astype(jnp.int32)
    before = jnp.cumsum(onehot, 0) - onehot
    position = jnp.sum(before * onehot, 1)
    slot = flat_ids * cap + position
    send = jnp.zeros((slots_all, width), jnp.bfloat16).at[slot].set(jnp.repeat(tokens, top, 0))
    send = send.reshape(experts, cap, width)
    arrived = lax.all_to_all(send, "expert", split_axis=0, concat_axis=0, tiled=True)
    packed = arrived.reshape(slots_all, width)
    result = expert_rows(
        packed,
        lax.all_gather(w_gate, "dp", axis=2, tiled=True)[0],
        lax.all_gather(w_up, "dp", axis=2, tiled=True)[0],
        lax.all_gather(w_down, "dp", axis=2, tiled=True)[0],
    )
    expert_out = result.astype(jnp.bfloat16)
    back = lax.all_to_all(
        expert_out.reshape(experts, cap, width), "expert", split_axis=0, concat_axis=0, tiled=True
    )
    picked = back.reshape(slots_all, width)[slot].reshape(tok_count, top, width)
    mixed = jnp.einsum("tk,tkd->td", router_weights, picked.astype(jnp.float32))
    return mixed.astype(jnp.bfloat16)


def ring_order(chips):
    half = chips // 2
    return [2 * row for row in range(half)] + [2 * row + 1 for row in reversed(range(half))]


def swap_pairs(experts):
    return [(index, index ^ 1) for index in range(experts)]


def ring_pairs(experts):
    order = ring_order(experts // 2)
    count = len(order)
    pairs = []
    for place, chip in enumerate(order):
        pairs.append((2 * chip, 2 * order[(place + 1) % count]))
        pairs.append((2 * chip + 1, 2 * order[(place - 1) % count] + 1))
    return pairs


def hidden_units(rows_ref, hidden_ref, gate_ref, up_ref):
    width, ff = gate_ref.shape[1:]
    step = math.gcd(ff, 256)
    for at in range(0, ff, step):
        part = slice(at, at + step)
        rows = rows_ref[:, :width]
        gate = jnp.dot(rows, gate_ref[0, :, part], preferred_element_type=jnp.float32)
        up = jnp.dot(rows, up_ref[0, :, part], preferred_element_type=jnp.float32)
        hidden_ref[:, part] = (gate / (1.0 + jnp.exp(-gate)) * up).astype(jnp.bfloat16)


def weighted_out(experts, own_ref, rows_ref, hidden_ref, down_ref, outs):
    width = down_ref.shape[1]
    each = outs[0].shape[0]
    tail = rows_ref[:, width:].astype(jnp.float32)
    lane = lax.broadcasted_iota(jnp.int32, tail.shape, 1)
    own = own_ref[0]
    mine = (lane == own) | (lane == own + experts)
    weight = jnp.sum(jnp.where(mine, tail, 0.0), axis=1, keepdims=True)
    step = math.gcd(width, 512)
    for at in range(0, width, step):
        part = slice(at, at + step)
        out = lax.dot_general(
            hidden_ref[...], down_ref[0, part, :], (((1,), (1,)), ((), ())),
            preferred_element_type=jnp.float32,
        )
        out = (out * weight).astype(jnp.bfloat16)
        for number, target in enumerate(outs):
            target[:, part] = out[number * each : (number + 1) * each]


def fill(rows_ref, blocks):
    at = 0
    for block in blocks:
        rows_ref[at : at + block.shape[0], :] = block[...]
        at += block.shape[0]


def expert_kernel(experts, blocks, own_ref, *refs):
    gate_ref, up_ref, down_ref = refs[blocks : blocks + 3]
    outs = refs[blocks + 3 : 2 * blocks + 3]
    rows_ref, hidden_ref = refs[2 * blocks + 3 :]
    fill(rows_ref, refs[:blocks])
    hidden_units(rows_ref, hidden_ref, gate_ref, up_ref)
    weighted_out(experts, own_ref, rows_ref, hidden_ref, down_ref, outs)


def first_kernel(experts, blocks, pieces, own_ref, *refs):
    sources = refs[blocks : blocks + 3]
    outs = refs[blocks + 3 : 2 * blocks + 3]
    gate_ref, up_ref, down_ref, rows_ref, hidden_ref, done = refs[2 * blocks + 3 :]
    copies = []
    for number, (source, target) in enumerate(zip(sources, (gate_ref, up_ref, down_ref))):
        depth = source.shape[1] // pieces
        for piece in range(pieces):
            part = pl.ds(piece * depth, depth)
            copy = pltpu.make_async_copy(
                source.at[:, part], target.at[:, part], done.at[number * pieces + piece]
            )
            copy.start()
            copies.append(copy)
    fill(rows_ref, refs[:blocks])
    for copy in copies[: 2 * pieces]:
        copy.wait()
    hidden_units(rows_ref, hidden_ref, gate_ref, up_ref)
    for copy in copies[2 * pieces :]:
        copy.wait()
    weighted_out(experts, own_ref, rows_ref, hidden_ref, down_ref, outs)


def run_expert(own, blocks, weights, experts, load):
    rows = sum(block.shape[0] for block in blocks)
    wide = blocks[0].shape[1]
    width, ff = weights[0].shape[1:]
    vmem = pl.BlockSpec(memory_space=pltpu.VMEM)
    pieces = 4
    out_shape = [jax.ShapeDtypeStruct((block.shape[0], width), jnp.bfloat16) for block in blocks]
    scratch = [pltpu.VMEM((rows, wide), jnp.bfloat16), pltpu.VMEM((rows, ff), jnp.bfloat16)]
    if load:
        kernel = functools.partial(first_kernel, experts, len(blocks), pieces)
        out_shape += [pltpu.VMEM(w.shape, w.dtype) for w in weights]
        scratch.append(pltpu.SemaphoreType.DMA((3 * pieces,)))
        place = pl.BlockSpec(memory_space=pltpu.HBM)
    else:
        kernel = functools.partial(expert_kernel, experts, len(blocks))
        place = vmem
    return pl.pallas_call(
        kernel,
        out_shape=out_shape,
        in_specs=[pl.BlockSpec(memory_space=pltpu.SMEM)] + [vmem] * len(blocks) + [place] * 3,
        out_specs=[vmem] * len(out_shape),
        scratch_shapes=scratch,
        compiler_params=pltpu.CompilerParams(vmem_limit_bytes=30 << 20),
        cost_estimate=pl.CostEstimate(
            flops=2 * rows * 3 * width * ff, bytes_accessed=4 * rows * width,
            transcendentals=rows * ff,
        ),
    )(own, *blocks, *weights)


def added(*terms):
    total = terms[0].astype(jnp.float32)
    for term in terms[1:]:
        total = total + term.astype(jnp.float32)
    return total.astype(jnp.bfloat16)


def after(value, *others):
    return lax.optimization_barrier((value, *others))[0]


def dense_body(tokens, expert_ids, router_weights, w_gate, w_up, w_down):
    experts = lax.axis_size("expert")
    count = tokens.shape[0]
    rounds = experts // 4
    swap = functools.partial(lax.ppermute, axis_name="expert", perm=swap_pairs(experts))
    ring = functools.partial(lax.ppermute, axis_name="expert", perm=ring_pairs(experts))
    own = lax.axis_index("expert").reshape(1)

    numbers = jnp.arange(experts, dtype=jnp.int32)
    chosen = expert_ids[:, :, None] == numbers[None, None, :]
    weight = jnp.sum(jnp.where(chosen, router_weights[:, :, None], 0.0), 1)
    high = weight.astype(jnp.bfloat16)
    low = (weight - high.astype(jnp.float32)).astype(jnp.bfloat16)
    empty = jnp.zeros((count, 128 - 2 * experts), jnp.bfloat16)
    mine = jnp.concatenate([tokens, high, low, empty], 1)

    sibling = swap(mine)
    first, second = ring(mine), ring(sibling)
    weights = [pltpu.with_memory_space_constraint(w, pltpu.HBM) for w in (w_gate, w_up, w_down)]
    kept, other, *weights = run_expert(own, [mine, sibling], weights, experts, True)
    done = [kept]
    turned = []
    for step in range(1, rounds):
        blocks = [swap(first), swap(second), first, second]
        if turned:
            blocks[0] = after(blocks[0], *turned[-1])
        first = ring(first)
        if step < rounds - 1:
            second = ring(after(second, *done))
        keep, keep_trail, send, send_trail = run_expert(own, blocks, weights, experts, False)
        done = [keep]
        send, send_trail = swap(send), swap(send_trail)
        turned.append((keep, keep_trail, send, send_trail))
    keep, keep_trail, send, send_trail = turned[-1]
    trail = added(keep_trail, send_trail)
    first = after(first, turned[-2][0])
    blocks = [after(swap(first), trail), first]
    trail = ring(trail)
    keep, send = run_expert(own, blocks, weights, experts, False)
    lead = ring(added(keep, swap(send)))
    for step, (keep, keep_trail, send, send_trail) in enumerate(reversed(turned)):
        if step > 0:
            trail = ring(added(keep_trail, send_trail, trail))
        lead = ring(after(added(keep, send, lead), trail))
    last = swap(added(lead, other))
    return added(trail, kept, last)


def solution(mesh):
    in_specs = (
        P(("parts", "expert", "dp"), None),
        P(("parts", "expert", "dp"), None),
        P(("parts", "expert", "dp"), None),
        P("expert", None, "dp"),
        P("expert", None, "dp"),
        P("expert", None, "dp"),
    )
    out_specs = P(("parts", "expert", "dp"), None)

    def whole(tokens, expert_ids, router_weights, w_gate, w_up, w_down):
        few = mesh.shape["dp"] == 1 and 2 * expert_ids.shape[1] >= mesh.shape["expert"]
        body = dense_body if few else routed_body
        return jax.shard_map(
            body, mesh=mesh, in_specs=in_specs, out_specs=out_specs, check_vma=False
        )(tokens, expert_ids, router_weights, w_gate, w_up, w_down)

    return whole
```

```python
import functools
import math

import jax
import jax.numpy as jnp
from jax import lax
from jax.experimental import pallas as pl
from jax.experimental.pallas import tpu as pltpu
from jax.sharding import PartitionSpec as P


def expert_rows(rows, gate_w, up_w, down_w):
    total = rows.shape[0]
    block = math.gcd(total, 128)
    pieces = []
    for index in range(total // block):
        block_rows = rows[index * block : (index + 1) * block]
        gate_val = jnp.dot(block_rows, gate_w, preferred_element_type=jnp.float32)
        up_val = jnp.dot(block_rows, up_w, preferred_element_type=jnp.float32)
        hidden = (jax.nn.silu(gate_val) * up_val).astype(jnp.bfloat16)
        pieces.append(
            lax.dot_general(
                hidden, down_w, (((1,), (1,)), ((), ())), preferred_element_type=jnp.float32
            )
        )
    return jnp.concatenate(pieces, 0)


def routed_body(tokens, expert_ids, router_weights, w_gate, w_up, w_down):
    tok_count, top = expert_ids.shape
    width = tokens.shape[1]
    experts = lax.axis_size("expert")
    cap = max(2, min(tok_count, 2 * tok_count * top // experts))
    slots_all = experts * cap
    flat_ids = expert_ids.reshape(-1)
    onehot = (flat_ids[:, None] == jnp.arange(experts, dtype=jnp.int32)[None, :]).astype(jnp.int32)
    before = jnp.cumsum(onehot, 0) - onehot
    position = jnp.sum(before * onehot, 1)
    slot = flat_ids * cap + position
    send = jnp.zeros((slots_all, width), jnp.bfloat16).at[slot].set(jnp.repeat(tokens, top, 0))
    send = send.reshape(experts, cap, width)
    arrived = lax.all_to_all(send, "expert", split_axis=0, concat_axis=0, tiled=True)
    packed = arrived.reshape(slots_all, width)
    result = expert_rows(
        packed,
        lax.all_gather(w_gate, "dp", axis=2, tiled=True)[0],
        lax.all_gather(w_up, "dp", axis=2, tiled=True)[0],
        lax.all_gather(w_down, "dp", axis=2, tiled=True)[0],
    )
    expert_out = result.astype(jnp.bfloat16)
    back = lax.all_to_all(
        expert_out.reshape(experts, cap, width), "expert", split_axis=0, concat_axis=0, tiled=True
    )
    picked = back.reshape(slots_all, width)[slot].reshape(tok_count, top, width)
    mixed = jnp.einsum("tk,tkd->td", router_weights, picked.astype(jnp.float32))
    return mixed.astype(jnp.bfloat16)


def ring_order(chips):
    half = chips // 2
    return [2 * row for row in range(half)] + [2 * row + 1 for row in reversed(range(half))]


def swap_pairs(experts):
    return [(index, index ^ 1) for index in range(experts)]


def ring_pairs(experts):
    order = ring_order(experts // 2)
    count = len(order)
    pairs = []
    for place, chip in enumerate(order):
        pairs.append((2 * chip, 2 * order[(place + 1) % count]))
        pairs.append((2 * chip + 1, 2 * order[(place - 1) % count] + 1))
    return pairs


def hidden_units(rows_ref, hidden_ref, gate_ref, up_ref, ready=lambda tile: None):
    width, ff = gate_ref.shape[1:]
    step = math.gcd(ff, 256)
    for at in range(0, ff, step):
        ready(at // step)
        part = slice(at, at + step)
        rows = rows_ref[:, :width]
        gate = jnp.dot(rows, gate_ref[0, :, part], preferred_element_type=jnp.float32)
        up = jnp.dot(rows, up_ref[0, :, part], preferred_element_type=jnp.float32)
        hidden_ref[:, part] = (gate / (1.0 + jnp.exp(-gate)) * up).astype(jnp.bfloat16)


def weighted_out(experts, own_ref, rows_ref, hidden_ref, down_ref, outs):
    width = down_ref.shape[1]
    each = outs[0].shape[0]
    tail = rows_ref[:, width:].astype(jnp.float32)
    lane = lax.broadcasted_iota(jnp.int32, tail.shape, 1)
    own = own_ref[0]
    mine = (lane == own) | (lane == own + experts)
    weight = jnp.sum(jnp.where(mine, tail, 0.0), axis=1, keepdims=True)
    step = math.gcd(width, 512)
    for at in range(0, width, step):
        part = slice(at, at + step)
        out = lax.dot_general(
            hidden_ref[...], down_ref[0, part, :], (((1,), (1,)), ((), ())),
            preferred_element_type=jnp.float32,
        )
        out = (out * weight).astype(jnp.bfloat16)
        for number, target in enumerate(outs):
            target[:, part] = out[number * each : (number + 1) * each]


def fill(rows_ref, blocks):
    at = 0
    for block in blocks:
        rows_ref[at : at + block.shape[0], :] = block[...]
        at += block.shape[0]


def expert_kernel(experts, blocks, own_ref, *refs):
    gate_ref, up_ref, down_ref = refs[blocks : blocks + 3]
    outs = refs[blocks + 3 : 2 * blocks + 3]
    rows_ref, hidden_ref = refs[2 * blocks + 3 :]
    fill(rows_ref, refs[:blocks])
    hidden_units(rows_ref, hidden_ref, gate_ref, up_ref)
    weighted_out(experts, own_ref, rows_ref, hidden_ref, down_ref, outs)


def first_kernel(experts, blocks, own_ref, *refs):
    sources = refs[blocks : blocks + 3]
    outs = refs[blocks + 3 : 2 * blocks + 3]
    gate_ref, up_ref, down_ref, rows_ref, hidden_ref, done = refs[2 * blocks + 3 :]
    step = math.gcd(gate_ref.shape[2], 256)
    tiles = gate_ref.shape[2] // step
    copies = []
    for tile in range(tiles):
        part = pl.ds(tile * step, step)
        for source, target in ((sources[0], gate_ref), (sources[1], up_ref)):
            copies.append(
                pltpu.make_async_copy(
                    source.at[:, :, part], target.at[:, :, part], done.at[len(copies)]
                )
            )
    copies.append(pltpu.make_async_copy(sources[2], down_ref, done.at[len(copies)]))
    for copy in copies:
        copy.start()
    fill(rows_ref, refs[:blocks])

    def ready(tile):
        copies[2 * tile].wait()
        copies[2 * tile + 1].wait()

    hidden_units(rows_ref, hidden_ref, gate_ref, up_ref, ready)
    copies[-1].wait()
    weighted_out(experts, own_ref, rows_ref, hidden_ref, down_ref, outs)


def run_expert(own, blocks, weights, experts, load):
    rows = sum(block.shape[0] for block in blocks)
    wide = blocks[0].shape[1]
    width, ff = weights[0].shape[1:]
    vmem = pl.BlockSpec(memory_space=pltpu.VMEM)
    out_shape = [jax.ShapeDtypeStruct((block.shape[0], width), jnp.bfloat16) for block in blocks]
    scratch = [pltpu.VMEM((rows, wide), jnp.bfloat16), pltpu.VMEM((rows, ff), jnp.bfloat16)]
    if load:
        kernel = functools.partial(first_kernel, experts, len(blocks))
        out_shape += [pltpu.VMEM(w.shape, w.dtype) for w in weights]
        scratch.append(pltpu.SemaphoreType.DMA((2 * (ff // math.gcd(ff, 256)) + 1,)))
        place = pl.BlockSpec(memory_space=pltpu.HBM)
    else:
        kernel = functools.partial(expert_kernel, experts, len(blocks))
        place = vmem
    return pl.pallas_call(
        kernel,
        out_shape=out_shape,
        in_specs=[pl.BlockSpec(memory_space=pltpu.SMEM)] + [vmem] * len(blocks) + [place] * 3,
        out_specs=[vmem] * len(out_shape),
        scratch_shapes=scratch,
        compiler_params=pltpu.CompilerParams(vmem_limit_bytes=30 << 20),
        cost_estimate=pl.CostEstimate(
            flops=rows * width, bytes_accessed=rows * width, transcendentals=0
        ),
    )(own, *blocks, *weights)


def added(*terms):
    total = terms[0].astype(jnp.float32)
    for term in terms[1:]:
        total = total + term.astype(jnp.float32)
    return total.astype(jnp.bfloat16)


def after(value, *others):
    return lax.optimization_barrier((value, *others))[0]


def dense_body(tokens, expert_ids, router_weights, w_gate, w_up, w_down):
    experts = lax.axis_size("expert")
    count = tokens.shape[0]
    rounds = experts // 4
    swap = functools.partial(lax.ppermute, axis_name="expert", perm=swap_pairs(experts))
    ring = functools.partial(lax.ppermute, axis_name="expert", perm=ring_pairs(experts))
    own = lax.axis_index("expert").reshape(1)

    numbers = jnp.arange(experts, dtype=jnp.int32)
    chosen = expert_ids[:, :, None] == numbers[None, None, :]
    weight = jnp.sum(jnp.where(chosen, router_weights[:, :, None], 0.0), 1)
    high = weight.astype(jnp.bfloat16)
    low = (weight - high.astype(jnp.float32)).astype(jnp.bfloat16)
    empty = jnp.zeros((count, 128 - 2 * experts), jnp.bfloat16)
    mine = jnp.concatenate([tokens, high, low, empty], 1)

    sibling = swap(mine)
    first, second = ring(mine), ring(sibling)
    weights = [pltpu.with_memory_space_constraint(w, pltpu.HBM) for w in (w_gate, w_up, w_down)]
    run = lambda blocks: run_expert(own, blocks, weights, experts, False)
    turned = []
    for step in range(1, rounds):
        blocks = [swap(first), swap(second), first, second]
        first = ring(first)
        if step < rounds - 1:
            second = ring(second)
        blocks[0] = after(blocks[0], first)
        if turned:
            blocks[0] = after(blocks[0], *turned[-1])
        if step == 1:
            *sums, gate_w, up_w, down_w = run_expert(own, blocks, weights, experts, True)
            weights = [gate_w, up_w, down_w]
        else:
            sums = run(blocks)
        keep, keep_trail, send, send_trail = sums
        turned.append((keep, keep_trail, swap(send), swap(send_trail)))
    keep, keep_trail, send, send_trail = turned[-1]
    trail = ring(added(keep_trail, send_trail))
    first = after(first, turned[-2][0])
    keep, send = run([after(swap(first), turned[-1][0]), first])
    kept, other = run([mine, sibling])
    lead = ring(added(keep, swap(send)))
    for step, (keep, keep_trail, send, send_trail) in enumerate(reversed(turned)):
        if step > 0:
            trail = ring(added(keep_trail, send_trail, trail))
        if step == 1:
            kept, other, trail = lax.optimization_barrier((kept, other, trail))
        lead = ring(added(keep, send, lead))
    last = swap(added(lead, other))
    return added(trail, kept, last)


def solution(mesh):
    in_specs = (
        P(("parts", "expert", "dp"), None),
        P(("parts", "expert", "dp"), None),
        P(("parts", "expert", "dp"), None),
        P("expert", None, "dp"),
        P("expert", None, "dp"),
        P("expert", None, "dp"),
    )
    out_specs = P(("parts", "expert", "dp"), None)

    def whole(tokens, expert_ids, router_weights, w_gate, w_up, w_down):
        few = mesh.shape["dp"] == 1 and 2 * expert_ids.shape[1] >= mesh.shape["expert"]
        body = dense_body if few else routed_body
        return jax.shard_map(
            body, mesh=mesh, in_specs=in_specs, out_specs=out_specs, check_vma=False
        )(tokens, expert_ids, router_weights, w_gate, w_up, w_down)

    return whole
```

```python
import functools
import math

import jax
import jax.numpy as jnp
from jax import lax
from jax.experimental import pallas as pl
from jax.experimental.pallas import tpu as pltpu
from jax.sharding import PartitionSpec as P


def expert_rows(rows, gate_w, up_w, down_w):
    total = rows.shape[0]
    block = math.gcd(total, 128)
    pieces = []
    for index in range(total // block):
        block_rows = rows[index * block : (index + 1) * block]
        gate_val = jnp.dot(block_rows, gate_w, preferred_element_type=jnp.float32)
        up_val = jnp.dot(block_rows, up_w, preferred_element_type=jnp.float32)
        hidden = (jax.nn.silu(gate_val) * up_val).astype(jnp.bfloat16)
        pieces.append(
            lax.dot_general(
                hidden, down_w, (((1,), (1,)), ((), ())), preferred_element_type=jnp.float32
            )
        )
    return jnp.concatenate(pieces, 0)


def routed_body(tokens, expert_ids, router_weights, w_gate, w_up, w_down):
    tok_count, top = expert_ids.shape
    width = tokens.shape[1]
    experts = lax.axis_size("expert")
    cap = max(2, min(tok_count, 2 * tok_count * top // experts))
    slots_all = experts * cap
    flat_ids = expert_ids.reshape(-1)
    onehot = (flat_ids[:, None] == jnp.arange(experts, dtype=jnp.int32)[None, :]).astype(jnp.int32)
    before = jnp.cumsum(onehot, 0) - onehot
    position = jnp.sum(before * onehot, 1)
    slot = flat_ids * cap + position
    send = jnp.zeros((slots_all, width), jnp.bfloat16).at[slot].set(jnp.repeat(tokens, top, 0))
    send = send.reshape(experts, cap, width)
    arrived = lax.all_to_all(send, "expert", split_axis=0, concat_axis=0, tiled=True)
    packed = arrived.reshape(slots_all, width)
    result = expert_rows(
        packed,
        lax.all_gather(w_gate, "dp", axis=2, tiled=True)[0],
        lax.all_gather(w_up, "dp", axis=2, tiled=True)[0],
        lax.all_gather(w_down, "dp", axis=2, tiled=True)[0],
    )
    expert_out = result.astype(jnp.bfloat16)
    back = lax.all_to_all(
        expert_out.reshape(experts, cap, width), "expert", split_axis=0, concat_axis=0, tiled=True
    )
    picked = back.reshape(slots_all, width)[slot].reshape(tok_count, top, width)
    mixed = jnp.einsum("tk,tkd->td", router_weights, picked.astype(jnp.float32))
    return mixed.astype(jnp.bfloat16)


def ring_order(chips):
    half = chips // 2
    return [2 * row for row in range(half)] + [2 * row + 1 for row in reversed(range(half))]


def swap_pairs(experts):
    return [(index, index ^ 1) for index in range(experts)]


def ring_pairs(experts):
    order = ring_order(experts // 2)
    count = len(order)
    pairs = []
    for place, chip in enumerate(order):
        pairs.append((2 * chip, 2 * order[(place + 1) % count]))
        pairs.append((2 * chip + 1, 2 * order[(place - 1) % count] + 1))
    return pairs


def expert_kernel(experts, blocks, own_ref, *refs):
    gate_ref, up_ref, down_ref = refs[blocks : blocks + 3]
    outs = refs[blocks + 3 : 2 * blocks + 3]
    rows_ref, hidden_ref = refs[2 * blocks + 3 :]
    width, ff = gate_ref.shape[1:]
    each = outs[0].shape[0]
    for number in range(blocks):
        rows_ref[number * each : (number + 1) * each, :] = refs[number][...]
    step = math.gcd(ff, 256)
    for at in range(0, ff, step):
        part = slice(at, at + step)
        rows = rows_ref[:, :width]
        gate = jnp.dot(rows, gate_ref[0, :, part], preferred_element_type=jnp.float32)
        up = jnp.dot(rows, up_ref[0, :, part], preferred_element_type=jnp.float32)
        hidden_ref[:, part] = (gate / (1.0 + jnp.exp(-gate)) * up).astype(jnp.bfloat16)
    tail = rows_ref[:, width:].astype(jnp.float32)
    lane = lax.broadcasted_iota(jnp.int32, tail.shape, 1)
    own = own_ref[0]
    mine = (lane == own) | (lane == own + experts)
    weight = jnp.sum(jnp.where(mine, tail, 0.0), axis=1, keepdims=True)
    step = math.gcd(width, 512)
    for at in range(0, width, step):
        part = slice(at, at + step)
        out = lax.dot_general(
            hidden_ref[...], down_ref[0, part, :], (((1,), (1,)), ((), ())),
            preferred_element_type=jnp.float32,
        )
        out = (out * weight).astype(jnp.bfloat16)
        for number, target in enumerate(outs):
            target[:, part] = out[number * each : (number + 1) * each]


def run_expert(own, blocks, weights, experts):
    rows = sum(block.shape[0] for block in blocks)
    wide = blocks[0].shape[1]
    width, ff = weights[0].shape[1:]
    vmem = pl.BlockSpec(memory_space=pltpu.VMEM)
    return pl.pallas_call(
        functools.partial(expert_kernel, experts, len(blocks)),
        out_shape=[jax.ShapeDtypeStruct((block.shape[0], width), jnp.bfloat16) for block in blocks],
        in_specs=[pl.BlockSpec(memory_space=pltpu.SMEM)] + [vmem] * (len(blocks) + 3),
        out_specs=[vmem] * len(blocks),
        scratch_shapes=[pltpu.VMEM((rows, wide), jnp.bfloat16), pltpu.VMEM((rows, ff), jnp.bfloat16)],
        compiler_params=pltpu.CompilerParams(vmem_limit_bytes=30 << 20),
        cost_estimate=pl.CostEstimate(
            flops=rows * width, bytes_accessed=rows * width, transcendentals=0
        ),
        name="expert",
    )(own, *blocks, *weights)


def load_kernel(pieces, *refs):
    done = refs[6]
    copies = []
    for source, target in zip(refs[:3], refs[3:6]):
        depth = source.shape[1] // pieces
        for piece in range(pieces):
            part = pl.ds(piece * depth, depth)
            copies.append(
                pltpu.make_async_copy(source.at[:, part], target.at[:, part], done.at[len(copies)])
            )
    for copy in copies:
        copy.start()
    for copy in copies:
        copy.wait()


def load_weights(weights):
    pieces = math.gcd(weights[0].shape[1] // 16, 4)
    return pl.pallas_call(
        functools.partial(load_kernel, pieces),
        out_shape=[pltpu.VMEM(w.shape, w.dtype) for w in weights],
        in_specs=[pl.BlockSpec(memory_space=pltpu.HBM)] * 3,
        out_specs=[pl.BlockSpec(memory_space=pltpu.VMEM)] * 3,
        scratch_shapes=[pltpu.SemaphoreType.DMA((3 * pieces,))],
        compiler_params=pltpu.CompilerParams(vmem_limit_bytes=30 << 20),
        cost_estimate=pl.CostEstimate(flops=0, bytes_accessed=1024, transcendentals=0),
        name="load",
    )(*[pltpu.with_memory_space_constraint(w, pltpu.HBM) for w in weights])


def pack_kernel(experts, tokens_ref, ids_ref, weights_ref, out_ref, own_ids, own_weights, done):
    count, width = tokens_ref.shape
    copies = [
        pltpu.make_async_copy(source, target, done.at[number])
        for number, (source, target) in enumerate(
            ((ids_ref, own_ids), (weights_ref, own_weights), (tokens_ref, out_ref.at[:, :width]))
        )
    ]
    for copy in copies:
        copy.start()
    copies[0].wait()
    copies[1].wait()
    ids = own_ids[...]
    scale = own_weights[...]
    number = lax.broadcasted_iota(jnp.int32, (experts, count), 0)
    weight = jnp.zeros((experts, count), jnp.float32)
    for choice in range(ids.shape[0]):
        weight += jnp.where(ids[choice : choice + 1] == number, scale[choice : choice + 1], 0.0)
    high = weight.astype(jnp.bfloat16).astype(jnp.float32)
    low = weight - high
    rest = jnp.zeros((128 - 2 * experts, count), jnp.float32)
    columns = jnp.concatenate([high, low, rest], 0)
    columns = jnp.concatenate([columns, jnp.zeros((128, 128 - count), jnp.float32)], 1)
    out_ref[:, width:] = columns.T[:count].astype(jnp.bfloat16)
    copies[2].wait()


def pack(tokens, expert_ids, router_weights, experts):
    count, width = tokens.shape
    ids, scale = expert_ids.T, router_weights.T
    return pl.pallas_call(
        functools.partial(pack_kernel, experts),
        out_shape=jax.ShapeDtypeStruct((count, width + 128), jnp.bfloat16),
        in_specs=[pl.BlockSpec(memory_space=pltpu.HBM)] * 3,
        out_specs=pl.BlockSpec(memory_space=pltpu.VMEM),
        scratch_shapes=[
            pltpu.VMEM(ids.shape, ids.dtype),
            pltpu.VMEM(scale.shape, scale.dtype),
            pltpu.SemaphoreType.DMA((3,)),
        ],
        cost_estimate=pl.CostEstimate(flops=0, bytes_accessed=1024, transcendentals=0),
        name="pack",
    )(*[pltpu.with_memory_space_constraint(array, pltpu.HBM) for array in (tokens, ids, scale)])


def added(*terms):
    total = terms[0].astype(jnp.float32)
    for term in terms[1:]:
        total = total + term.astype(jnp.float32)
    return total.astype(jnp.bfloat16)


def after(value, *others):
    return lax.optimization_barrier((value, *others))[0]


def dense_body(tokens, expert_ids, router_weights, w_gate, w_up, w_down):
    experts = lax.axis_size("expert")
    count = tokens.shape[0]
    rounds = experts // 4
    swap = functools.partial(lax.ppermute, axis_name="expert", perm=swap_pairs(experts))
    ring = functools.partial(lax.ppermute, axis_name="expert", perm=ring_pairs(experts))
    own = lax.axis_index("expert").reshape(1)

    mine = pack(tokens, expert_ids, router_weights, experts)
    sibling = swap(mine)
    first, second = ring(mine), ring(sibling)
    weights = load_weights((after(w_gate, sibling), w_up, w_down))
    first = after(first, weights[0])
    run = lambda *blocks: run_expert(own, blocks, weights, experts)
    blocks = {}
    for step in range(1, rounds):
        if step > 1:
            second = ring(second)
        blocks[step] = (swap(first), swap(second), first, second)
        first = ring(first)
    sums = {2: run(*blocks[2])}
    first = after(first, sums[2][0], *blocks[1][:2], blocks[3][0])
    keep, send, *sums[3] = run(swap(first), first, *blocks[3])
    lead, trail = ring(added(keep, swap(send))), None
    for step in (3, 2, 1):
        if step == 3:
            sums[1] = run(after(blocks[1][0], lead), *blocks[1][1:])
        if step == 2:
            lead = after(lead, sums[1][0])
        keep, keep_trail, send, send_trail = sums[step]
        send, send_trail = swap(send), swap(send_trail)
        trail = ring(added(*([keep_trail, send_trail] + ([] if trail is None else [trail]))))
        lead = ring(added(keep, send, lead))
        if step == 2:
            kept, other = run(after(mine, lead), sibling)
    last = swap(added(lead, other))
    return added(trail, kept, last)


def solution(mesh):
    in_specs = (
        P(("parts", "expert", "dp"), None),
        P(("parts", "expert", "dp"), None),
        P(("parts", "expert", "dp"), None),
        P("expert", None, "dp"),
        P("expert", None, "dp"),
        P("expert", None, "dp"),
    )
    out_specs = P(("parts", "expert", "dp"), None)

    def whole(tokens, expert_ids, router_weights, w_gate, w_up, w_down):
        few = mesh.shape["dp"] == 1 and 2 * expert_ids.shape[1] >= mesh.shape["expert"]
        body = dense_body if few else routed_body
        return jax.shard_map(
            body, mesh=mesh, in_specs=in_specs, out_specs=out_specs, check_vma=False
        )(tokens, expert_ids, router_weights, w_gate, w_up, w_down)

    return whole
```

```python
import functools
import math

import jax
import jax.numpy as jnp
from jax import lax
from jax.experimental import pallas as pl
from jax.experimental.pallas import tpu as pltpu
from jax.sharding import PartitionSpec as P


def expert_rows(rows, gate_w, up_w, down_w):
    total = rows.shape[0]
    block = math.gcd(total, 128)
    pieces = []
    for index in range(total // block):
        block_rows = rows[index * block : (index + 1) * block]
        gate_val = jnp.dot(block_rows, gate_w, preferred_element_type=jnp.float32)
        up_val = jnp.dot(block_rows, up_w, preferred_element_type=jnp.float32)
        hidden = (jax.nn.silu(gate_val) * up_val).astype(jnp.bfloat16)
        pieces.append(
            lax.dot_general(
                hidden, down_w, (((1,), (1,)), ((), ())), preferred_element_type=jnp.float32
            )
        )
    return jnp.concatenate(pieces, 0)


def routed_body(tokens, expert_ids, router_weights, w_gate, w_up, w_down):
    tok_count, top = expert_ids.shape
    width = tokens.shape[1]
    experts = lax.axis_size("expert")
    cap = max(2, min(tok_count, 2 * tok_count * top // experts))
    slots_all = experts * cap
    flat_ids = expert_ids.reshape(-1)
    onehot = (flat_ids[:, None] == jnp.arange(experts, dtype=jnp.int32)[None, :]).astype(jnp.int32)
    before = jnp.cumsum(onehot, 0) - onehot
    position = jnp.sum(before * onehot, 1)
    slot = flat_ids * cap + position
    send = jnp.zeros((slots_all, width), jnp.bfloat16).at[slot].set(jnp.repeat(tokens, top, 0))
    send = send.reshape(experts, cap, width)
    arrived = lax.all_to_all(send, "expert", split_axis=0, concat_axis=0, tiled=True)
    packed = arrived.reshape(slots_all, width)
    result = expert_rows(
        packed,
        lax.all_gather(w_gate, "dp", axis=2, tiled=True)[0],
        lax.all_gather(w_up, "dp", axis=2, tiled=True)[0],
        lax.all_gather(w_down, "dp", axis=2, tiled=True)[0],
    )
    expert_out = result.astype(jnp.bfloat16)
    back = lax.all_to_all(
        expert_out.reshape(experts, cap, width), "expert", split_axis=0, concat_axis=0, tiled=True
    )
    picked = back.reshape(slots_all, width)[slot].reshape(tok_count, top, width)
    mixed = jnp.einsum("tk,tkd->td", router_weights, picked.astype(jnp.float32))
    return mixed.astype(jnp.bfloat16)


def ring_order(chips):
    half = chips // 2
    return [2 * row for row in range(half)] + [2 * row + 1 for row in reversed(range(half))]


def swap_pairs(experts):
    return [(index, index ^ 1) for index in range(experts)]


def ring_pairs(experts):
    order = ring_order(experts // 2)
    count = len(order)
    pairs = []
    for place, chip in enumerate(order):
        pairs.append((2 * chip, 2 * order[(place + 1) % count]))
        pairs.append((2 * chip + 1, 2 * order[(place - 1) % count] + 1))
    return pairs


def expert_kernel(experts, blocks, own_ref, *refs):
    gate_ref, up_ref, down_ref = refs[blocks : blocks + 3]
    outs = refs[blocks + 3 : 2 * blocks + 3]
    rows_ref, hidden_ref = refs[2 * blocks + 3 :]
    width, ff = gate_ref.shape[1:]
    each = outs[0].shape[0]
    for number in range(blocks):
        rows_ref[number * each : (number + 1) * each, :] = refs[number][...]
    step = math.gcd(ff, 256)
    for at in range(0, ff, step):
        part = slice(at, at + step)
        rows = rows_ref[:, :width]
        gate = jnp.dot(rows, gate_ref[0, :, part], preferred_element_type=jnp.float32)
        up = jnp.dot(rows, up_ref[0, :, part], preferred_element_type=jnp.float32)
        hidden_ref[:, part] = (gate / (1.0 + jnp.exp(-gate)) * up).astype(jnp.bfloat16)
    tail = rows_ref[:, width:].astype(jnp.float32)
    lane = lax.broadcasted_iota(jnp.int32, tail.shape, 1)
    own = own_ref[0]
    mine = (lane == own) | (lane == own + experts)
    weight = jnp.sum(jnp.where(mine, tail, 0.0), axis=1, keepdims=True)
    step = math.gcd(width, 512)
    for at in range(0, width, step):
        part = slice(at, at + step)
        out = lax.dot_general(
            hidden_ref[...], down_ref[0, part, :], (((1,), (1,)), ((), ())),
            preferred_element_type=jnp.float32,
        )
        out = (out * weight).astype(jnp.bfloat16)
        for number, target in enumerate(outs):
            target[:, part] = out[number * each : (number + 1) * each]


def run_expert(own, blocks, weights, experts):
    rows = sum(block.shape[0] for block in blocks)
    wide = blocks[0].shape[1]
    width, ff = weights[0].shape[1:]
    vmem = pl.BlockSpec(memory_space=pltpu.VMEM)
    return pl.pallas_call(
        functools.partial(expert_kernel, experts, len(blocks)),
        out_shape=[jax.ShapeDtypeStruct((block.shape[0], width), jnp.bfloat16) for block in blocks],
        in_specs=[pl.BlockSpec(memory_space=pltpu.SMEM)] + [vmem] * (len(blocks) + 3),
        out_specs=[vmem] * len(blocks),
        scratch_shapes=[pltpu.VMEM((rows, wide), jnp.bfloat16), pltpu.VMEM((rows, ff), jnp.bfloat16)],
        compiler_params=pltpu.CompilerParams(vmem_limit_bytes=16 << 20),
        cost_estimate=pl.CostEstimate(
            flops=rows * width, bytes_accessed=rows * width, transcendentals=0
        ),
        name="expert",
    )(own, *blocks, *weights)


def load_kernel(pieces, *refs):
    *arrays, done = refs
    count = len(arrays) // 2
    copies = []
    for source, target in zip(arrays[:count], arrays[count:]):
        depth = source.shape[1] // pieces
        for piece in range(pieces):
            part = pl.ds(piece * depth, depth)
            copies.append(
                pltpu.make_async_copy(source.at[:, part], target.at[:, part], done.at[len(copies)])
            )
    for copy in copies:
        copy.start()
    for copy in copies:
        copy.wait()


def load_weights(weights):
    pieces = math.gcd(weights[0].shape[1] // 16, 4)
    return pl.pallas_call(
        functools.partial(load_kernel, pieces),
        out_shape=[pltpu.VMEM(w.shape, w.dtype) for w in weights],
        in_specs=[pl.BlockSpec(memory_space=pltpu.HBM)] * len(weights),
        out_specs=[pl.BlockSpec(memory_space=pltpu.VMEM)] * len(weights),
        scratch_shapes=[pltpu.SemaphoreType.DMA((len(weights) * pieces,))],
        compiler_params=pltpu.CompilerParams(vmem_limit_bytes=16 << 20),
        cost_estimate=pl.CostEstimate(flops=0, bytes_accessed=1024, transcendentals=0),
        name="load",
    )(*[pltpu.with_memory_space_constraint(w, pltpu.HBM) for w in weights])


def pack_kernel(experts, tokens_ref, ids_ref, weights_ref, out_ref, own_ids, own_weights, done):
    count, width = tokens_ref.shape
    copies = [
        pltpu.make_async_copy(source, target, done.at[number])
        for number, (source, target) in enumerate(
            ((ids_ref, own_ids), (weights_ref, own_weights), (tokens_ref, out_ref.at[:, :width]))
        )
    ]
    for copy in copies:
        copy.start()
    copies[0].wait()
    copies[1].wait()
    ids = own_ids[...]
    scale = own_weights[...]
    number = lax.broadcasted_iota(jnp.int32, (experts, count), 0)
    weight = jnp.zeros((experts, count), jnp.float32)
    for choice in range(ids.shape[0]):
        weight += jnp.where(ids[choice : choice + 1] == number, scale[choice : choice + 1], 0.0)
    high = weight.astype(jnp.bfloat16).astype(jnp.float32)
    low = weight - high
    rest = jnp.zeros((128 - 2 * experts, count), jnp.float32)
    columns = jnp.concatenate([high, low, rest], 0)
    columns = jnp.concatenate([columns, jnp.zeros((128, 128 - count), jnp.float32)], 1)
    out_ref[:, width:] = columns.T[:count].astype(jnp.bfloat16)
    copies[2].wait()


def pack(tokens, expert_ids, router_weights, experts):
    count, width = tokens.shape
    ids, scale = expert_ids.T, router_weights.T
    return pl.pallas_call(
        functools.partial(pack_kernel, experts),
        out_shape=jax.ShapeDtypeStruct((count, width + 128), jnp.bfloat16),
        in_specs=[pl.BlockSpec(memory_space=pltpu.HBM)] * 3,
        out_specs=pl.BlockSpec(memory_space=pltpu.VMEM),
        scratch_shapes=[
            pltpu.VMEM(ids.shape, ids.dtype),
            pltpu.VMEM(scale.shape, scale.dtype),
            pltpu.SemaphoreType.DMA((3,)),
        ],
        cost_estimate=pl.CostEstimate(flops=0, bytes_accessed=1024, transcendentals=0),
        name="pack",
    )(*[pltpu.with_memory_space_constraint(array, pltpu.HBM) for array in (tokens, ids, scale)])


def added(*terms):
    total = terms[0].astype(jnp.float32)
    for term in terms[1:]:
        total = total + term.astype(jnp.float32)
    return total.astype(jnp.bfloat16)


def after(value, *others):
    return lax.optimization_barrier((value, *others))[0]


def dense_body(tokens, expert_ids, router_weights, w_gate, w_up, w_down):
    experts = lax.axis_size("expert")
    count = tokens.shape[0]
    rounds = experts // 4
    swap = functools.partial(lax.ppermute, axis_name="expert", perm=swap_pairs(experts))
    ring = functools.partial(lax.ppermute, axis_name="expert", perm=ring_pairs(experts))
    own = lax.axis_index("expert").reshape(1)

    mine = pack(after(tokens, own), expert_ids, router_weights, experts)
    sibling = swap(mine)
    first, second = ring(mine), ring(sibling)
    gate_w, up_w = load_weights((after(w_gate, sibling), w_up))
    first = after(first, gate_w)
    down_w, = load_weights((after(w_down, first),))
    weights = [gate_w, up_w, down_w]
    run = lambda *blocks: run_expert(own, blocks, weights, experts)
    blocks = {}
    for step in range(1, rounds):
        if step > 1:
            second = ring(second)
        blocks[step] = (swap(first), swap(second), first, second)
        first = ring(first)
        if step == 1:
            first = after(first, down_w)
    sums = {2: run(*blocks[2])}
    first = after(first, sums[2][0], *blocks[1][:2], blocks[3][0])
    keep, send, *sums[3] = run(swap(first), first, *blocks[3])
    lead, trail = ring(added(keep, swap(send))), None
    for step in (3, 2, 1):
        if step == 3:
            sums[1] = run(after(blocks[1][0], lead), *blocks[1][1:])
        if step == 2:
            lead = after(lead, sums[1][0])
        keep, keep_trail, send, send_trail = sums[step]
        send, send_trail = swap(send), swap(send_trail)
        trail = ring(added(*([keep_trail, send_trail] + ([] if trail is None else [trail]))))
        lead = ring(added(keep, send, lead))
        if step == 2:
            kept, other = run(after(mine, lead), sibling)
    last = swap(added(lead, other))
    return added(trail, kept, last)


def solution(mesh):
    in_specs = (
        P(("parts", "expert", "dp"), None),
        P(("parts", "expert", "dp"), None),
        P(("parts", "expert", "dp"), None),
        P("expert", None, "dp"),
        P("expert", None, "dp"),
        P("expert", None, "dp"),
    )
    out_specs = P(("parts", "expert", "dp"), None)

    def whole(tokens, expert_ids, router_weights, w_gate, w_up, w_down):
        few = mesh.shape["dp"] == 1 and 2 * expert_ids.shape[1] >= mesh.shape["expert"]
        body = dense_body if few else routed_body
        return jax.shard_map(
            body, mesh=mesh, in_specs=in_specs, out_specs=out_specs, check_vma=False
        )(tokens, expert_ids, router_weights, w_gate, w_up, w_down)

    return whole
```

```python
import functools
import math

import jax
import jax.numpy as jnp
from jax import lax
from jax.experimental import pallas as pl
from jax.experimental.pallas import tpu as pltpu
from jax.sharding import PartitionSpec as P


def expert_rows(rows, gate_w, up_w, down_w):
    total = rows.shape[0]
    block = math.gcd(total, 128)
    pieces = []
    for index in range(total // block):
        block_rows = rows[index * block : (index + 1) * block]
        gate_val = jnp.dot(block_rows, gate_w, preferred_element_type=jnp.float32)
        up_val = jnp.dot(block_rows, up_w, preferred_element_type=jnp.float32)
        hidden = (jax.nn.silu(gate_val) * up_val).astype(jnp.bfloat16)
        pieces.append(
            lax.dot_general(
                hidden, down_w, (((1,), (1,)), ((), ())), preferred_element_type=jnp.float32
            )
        )
    return jnp.concatenate(pieces, 0)


def routed_body(tokens, expert_ids, router_weights, w_gate, w_up, w_down):
    tok_count, top = expert_ids.shape
    width = tokens.shape[1]
    experts = lax.axis_size("expert")
    cap = max(2, min(tok_count, 2 * tok_count * top // experts))
    slots_all = experts * cap
    flat_ids = expert_ids.reshape(-1)
    onehot = (flat_ids[:, None] == jnp.arange(experts, dtype=jnp.int32)[None, :]).astype(jnp.int32)
    before = jnp.cumsum(onehot, 0) - onehot
    position = jnp.sum(before * onehot, 1)
    slot = flat_ids * cap + position
    send = jnp.zeros((slots_all, width), jnp.bfloat16).at[slot].set(jnp.repeat(tokens, top, 0))
    send = send.reshape(experts, cap, width)
    arrived = lax.all_to_all(send, "expert", split_axis=0, concat_axis=0, tiled=True)
    packed = arrived.reshape(slots_all, width)
    result = expert_rows(
        packed,
        lax.all_gather(w_gate, "dp", axis=2, tiled=True)[0],
        lax.all_gather(w_up, "dp", axis=2, tiled=True)[0],
        lax.all_gather(w_down, "dp", axis=2, tiled=True)[0],
    )
    expert_out = result.astype(jnp.bfloat16)
    back = lax.all_to_all(
        expert_out.reshape(experts, cap, width), "expert", split_axis=0, concat_axis=0, tiled=True
    )
    picked = back.reshape(slots_all, width)[slot].reshape(tok_count, top, width)
    mixed = jnp.einsum("tk,tkd->td", router_weights, picked.astype(jnp.float32))
    return mixed.astype(jnp.bfloat16)


def ring_order(chips):
    half = chips // 2
    return [2 * row for row in range(half)] + [2 * row + 1 for row in reversed(range(half))]


def swap_pairs(experts):
    return [(index, index ^ 1) for index in range(experts)]


def ring_pairs(experts):
    order = ring_order(experts // 2)
    count = len(order)
    pairs = []
    for place, chip in enumerate(order):
        pairs.append((2 * chip, 2 * order[(place + 1) % count]))
        pairs.append((2 * chip + 1, 2 * order[(place - 1) % count] + 1))
    return pairs


def expert_kernel(experts, blocks, own_ref, *refs):
    gate_ref, up_ref, down_ref = refs[blocks : blocks + 3]
    outs = refs[blocks + 3 : 2 * blocks + 3]
    rows_ref, hidden_ref = refs[2 * blocks + 3 :]
    width, ff = gate_ref.shape[1:]
    each = outs[0].shape[0]
    for number in range(blocks):
        rows_ref[number * each : (number + 1) * each, :] = refs[number][...]
    step = math.gcd(ff, 256)
    for at in range(0, ff, step):
        part = slice(at, at + step)
        rows = rows_ref[:, :width]
        gate = jnp.dot(rows, gate_ref[0, :, part], preferred_element_type=jnp.float32)
        up = jnp.dot(rows, up_ref[0, :, part], preferred_element_type=jnp.float32)
        hidden_ref[:, part] = (gate / (1.0 + jnp.exp(-gate)) * up).astype(jnp.bfloat16)
    tail = rows_ref[:, width:].astype(jnp.float32)
    lane = lax.broadcasted_iota(jnp.int32, tail.shape, 1)
    own = own_ref[0]
    mine = (lane == own) | (lane == own + experts)
    weight = jnp.sum(jnp.where(mine, tail, 0.0), axis=1, keepdims=True)
    step = math.gcd(width, 512)
    for at in range(0, width, step):
        part = slice(at, at + step)
        out = lax.dot_general(
            hidden_ref[...], down_ref[0, part, :], (((1,), (1,)), ((), ())),
            preferred_element_type=jnp.float32,
        )
        out = (out * weight).astype(jnp.bfloat16)
        for number, target in enumerate(outs):
            target[:, part] = out[number * each : (number + 1) * each]


def run_expert(own, blocks, weights, experts, cost=1):
    rows = sum(block.shape[0] for block in blocks)
    wide = blocks[0].shape[1]
    width, ff = weights[0].shape[1:]
    vmem = pl.BlockSpec(memory_space=pltpu.VMEM)
    return pl.pallas_call(
        functools.partial(expert_kernel, experts, len(blocks)),
        out_shape=[jax.ShapeDtypeStruct((block.shape[0], width), jnp.bfloat16) for block in blocks],
        in_specs=[pl.BlockSpec(memory_space=pltpu.SMEM)] + [vmem] * (len(blocks) + 3),
        out_specs=[vmem] * len(blocks),
        scratch_shapes=[pltpu.VMEM((rows, wide), jnp.bfloat16), pltpu.VMEM((rows, ff), jnp.bfloat16)],
        compiler_params=pltpu.CompilerParams(vmem_limit_bytes=16 << 20),
        cost_estimate=pl.CostEstimate(
            flops=cost * rows * width, bytes_accessed=rows * width, transcendentals=0
        ),
        name="expert",
    )(own, *blocks, *weights)


def load_kernel(pieces, *refs):
    *arrays, done = refs
    count = len(arrays) // 2
    copies = []
    for source, target in zip(arrays[:count], arrays[count:]):
        depth = source.shape[1] // pieces
        for piece in range(pieces):
            part = pl.ds(piece * depth, depth)
            copies.append(
                pltpu.make_async_copy(source.at[:, part], target.at[:, part], done.at[len(copies)])
            )
    for copy in copies:
        copy.start()
    for copy in copies:
        copy.wait()


def load_weights(weights):
    pieces = math.gcd(weights[0].shape[1] // 16, 4)
    return pl.pallas_call(
        functools.partial(load_kernel, pieces),
        out_shape=[pltpu.VMEM(w.shape, w.dtype) for w in weights],
        in_specs=[pl.BlockSpec(memory_space=pltpu.HBM)] * len(weights),
        out_specs=[pl.BlockSpec(memory_space=pltpu.VMEM)] * len(weights),
        scratch_shapes=[pltpu.SemaphoreType.DMA((len(weights) * pieces,))],
        compiler_params=pltpu.CompilerParams(vmem_limit_bytes=16 << 20),
        cost_estimate=pl.CostEstimate(flops=0, bytes_accessed=1024, transcendentals=0),
        name="load",
    )(*[pltpu.with_memory_space_constraint(w, pltpu.HBM) for w in weights])


def pack_kernel(experts, tokens_ref, ids_ref, weights_ref, out_ref, own_ids, own_weights, done):
    count, width = tokens_ref.shape
    copies = [
        pltpu.make_async_copy(source, target, done.at[number])
        for number, (source, target) in enumerate(
            ((ids_ref, own_ids), (weights_ref, own_weights), (tokens_ref, out_ref.at[:, :width]))
        )
    ]
    for copy in copies:
        copy.start()
    copies[0].wait()
    copies[1].wait()
    ids = own_ids[...]
    scale = own_weights[...]
    number = lax.broadcasted_iota(jnp.int32, (experts, count), 0)
    weight = jnp.zeros((experts, count), jnp.float32)
    for choice in range(ids.shape[0]):
        weight += jnp.where(ids[choice : choice + 1] == number, scale[choice : choice + 1], 0.0)
    high = weight.astype(jnp.bfloat16).astype(jnp.float32)
    low = weight - high
    rest = jnp.zeros((128 - 2 * experts, count), jnp.float32)
    columns = jnp.concatenate([high, low, rest], 0)
    columns = jnp.concatenate([columns, jnp.zeros((128, 128 - count), jnp.float32)], 1)
    out_ref[:, width:] = columns.T[:count].astype(jnp.bfloat16)
    copies[2].wait()


def pack(tokens, expert_ids, router_weights, experts):
    count, width = tokens.shape
    ids, scale = expert_ids.T, router_weights.T
    return pl.pallas_call(
        functools.partial(pack_kernel, experts),
        out_shape=jax.ShapeDtypeStruct((count, width + 128), jnp.bfloat16),
        in_specs=[pl.BlockSpec(memory_space=pltpu.HBM)] * 3,
        out_specs=pl.BlockSpec(memory_space=pltpu.VMEM),
        scratch_shapes=[
            pltpu.VMEM(ids.shape, ids.dtype),
            pltpu.VMEM(scale.shape, scale.dtype),
            pltpu.SemaphoreType.DMA((3,)),
        ],
        cost_estimate=pl.CostEstimate(flops=0, bytes_accessed=1024, transcendentals=0),
        name="pack",
    )(*[pltpu.with_memory_space_constraint(array, pltpu.HBM) for array in (tokens, ids, scale)])


def added(*terms):
    total = terms[0].astype(jnp.float32)
    for term in terms[1:]:
        total = total + term.astype(jnp.float32)
    return total.astype(jnp.bfloat16)


def after(value, *others):
    return lax.optimization_barrier((value, *others))[0]


def dense_body(tokens, expert_ids, router_weights, w_gate, w_up, w_down):
    experts = lax.axis_size("expert")
    count = tokens.shape[0]
    rounds = experts // 4
    swap = functools.partial(lax.ppermute, axis_name="expert", perm=swap_pairs(experts))
    ring = functools.partial(lax.ppermute, axis_name="expert", perm=ring_pairs(experts))
    own = lax.axis_index("expert").reshape(1)

    mine = pack(after(tokens, own), expert_ids, router_weights, experts)
    sibling = swap(mine)
    first, second = ring(mine), ring(sibling)
    gate_w, up_w = load_weights((after(w_gate, sibling), w_up))
    first = after(first, gate_w)
    down_w, = load_weights((after(w_down, first),))
    weights = [gate_w, up_w, down_w]
    run = lambda *blocks: run_expert(own, blocks, weights, experts)
    blocks = {}
    for step in range(1, rounds):
        if step > 1:
            second = ring(second)
        blocks[step] = (swap(first), swap(second), first, second)
        if step == rounds - 1:
            first = after(first, *blocks[1][:2])
        first = ring(first)
        if step == 1:
            first = after(first, down_w)
    sums = {2: run(*blocks[2])}
    first = after(first, sums[2][0], blocks[3][0])
    sums[3] = run_expert(own, blocks[3], weights, experts, cost=6 * w_gate.shape[2])
    keep, send = run(after(swap(first), sums[3][0]), first)
    lead, trail = ring(added(keep, swap(send))), None
    for step in (3, 2, 1):
        if step == 3:
            sums[1] = run(after(blocks[1][0], lead), *blocks[1][1:])
        if step == 2:
            lead = after(lead, sums[1][0])
        keep, keep_trail, send, send_trail = sums[step]
        send, send_trail = swap(send), swap(send_trail)
        trail = ring(added(*([keep_trail, send_trail] + ([] if trail is None else [trail]))))
        lead = ring(added(keep, send, lead))
        if step == 2:
            kept, other = run(after(mine, lead), sibling)
    last = swap(after(added(lead, other), trail))
    return added(trail, kept, last)


def solution(mesh):
    in_specs = (
        P(("parts", "expert", "dp"), None),
        P(("parts", "expert", "dp"), None),
        P(("parts", "expert", "dp"), None),
        P("expert", None, "dp"),
        P("expert", None, "dp"),
        P("expert", None, "dp"),
    )
    out_specs = P(("parts", "expert", "dp"), None)

    def whole(tokens, expert_ids, router_weights, w_gate, w_up, w_down):
        few = mesh.shape["dp"] == 1 and 2 * expert_ids.shape[1] >= mesh.shape["expert"]
        body = dense_body if few else routed_body
        return jax.shard_map(
            body, mesh=mesh, in_specs=in_specs, out_specs=out_specs, check_vma=False
        )(tokens, expert_ids, router_weights, w_gate, w_up, w_down)

    return whole
```

```python
import functools
import math

import jax
import jax.numpy as jnp
from jax import lax
from jax.experimental import pallas as pl
from jax.experimental.pallas import tpu as pltpu
from jax.sharding import PartitionSpec as P


def expert_rows(rows, gate_w, up_w, down_w):
    total = rows.shape[0]
    block = math.gcd(total, 128)
    pieces = []
    for index in range(total // block):
        block_rows = rows[index * block : (index + 1) * block]
        gate_val = jnp.dot(block_rows, gate_w, preferred_element_type=jnp.float32)
        up_val = jnp.dot(block_rows, up_w, preferred_element_type=jnp.float32)
        hidden = (jax.nn.silu(gate_val) * up_val).astype(jnp.bfloat16)
        pieces.append(
            lax.dot_general(
                hidden, down_w, (((1,), (1,)), ((), ())), preferred_element_type=jnp.float32
            )
        )
    return jnp.concatenate(pieces, 0)


def routed_body(tokens, expert_ids, router_weights, w_gate, w_up, w_down):
    tok_count, top = expert_ids.shape
    width = tokens.shape[1]
    experts = lax.axis_size("expert")
    cap = max(2, min(tok_count, 2 * tok_count * top // experts))
    slots_all = experts * cap
    flat_ids = expert_ids.reshape(-1)
    onehot = (flat_ids[:, None] == jnp.arange(experts, dtype=jnp.int32)[None, :]).astype(jnp.int32)
    before = jnp.cumsum(onehot, 0) - onehot
    position = jnp.sum(before * onehot, 1)
    slot = flat_ids * cap + position
    send = jnp.zeros((slots_all, width), jnp.bfloat16).at[slot].set(jnp.repeat(tokens, top, 0))
    send = send.reshape(experts, cap, width)
    arrived = lax.all_to_all(send, "expert", split_axis=0, concat_axis=0, tiled=True)
    packed = arrived.reshape(slots_all, width)
    result = expert_rows(
        packed,
        lax.all_gather(w_gate, "dp", axis=2, tiled=True)[0],
        lax.all_gather(w_up, "dp", axis=2, tiled=True)[0],
        lax.all_gather(w_down, "dp", axis=2, tiled=True)[0],
    )
    expert_out = result.astype(jnp.bfloat16)
    back = lax.all_to_all(
        expert_out.reshape(experts, cap, width), "expert", split_axis=0, concat_axis=0, tiled=True
    )
    picked = back.reshape(slots_all, width)[slot].reshape(tok_count, top, width)
    mixed = jnp.einsum("tk,tkd->td", router_weights, picked.astype(jnp.float32))
    return mixed.astype(jnp.bfloat16)


def ring_order(chips):
    half = chips // 2
    return [2 * row for row in range(half)] + [2 * row + 1 for row in reversed(range(half))]


def swap_pairs(experts):
    return [(index, index ^ 1) for index in range(experts)]


def ring_pairs(experts):
    order = ring_order(experts // 2)
    count = len(order)
    pairs = []
    for place, chip in enumerate(order):
        pairs.append((2 * chip, 2 * order[(place + 1) % count]))
        pairs.append((2 * chip + 1, 2 * order[(place - 1) % count] + 1))
    return pairs


def expert_kernel(experts, blocks, own_ref, *refs):
    gate_ref, up_ref, down_ref = refs[blocks : blocks + 3]
    outs = refs[blocks + 3 : 2 * blocks + 3]
    rows_ref, hidden_ref = refs[2 * blocks + 3 :]
    width, ff = gate_ref.shape[1:]
    each = outs[0].shape[0]
    for number in range(blocks):
        rows_ref[number * each : (number + 1) * each, :] = refs[number][...]
    step = math.gcd(ff, 256)
    for at in range(0, ff, step):
        part = slice(at, at + step)
        rows = rows_ref[:, :width]
        gate = jnp.dot(rows, gate_ref[0, :, part], preferred_element_type=jnp.float32)
        up = jnp.dot(rows, up_ref[0, :, part], preferred_element_type=jnp.float32)
        hidden_ref[:, part] = (gate / (1.0 + jnp.exp(-gate)) * up).astype(jnp.bfloat16)
    tail = rows_ref[:, width:].astype(jnp.float32)
    lane = lax.broadcasted_iota(jnp.int32, tail.shape, 1)
    own = own_ref[0]
    mine = (lane == own) | (lane == own + experts)
    weight = jnp.sum(jnp.where(mine, tail, 0.0), axis=1, keepdims=True)
    step = math.gcd(width, 512)
    for at in range(0, width, step):
        part = slice(at, at + step)
        out = lax.dot_general(
            hidden_ref[...], down_ref[0, part, :], (((1,), (1,)), ((), ())),
            preferred_element_type=jnp.float32,
        )
        out = (out * weight).astype(jnp.bfloat16)
        for number, target in enumerate(outs):
            target[:, part] = out[number * each : (number + 1) * each]


def run_expert(own, blocks, weights, experts):
    rows = sum(block.shape[0] for block in blocks)
    wide = blocks[0].shape[1]
    width, ff = weights[0].shape[1:]
    vmem = pl.BlockSpec(memory_space=pltpu.VMEM)
    return pl.pallas_call(
        functools.partial(expert_kernel, experts, len(blocks)),
        out_shape=[jax.ShapeDtypeStruct((block.shape[0], width), jnp.bfloat16) for block in blocks],
        in_specs=[pl.BlockSpec(memory_space=pltpu.SMEM)] + [vmem] * (len(blocks) + 3),
        out_specs=[vmem] * len(blocks),
        scratch_shapes=[pltpu.VMEM((rows, wide), jnp.bfloat16), pltpu.VMEM((rows, ff), jnp.bfloat16)],
        compiler_params=pltpu.CompilerParams(vmem_limit_bytes=16 << 20),
        cost_estimate=pl.CostEstimate(
            flops=rows * width, bytes_accessed=rows * width, transcendentals=0
        ),
        name="expert",
    )(own, *blocks, *weights)


def load_kernel(pieces, *refs):
    *arrays, done = refs
    count = len(arrays) // 2
    copies = []
    for source, target in zip(arrays[:count], arrays[count:]):
        depth = source.shape[1] // pieces
        for piece in range(pieces):
            part = pl.ds(piece * depth, depth)
            copies.append(
                pltpu.make_async_copy(source.at[:, part], target.at[:, part], done.at[len(copies)])
            )
    for copy in copies:
        copy.start()
    for copy in copies:
        copy.wait()


def load_weights(weights):
    pieces = math.gcd(weights[0].shape[1] // 16, 4)
    return pl.pallas_call(
        functools.partial(load_kernel, pieces),
        out_shape=[pltpu.VMEM(w.shape, w.dtype) for w in weights],
        in_specs=[pl.BlockSpec(memory_space=pltpu.HBM)] * len(weights),
        out_specs=[pl.BlockSpec(memory_space=pltpu.VMEM)] * len(weights),
        scratch_shapes=[pltpu.SemaphoreType.DMA((len(weights) * pieces,))],
        compiler_params=pltpu.CompilerParams(vmem_limit_bytes=16 << 20),
        cost_estimate=pl.CostEstimate(flops=0, bytes_accessed=1024, transcendentals=0),
        name="load",
    )(*[pltpu.with_memory_space_constraint(w, pltpu.HBM) for w in weights])


def pack_kernel(experts, tokens_ref, ids_ref, weights_ref, out_ref, own_ids, own_weights, done):
    count, width = tokens_ref.shape
    copies = [
        pltpu.make_async_copy(source, target, done.at[number])
        for number, (source, target) in enumerate(
            ((ids_ref, own_ids), (weights_ref, own_weights), (tokens_ref, out_ref.at[:, :width]))
        )
    ]
    for copy in copies:
        copy.start()
    copies[0].wait()
    copies[1].wait()
    ids = own_ids[...]
    scale = own_weights[...]
    number = lax.broadcasted_iota(jnp.int32, (experts, count), 0)
    weight = jnp.zeros((experts, count), jnp.float32)
    for choice in range(ids.shape[0]):
        weight += jnp.where(ids[choice : choice + 1] == number, scale[choice : choice + 1], 0.0)
    high = weight.astype(jnp.bfloat16).astype(jnp.float32)
    low = weight - high
    rest = jnp.zeros((128 - 2 * experts, count), jnp.float32)
    columns = jnp.concatenate([high, low, rest], 0)
    columns = jnp.concatenate([columns, jnp.zeros((128, 128 - count), jnp.float32)], 1)
    out_ref[:, width:] = columns.T[:count].astype(jnp.bfloat16)
    copies[2].wait()


def pack(tokens, expert_ids, router_weights, experts):
    count, width = tokens.shape
    ids, scale = expert_ids.T, router_weights.T
    return pl.pallas_call(
        functools.partial(pack_kernel, experts),
        out_shape=jax.ShapeDtypeStruct((count, width + 128), jnp.bfloat16),
        in_specs=[pl.BlockSpec(memory_space=pltpu.HBM)] * 3,
        out_specs=pl.BlockSpec(memory_space=pltpu.VMEM),
        scratch_shapes=[
            pltpu.VMEM(ids.shape, ids.dtype),
            pltpu.VMEM(scale.shape, scale.dtype),
            pltpu.SemaphoreType.DMA((3,)),
        ],
        cost_estimate=pl.CostEstimate(flops=0, bytes_accessed=1024, transcendentals=0),
        name="pack",
    )(*[pltpu.with_memory_space_constraint(array, pltpu.HBM) for array in (tokens, ids, scale)])


def added(*terms):
    total = terms[0].astype(jnp.float32)
    for term in terms[1:]:
        total = total + term.astype(jnp.float32)
    return total.astype(jnp.bfloat16)


def after(value, *others):
    return lax.optimization_barrier((value, *others))[0]


def dense_body(tokens, expert_ids, router_weights, w_gate, w_up, w_down):
    experts = lax.axis_size("expert")
    count = tokens.shape[0]
    rounds = experts // 4
    swap = functools.partial(lax.ppermute, axis_name="expert", perm=swap_pairs(experts))
    ring = functools.partial(lax.ppermute, axis_name="expert", perm=ring_pairs(experts))
    own = lax.axis_index("expert").reshape(1)

    mine = pack(after(tokens, own), expert_ids, router_weights, experts)
    sibling = swap(mine)
    first, second = ring(mine), ring(sibling)
    gate_w, up_w = load_weights((after(w_gate, sibling), w_up))
    first = after(first, gate_w)
    down_w, = load_weights((after(w_down, first),))
    weights = [gate_w, up_w, down_w]
    run = lambda *blocks: run_expert(own, blocks, weights, experts)
    blocks = {}
    for step in range(1, rounds):
        if step > 1:
            second = ring(second)
        blocks[step] = (swap(first), swap(second), first, second)
        if step == rounds - 1:
            first = after(first, *blocks[1][:2])
        first = ring(first)
        if step == 1:
            first = after(first, down_w)
    *second_sums, early, early_send = run(*blocks[2], blocks[3][0], blocks[3][2])
    late = run(blocks[3][1], blocks[3][3])
    sums = {2: second_sums, 3: (early, late[0], early_send, late[1])}
    first = after(first, early, blocks[3][1])
    send, keep = run(after(swap(first), late[0]), first)
    lead, trail = ring(added(keep, swap(send))), None
    for step in (3, 2, 1):
        if step == 3:
            sums[1] = run(after(blocks[1][0], lead), *blocks[1][1:])
        if step == 2:
            lead = after(lead, sums[1][0])
        keep_trail, keep, send_trail, send = sums[step]
        send, send_trail = swap(send), swap(send_trail)
        trail = ring(added(*([keep_trail, send_trail] + ([] if trail is None else [trail]))))
        lead = ring(added(keep, send, lead))
        if step == 3:
            kept, other = run(after(mine, lead), sibling)
    last = swap(added(trail, other))
    return added(lead, kept, last)


def solution(mesh):
    in_specs = (
        P(("parts", "expert", "dp"), None),
        P(("parts", "expert", "dp"), None),
        P(("parts", "expert", "dp"), None),
        P("expert", None, "dp"),
        P("expert", None, "dp"),
        P("expert", None, "dp"),
    )
    out_specs = P(("parts", "expert", "dp"), None)

    def whole(tokens, expert_ids, router_weights, w_gate, w_up, w_down):
        few = mesh.shape["dp"] == 1 and 2 * expert_ids.shape[1] >= mesh.shape["expert"]
        body = dense_body if few else routed_body
        return jax.shard_map(
            body, mesh=mesh, in_specs=in_specs, out_specs=out_specs, check_vma=False
        )(tokens, expert_ids, router_weights, w_gate, w_up, w_down)

    return whole
```

```python
import functools
import math

import jax
import jax.numpy as jnp
from jax import lax
from jax.experimental import pallas as pl
from jax.experimental.pallas import tpu as pltpu
from jax.sharding import PartitionSpec as P


def expert_rows(rows, gate_w, up_w, down_w):
    total = rows.shape[0]
    block = math.gcd(total, 128)
    pieces = []
    for index in range(total // block):
        block_rows = rows[index * block : (index + 1) * block]
        gate_val = jnp.dot(block_rows, gate_w, preferred_element_type=jnp.float32)
        up_val = jnp.dot(block_rows, up_w, preferred_element_type=jnp.float32)
        hidden = (jax.nn.silu(gate_val) * up_val).astype(jnp.bfloat16)
        pieces.append(
            lax.dot_general(
                hidden, down_w, (((1,), (1,)), ((), ())), preferred_element_type=jnp.float32
            )
        )
    return jnp.concatenate(pieces, 0)


def routed_body(tokens, expert_ids, router_weights, w_gate, w_up, w_down):
    tok_count, top = expert_ids.shape
    width = tokens.shape[1]
    experts = lax.axis_size("expert")
    cap = max(2, min(tok_count, 2 * tok_count * top // experts))
    slots_all = experts * cap
    flat_ids = expert_ids.reshape(-1)
    onehot = (flat_ids[:, None] == jnp.arange(experts, dtype=jnp.int32)[None, :]).astype(jnp.int32)
    before = jnp.cumsum(onehot, 0) - onehot
    position = jnp.sum(before * onehot, 1)
    slot = flat_ids * cap + position
    send = jnp.zeros((slots_all, width), jnp.bfloat16).at[slot].set(jnp.repeat(tokens, top, 0))
    send = send.reshape(experts, cap, width)
    arrived = lax.all_to_all(send, "expert", split_axis=0, concat_axis=0, tiled=True)
    packed = arrived.reshape(slots_all, width)
    result = expert_rows(
        packed,
        lax.all_gather(w_gate, "dp", axis=2, tiled=True)[0],
        lax.all_gather(w_up, "dp", axis=2, tiled=True)[0],
        lax.all_gather(w_down, "dp", axis=2, tiled=True)[0],
    )
    expert_out = result.astype(jnp.bfloat16)
    back = lax.all_to_all(
        expert_out.reshape(experts, cap, width), "expert", split_axis=0, concat_axis=0, tiled=True
    )
    picked = back.reshape(slots_all, width)[slot].reshape(tok_count, top, width)
    mixed = jnp.einsum("tk,tkd->td", router_weights, picked.astype(jnp.float32))
    return mixed.astype(jnp.bfloat16)


def ring_order(chips):
    half = chips // 2
    return [2 * row for row in range(half)] + [2 * row + 1 for row in reversed(range(half))]


def swap_pairs(experts):
    return [(index, index ^ 1) for index in range(experts)]


def ring_pairs(experts, places):
    order = ring_order(experts // 2)
    count = len(order)
    pairs = []
    for place, chip in enumerate(order):
        pairs.append((2 * chip, 2 * order[(place + places) % count]))
        pairs.append((2 * chip + 1, 2 * order[(place - places) % count] + 1))
    return pairs


def expert_kernel(experts, blocks, own_ref, *refs):
    gate_ref, up_ref, down_ref = refs[blocks : blocks + 3]
    outs = refs[blocks + 3 : 2 * blocks + 3]
    rows_ref, hidden_ref = refs[2 * blocks + 3 :]
    width, ff = gate_ref.shape[1:]
    each = outs[0].shape[0]
    for number in range(blocks):
        rows_ref[number * each : (number + 1) * each, :] = refs[number][...]
    step = math.gcd(ff, 256)
    for at in range(0, ff, step):
        part = slice(at, at + step)
        rows = rows_ref[:, :width]
        gate = jnp.dot(rows, gate_ref[0, :, part], preferred_element_type=jnp.float32)
        up = jnp.dot(rows, up_ref[0, :, part], preferred_element_type=jnp.float32)
        hidden_ref[:, part] = (gate / (1.0 + jnp.exp(-gate)) * up).astype(jnp.bfloat16)
    tail = rows_ref[:, width:].astype(jnp.float32)
    lane = lax.broadcasted_iota(jnp.int32, tail.shape, 1)
    own = own_ref[0]
    mine = (lane == own) | (lane == own + experts)
    weight = jnp.sum(jnp.where(mine, tail, 0.0), axis=1, keepdims=True)
    step = math.gcd(width, 512)
    for at in range(0, width, step):
        part = slice(at, at + step)
        out = lax.dot_general(
            hidden_ref[...], down_ref[0, part, :], (((1,), (1,)), ((), ())),
            preferred_element_type=jnp.float32,
        )
        out = (out * weight).astype(jnp.bfloat16)
        for number, target in enumerate(outs):
            target[:, part] = out[number * each : (number + 1) * each]


def run_expert(own, blocks, weights, experts):
    rows = sum(block.shape[0] for block in blocks)
    wide = blocks[0].shape[1]
    width, ff = weights[0].shape[1:]
    vmem = pl.BlockSpec(memory_space=pltpu.VMEM)
    return pl.pallas_call(
        functools.partial(expert_kernel, experts, len(blocks)),
        out_shape=[jax.ShapeDtypeStruct((block.shape[0], width), jnp.bfloat16) for block in blocks],
        in_specs=[pl.BlockSpec(memory_space=pltpu.SMEM)] + [vmem] * (len(blocks) + 3),
        out_specs=[vmem] * len(blocks),
        scratch_shapes=[pltpu.VMEM((rows, wide), jnp.bfloat16), pltpu.VMEM((rows, ff), jnp.bfloat16)],
        compiler_params=pltpu.CompilerParams(vmem_limit_bytes=16 << 20),
        cost_estimate=pl.CostEstimate(
            flops=rows * width, bytes_accessed=rows * width, transcendentals=0
        ),
        name="expert",
    )(own, *blocks, *weights)


def load_kernel(pieces, *refs):
    *arrays, done = refs
    count = len(arrays) // 2
    copies = []
    for source, target in zip(arrays[:count], arrays[count:]):
        depth = source.shape[1] // pieces
        for piece in range(pieces):
            part = pl.ds(piece * depth, depth)
            copies.append(
                pltpu.make_async_copy(source.at[:, part], target.at[:, part], done.at[len(copies)])
            )
    for copy in copies:
        copy.start()
    for copy in copies:
        copy.wait()


def load_weights(weights):
    pieces = math.gcd(weights[0].shape[1] // 16, 4)
    return pl.pallas_call(
        functools.partial(load_kernel, pieces),
        out_shape=[pltpu.VMEM(w.shape, w.dtype) for w in weights],
        in_specs=[pl.BlockSpec(memory_space=pltpu.HBM)] * len(weights),
        out_specs=[pl.BlockSpec(memory_space=pltpu.VMEM)] * len(weights),
        scratch_shapes=[pltpu.SemaphoreType.DMA((len(weights) * pieces,))],
        compiler_params=pltpu.CompilerParams(vmem_limit_bytes=16 << 20),
        cost_estimate=pl.CostEstimate(flops=0, bytes_accessed=1024, transcendentals=0),
        name="load",
    )(*[pltpu.with_memory_space_constraint(w, pltpu.HBM) for w in weights])


def pack_kernel(experts, tokens_ref, ids_ref, weights_ref, out_ref, own_ids, own_weights, done):
    count, width = tokens_ref.shape
    copies = [
        pltpu.make_async_copy(source, target, done.at[number])
        for number, (source, target) in enumerate(
            ((ids_ref, own_ids), (weights_ref, own_weights), (tokens_ref, out_ref.at[:, :width]))
        )
    ]
    for copy in copies:
        copy.start()
    copies[0].wait()
    copies[1].wait()
    ids = own_ids[...]
    scale = own_weights[...]
    number = lax.broadcasted_iota(jnp.int32, (experts, count), 0)
    weight = jnp.zeros((experts, count), jnp.float32)
    for choice in range(ids.shape[0]):
        weight += jnp.where(ids[choice : choice + 1] == number, scale[choice : choice + 1], 0.0)
    high = weight.astype(jnp.bfloat16).astype(jnp.float32)
    low = weight - high
    rest = jnp.zeros((128 - 2 * experts, count), jnp.float32)
    columns = jnp.concatenate([high, low, rest], 0)
    columns = jnp.concatenate([columns, jnp.zeros((128, 128 - count), jnp.float32)], 1)
    out_ref[:, width:] = columns.T[:count].astype(jnp.bfloat16)
    copies[2].wait()


def pack(tokens, expert_ids, router_weights, experts):
    count, width = tokens.shape
    ids, scale = expert_ids.T, router_weights.T
    return pl.pallas_call(
        functools.partial(pack_kernel, experts),
        out_shape=jax.ShapeDtypeStruct((count, width + 128), jnp.bfloat16),
        in_specs=[pl.BlockSpec(memory_space=pltpu.HBM)] * 3,
        out_specs=pl.BlockSpec(memory_space=pltpu.VMEM),
        scratch_shapes=[
            pltpu.VMEM(ids.shape, ids.dtype),
            pltpu.VMEM(scale.shape, scale.dtype),
            pltpu.SemaphoreType.DMA((3,)),
        ],
        cost_estimate=pl.CostEstimate(flops=0, bytes_accessed=1024, transcendentals=0),
        name="pack",
    )(*[pltpu.with_memory_space_constraint(array, pltpu.HBM) for array in (tokens, ids, scale)])


def added(*terms):
    total = terms[0].astype(jnp.float32)
    for term in terms[1:]:
        total = total + term.astype(jnp.float32)
    return total.astype(jnp.bfloat16)


def after(value, *others):
    return lax.optimization_barrier((value, *others))[0]


def dense_body(tokens, expert_ids, router_weights, w_gate, w_up, w_down):
    experts = lax.axis_size("expert")
    count = tokens.shape[0]
    rounds = experts // 4
    swap = functools.partial(lax.ppermute, axis_name="expert", perm=swap_pairs(experts))
    ring = functools.partial(lax.ppermute, axis_name="expert", perm=ring_pairs(experts, 1))
    leap = functools.partial(lax.ppermute, axis_name="expert", perm=ring_pairs(experts, 2))
    own = lax.axis_index("expert").reshape(1)

    mine = pack(after(tokens, own), expert_ids, router_weights, experts)
    sibling = swap(mine)
    first, second = ring(mine), ring(sibling)
    gate_w, up_w = load_weights((after(w_gate, sibling), w_up))
    first = after(first, gate_w)
    down_w, = load_weights((after(w_down, first),))
    weights = [gate_w, up_w, down_w]
    run = lambda *blocks: run_expert(own, blocks, weights, experts)
    blocks = {}
    for step in range(1, rounds):
        if step > 1:
            second = ring(second)
        blocks[step] = (swap(first), swap(second), first, second)
        if step == rounds - 2:
            far = leap(first)
        if step < rounds - 1:
            first = ring(first)
        if step == 1:
            first = after(first, down_w)
    turned = lambda keep_trail, keep, send_trail, send: (keep_trail, keep, swap(send_trail), swap(send))
    sums = {2: run(after(blocks[2][0], *blocks[1][:2]), *blocks[2][1:])}
    far = after(far, sums[2][0])
    sums[2] = turned(*sums[2])
    near = after(blocks[3][0], *sums[2][2:])
    send, keep, early, early_send = run(swap(far), far, near, blocks[3][2])
    late, late_send = run(after(blocks[3][1], early), blocks[3][3])
    sums[3] = turned(early, late, early_send, late_send)
    far = leap(added(keep, swap(send)))
    lead, trail = [], []
    for step in range(rounds - 1, 0, -1):
        if step == 2:
            lead = [after(lead[0], sums[1][0]), far]
        if step == 1:
            lead = [after(lead[0], kept)]
        keep_trail, keep, send_trail, send = sums[step]
        trail = [ring(added(keep_trail, send_trail, *trail))]
        lead = [added(keep, send, *lead)]
        if step == 3:
            sums[1] = turned(*run(after(blocks[1][0], lead[0]), *blocks[1][1:]))
        if step == 2:
            kept, other = run(after(mine, lead[0]), sibling)
        lead = [ring(lead[0])]
    last = swap(added(trail[0], other))
    return added(lead[0], kept, last)


def solution(mesh):
    in_specs = (
        P(("parts", "expert", "dp"), None),
        P(("parts", "expert", "dp"), None),
        P(("parts", "expert", "dp"), None),
        P("expert", None, "dp"),
        P("expert", None, "dp"),
        P("expert", None, "dp"),
    )
    out_specs = P(("parts", "expert", "dp"), None)

    def whole(tokens, expert_ids, router_weights, w_gate, w_up, w_down):
        few = mesh.shape["dp"] == 1 and 2 * expert_ids.shape[1] >= mesh.shape["expert"]
        body = dense_body if few else routed_body
        return jax.shard_map(
            body, mesh=mesh, in_specs=in_specs, out_specs=out_specs, check_vma=False
        )(tokens, expert_ids, router_weights, w_gate, w_up, w_down)

    return whole
```

```python
import functools
import math

import jax
import jax.numpy as jnp
from jax import lax
from jax.experimental import pallas as pl
from jax.experimental.pallas import tpu as pltpu
from jax.sharding import PartitionSpec as P


def expert_rows(rows, gate_w, up_w, down_w):
    total = rows.shape[0]
    block = math.gcd(total, 128)
    pieces = []
    for index in range(total // block):
        block_rows = rows[index * block : (index + 1) * block]
        gate_val = jnp.dot(block_rows, gate_w, preferred_element_type=jnp.float32)
        up_val = jnp.dot(block_rows, up_w, preferred_element_type=jnp.float32)
        hidden = (jax.nn.silu(gate_val) * up_val).astype(jnp.bfloat16)
        pieces.append(
            lax.dot_general(
                hidden, down_w, (((1,), (1,)), ((), ())), preferred_element_type=jnp.float32
            )
        )
    return jnp.concatenate(pieces, 0)


def routed_body(tokens, expert_ids, router_weights, w_gate, w_up, w_down):
    tok_count, top = expert_ids.shape
    width = tokens.shape[1]
    experts = lax.axis_size("expert")
    cap = max(2, min(tok_count, 2 * tok_count * top // experts))
    slots_all = experts * cap
    flat_ids = expert_ids.reshape(-1)
    onehot = (flat_ids[:, None] == jnp.arange(experts, dtype=jnp.int32)[None, :]).astype(jnp.int32)
    before = jnp.cumsum(onehot, 0) - onehot
    position = jnp.sum(before * onehot, 1)
    slot = flat_ids * cap + position
    send = jnp.zeros((slots_all, width), jnp.bfloat16).at[slot].set(jnp.repeat(tokens, top, 0))
    send = send.reshape(experts, cap, width)
    arrived = lax.all_to_all(send, "expert", split_axis=0, concat_axis=0, tiled=True)
    packed = arrived.reshape(slots_all, width)
    result = expert_rows(
        packed,
        lax.all_gather(w_gate, "dp", axis=2, tiled=True)[0],
        lax.all_gather(w_up, "dp", axis=2, tiled=True)[0],
        lax.all_gather(w_down, "dp", axis=2, tiled=True)[0],
    )
    expert_out = result.astype(jnp.bfloat16)
    back = lax.all_to_all(
        expert_out.reshape(experts, cap, width), "expert", split_axis=0, concat_axis=0, tiled=True
    )
    picked = back.reshape(slots_all, width)[slot].reshape(tok_count, top, width)
    mixed = jnp.einsum("tk,tkd->td", router_weights, picked.astype(jnp.float32))
    return mixed.astype(jnp.bfloat16)


def ring_order(chips):
    half = chips // 2
    return [2 * row for row in range(half)] + [2 * row + 1 for row in reversed(range(half))]


def swap_pairs(experts):
    return [(index, index ^ 1) for index in range(experts)]


def ring_pairs(experts, places):
    order = ring_order(experts // 2)
    count = len(order)
    pairs = []
    for place, chip in enumerate(order):
        pairs.append((2 * chip, 2 * order[(place + places) % count]))
        pairs.append((2 * chip + 1, 2 * order[(place - places) % count] + 1))
    return pairs


def expert_kernel(experts, blocks, own_ref, *refs):
    gate_ref, up_ref, down_ref, *outs = refs[blocks:-2]
    rows_ref, hidden_ref = refs[-2:]
    width, ff = gate_ref.shape[1:]
    each = outs[0].shape[0]
    at = 0
    for block in refs[:blocks]:
        rows_ref[at : at + block.shape[0], :] = block[...]
        at += block.shape[0]
    step = math.gcd(ff, 256)
    for at in range(0, ff, step):
        part = slice(at, at + step)
        rows = rows_ref[:, :width]
        gate = jnp.dot(rows, gate_ref[0, :, part], preferred_element_type=jnp.float32)
        up = jnp.dot(rows, up_ref[0, :, part], preferred_element_type=jnp.float32)
        hidden_ref[:, part] = (gate / (1.0 + jnp.exp(-gate)) * up).astype(jnp.bfloat16)
    tail = rows_ref[:, width:].astype(jnp.float32)
    lane = lax.broadcasted_iota(jnp.int32, tail.shape, 1)
    own = own_ref[0]
    mine = (lane == own) | (lane == own + experts)
    weight = jnp.sum(jnp.where(mine, tail, 0.0), axis=1, keepdims=True)
    step = math.gcd(width, 512)
    for at in range(0, width, step):
        part = slice(at, at + step)
        out = lax.dot_general(
            hidden_ref[...], down_ref[0, part, :], (((1,), (1,)), ((), ())),
            preferred_element_type=jnp.float32,
        )
        out = (out * weight).astype(jnp.bfloat16)
        for number, target in enumerate(outs):
            target[:, part] = out[number * each : (number + 1) * each]


def run_expert(own, blocks, weights, experts, each):
    rows = sum(block.shape[0] for block in blocks)
    wide = blocks[0].shape[1]
    width, ff = weights[0].shape[1:]
    vmem = pl.BlockSpec(memory_space=pltpu.VMEM)
    return pl.pallas_call(
        functools.partial(expert_kernel, experts, len(blocks)),
        out_shape=[jax.ShapeDtypeStruct((each, width), jnp.bfloat16)] * (rows // each),
        in_specs=[pl.BlockSpec(memory_space=pltpu.SMEM)] + [vmem] * (len(blocks) + 3),
        out_specs=[vmem] * (rows // each),
        scratch_shapes=[pltpu.VMEM((rows, wide), jnp.bfloat16), pltpu.VMEM((rows, ff), jnp.bfloat16)],
        compiler_params=pltpu.CompilerParams(vmem_limit_bytes=16 << 20),
        cost_estimate=pl.CostEstimate(
            flops=rows * width, bytes_accessed=rows * width, transcendentals=0
        ),
        name="expert",
    )(own, *blocks, *weights)


def load_kernel(pieces, *refs):
    *arrays, done = refs
    count = len(arrays) // 2
    copies = []
    for source, target in zip(arrays[:count], arrays[count:]):
        depth = source.shape[1] // pieces
        for piece in range(pieces):
            part = pl.ds(piece * depth, depth)
            copies.append(
                pltpu.make_async_copy(source.at[:, part], target.at[:, part], done.at[len(copies)])
            )
    for copy in copies:
        copy.start()
    for copy in copies:
        copy.wait()


def load_weights(weights):
    pieces = math.gcd(weights[0].shape[1] // 16, 4)
    return pl.pallas_call(
        functools.partial(load_kernel, pieces),
        out_shape=[pltpu.VMEM(w.shape, w.dtype) for w in weights],
        in_specs=[pl.BlockSpec(memory_space=pltpu.HBM)] * len(weights),
        out_specs=[pl.BlockSpec(memory_space=pltpu.VMEM)] * len(weights),
        scratch_shapes=[pltpu.SemaphoreType.DMA((len(weights) * pieces,))],
        compiler_params=pltpu.CompilerParams(vmem_limit_bytes=16 << 20),
        cost_estimate=pl.CostEstimate(flops=0, bytes_accessed=1024, transcendentals=0),
        name="load",
    )(*[pltpu.with_memory_space_constraint(w, pltpu.HBM) for w in weights])


def pack_kernel(experts, tokens_ref, ids_ref, weights_ref, out_ref, own_ids, own_weights, done):
    count, width = tokens_ref.shape
    copies = [
        pltpu.make_async_copy(source, target, done.at[number])
        for number, (source, target) in enumerate(
            ((ids_ref, own_ids), (weights_ref, own_weights), (tokens_ref, out_ref.at[:, :width]))
        )
    ]
    for copy in copies:
        copy.start()
    copies[0].wait()
    copies[1].wait()
    ids = own_ids[...]
    scale = own_weights[...]
    number = lax.broadcasted_iota(jnp.int32, (experts, count), 0)
    weight = jnp.zeros((experts, count), jnp.float32)
    for choice in range(ids.shape[0]):
        weight += jnp.where(ids[choice : choice + 1] == number, scale[choice : choice + 1], 0.0)
    high = weight.astype(jnp.bfloat16).astype(jnp.float32)
    low = weight - high
    rest = jnp.zeros((128 - 2 * experts, count), jnp.float32)
    columns = jnp.concatenate([high, low, rest], 0)
    columns = jnp.concatenate([columns, jnp.zeros((128, 128 - count), jnp.float32)], 1)
    out_ref[:, width:] = columns.T[:count].astype(jnp.bfloat16)
    copies[2].wait()


def pack(tokens, expert_ids, router_weights, experts):
    count, width = tokens.shape
    ids, scale = expert_ids.T, router_weights.T
    return pl.pallas_call(
        functools.partial(pack_kernel, experts),
        out_shape=jax.ShapeDtypeStruct((count, width + 128), jnp.bfloat16),
        in_specs=[pl.BlockSpec(memory_space=pltpu.HBM)] * 3,
        out_specs=pl.BlockSpec(memory_space=pltpu.VMEM),
        scratch_shapes=[
            pltpu.VMEM(ids.shape, ids.dtype),
            pltpu.VMEM(scale.shape, scale.dtype),
            pltpu.SemaphoreType.DMA((3,)),
        ],
        cost_estimate=pl.CostEstimate(flops=0, bytes_accessed=1024, transcendentals=0),
        name="pack",
    )(*[pltpu.with_memory_space_constraint(array, pltpu.HBM) for array in (tokens, ids, scale)])


def added(*terms):
    total = terms[0].astype(jnp.float32)
    for term in terms[1:]:
        total = total + term.astype(jnp.float32)
    return total.astype(jnp.bfloat16)


def after(value, *others):
    return lax.optimization_barrier((value, *others))[0]


def dense_body(tokens, expert_ids, router_weights, w_gate, w_up, w_down):
    experts = lax.axis_size("expert")
    count = tokens.shape[0]
    rounds = experts // 4
    swap = functools.partial(lax.ppermute, axis_name="expert", perm=swap_pairs(experts))
    ring = functools.partial(lax.ppermute, axis_name="expert", perm=ring_pairs(experts, 1))
    leap = functools.partial(lax.ppermute, axis_name="expert", perm=ring_pairs(experts, 2))
    own = lax.axis_index("expert").reshape(1)

    mine = pack(after(tokens, own), expert_ids, router_weights, experts)
    sibling = swap(mine)
    first, second = ring(mine), ring(sibling)
    gate_w, up_w = load_weights((after(w_gate, sibling), w_up))
    first = after(first, gate_w)
    down_w, = load_weights((after(w_down, first),))
    weights = [gate_w, up_w, down_w]
    run = lambda *blocks: run_expert(own, blocks, weights, experts, count)
    blocks = {}
    for step in range(1, rounds - 1):
        if step > 1:
            first, second = ring(first), ring(second)
        if step == 2:
            first = after(first, down_w)
        blocks[step] = (swap(first), swap(second), first, second)
    far = leap(first)
    both = ring(jnp.concatenate([first, second], 0))
    turned = lambda keep, keep_trail, send, send_trail: (keep_trail, keep, swap(send_trail), swap(send))
    sums = {2: run(after(blocks[2][0], *blocks[1][:2]), *blocks[2][1:])}
    far = after(far, sums[2][0])
    sums[2] = turned(*sums[2])
    keep, send = run(swap(far), far)
    lead, trail = [added(keep, swap(send))], []
    sums[3] = turned(*run(after(swap(both), lead[0]), both))
    lead = [ring(lead[0])]
    for step in range(rounds - 1, 0, -1):
        if step == 2:
            lead = [after(lead[0], sums[1][0])]
        if step == 1:
            lead = [after(lead[0], kept)]
        keep_trail, keep, send_trail, send = sums[step]
        trail = [added(keep_trail, send_trail, *trail)]
        lead = [added(keep, send, *lead)]
        if step == 3:
            sums[1] = turned(*run(after(blocks[1][0], lead[0], trail[0]), *blocks[1][1:]))
        if step == 2:
            kept, other = run(after(mine, lead[0]), sibling)
        lead, trail = [ring(lead[0])], [ring(trail[0])]
    last = swap(added(lead[0], other))
    return added(trail[0], kept, last)


def solution(mesh):
    in_specs = (
        P(("parts", "expert", "dp"), None),
        P(("parts", "expert", "dp"), None),
        P(("parts", "expert", "dp"), None),
        P("expert", None, "dp"),
        P("expert", None, "dp"),
        P("expert", None, "dp"),
    )
    out_specs = P(("parts", "expert", "dp"), None)

    def whole(tokens, expert_ids, router_weights, w_gate, w_up, w_down):
        few = mesh.shape["dp"] == 1 and 2 * expert_ids.shape[1] >= mesh.shape["expert"]
        body = dense_body if few else routed_body
        return jax.shard_map(
            body, mesh=mesh, in_specs=in_specs, out_specs=out_specs, check_vma=False
        )(tokens, expert_ids, router_weights, w_gate, w_up, w_down)

    return whole
```

```python
import functools
import math

import jax
import jax.numpy as jnp
from jax import lax
from jax.experimental import pallas as pl
from jax.experimental.pallas import tpu as pltpu
from jax.sharding import PartitionSpec as P


def expert_rows(rows, gate_w, up_w, down_w):
    total = rows.shape[0]
    block = math.gcd(total, 128)
    pieces = []
    for index in range(total // block):
        block_rows = rows[index * block : (index + 1) * block]
        gate_val = jnp.dot(block_rows, gate_w, preferred_element_type=jnp.float32)
        up_val = jnp.dot(block_rows, up_w, preferred_element_type=jnp.float32)
        hidden = (jax.nn.silu(gate_val) * up_val).astype(jnp.bfloat16)
        pieces.append(
            lax.dot_general(
                hidden, down_w, (((1,), (1,)), ((), ())), preferred_element_type=jnp.float32
            )
        )
    return jnp.concatenate(pieces, 0)


def routed_body(tokens, expert_ids, router_weights, w_gate, w_up, w_down):
    tok_count, top = expert_ids.shape
    width = tokens.shape[1]
    experts = lax.axis_size("expert")
    cap = max(2, min(tok_count, 2 * tok_count * top // experts))
    slots_all = experts * cap
    flat_ids = expert_ids.reshape(-1)
    onehot = (flat_ids[:, None] == jnp.arange(experts, dtype=jnp.int32)[None, :]).astype(jnp.int32)
    before = jnp.cumsum(onehot, 0) - onehot
    position = jnp.sum(before * onehot, 1)
    slot = flat_ids * cap + position
    send = jnp.zeros((slots_all, width), jnp.bfloat16).at[slot].set(jnp.repeat(tokens, top, 0))
    send = send.reshape(experts, cap, width)
    arrived = lax.all_to_all(send, "expert", split_axis=0, concat_axis=0, tiled=True)
    packed = arrived.reshape(slots_all, width)
    result = expert_rows(
        packed,
        lax.all_gather(w_gate, "dp", axis=2, tiled=True)[0],
        lax.all_gather(w_up, "dp", axis=2, tiled=True)[0],
        lax.all_gather(w_down, "dp", axis=2, tiled=True)[0],
    )
    expert_out = result.astype(jnp.bfloat16)
    back = lax.all_to_all(
        expert_out.reshape(experts, cap, width), "expert", split_axis=0, concat_axis=0, tiled=True
    )
    picked = back.reshape(slots_all, width)[slot].reshape(tok_count, top, width)
    mixed = jnp.einsum("tk,tkd->td", router_weights, picked.astype(jnp.float32))
    return mixed.astype(jnp.bfloat16)


def ring_order(chips):
    half = chips // 2
    return [2 * row for row in range(half)] + [2 * row + 1 for row in reversed(range(half))]


def swap_pairs(experts):
    return [(index, index ^ 1) for index in range(experts)]


def ring_pairs(experts, places, cross=0):
    order = ring_order(experts // 2)
    count = len(order)
    pairs = []
    for place, chip in enumerate(order):
        pairs.append((2 * chip, 2 * order[(place + places) % count] + cross))
        pairs.append((2 * chip + 1, 2 * order[(place - places) % count] + 1 - cross))
    return pairs


def expert_kernel(experts, blocks, own_ref, *refs):
    gate_ref, up_ref, down_ref, *outs = refs[blocks:-2]
    rows_ref, hidden_ref = refs[-2:]
    width, ff = gate_ref.shape[1:]
    each = outs[0].shape[0]
    at = 0
    for block in refs[:blocks]:
        rows_ref[at : at + block.shape[0], :] = block[...]
        at += block.shape[0]
    step = math.gcd(ff, 256)
    for at in range(0, ff, step):
        part = slice(at, at + step)
        rows = rows_ref[:, :width]
        gate = jnp.dot(rows, gate_ref[0, :, part], preferred_element_type=jnp.float32)
        up = jnp.dot(rows, up_ref[0, :, part], preferred_element_type=jnp.float32)
        hidden_ref[:, part] = (gate / (1.0 + jnp.exp(-gate)) * up).astype(jnp.bfloat16)
    tail = rows_ref[:, width:].astype(jnp.float32)
    lane = lax.broadcasted_iota(jnp.int32, tail.shape, 1)
    own = own_ref[0]
    mine = (lane == own) | (lane == own + experts)
    weight = jnp.sum(jnp.where(mine, tail, 0.0), axis=1, keepdims=True)
    step = math.gcd(width, 512)
    for at in range(0, width, step):
        part = slice(at, at + step)
        out = lax.dot_general(
            hidden_ref[...], down_ref[0, part, :], (((1,), (1,)), ((), ())),
            preferred_element_type=jnp.float32,
        )
        out = (out * weight).astype(jnp.bfloat16)
        for number, target in enumerate(outs):
            target[:, part] = out[number * each : (number + 1) * each]


def run_expert(own, blocks, weights, experts, each):
    rows = sum(block.shape[0] for block in blocks)
    wide = blocks[0].shape[1]
    width, ff = weights[0].shape[1:]
    vmem = pl.BlockSpec(memory_space=pltpu.VMEM)
    return pl.pallas_call(
        functools.partial(expert_kernel, experts, len(blocks)),
        out_shape=[jax.ShapeDtypeStruct((each, width), jnp.bfloat16)] * (rows // each),
        in_specs=[pl.BlockSpec(memory_space=pltpu.SMEM)] + [vmem] * (len(blocks) + 3),
        out_specs=[vmem] * (rows // each),
        scratch_shapes=[pltpu.VMEM((rows, wide), jnp.bfloat16), pltpu.VMEM((rows, ff), jnp.bfloat16)],
        compiler_params=pltpu.CompilerParams(vmem_limit_bytes=16 << 20),
        cost_estimate=pl.CostEstimate(
            flops=rows * width, bytes_accessed=rows * width, transcendentals=0
        ),
        name="expert",
    )(own, *blocks, *weights)


def load_kernel(pieces, *refs):
    *arrays, done = refs
    count = len(arrays) // 2
    copies = []
    for source, target in zip(arrays[:count], arrays[count:]):
        depth = source.shape[1] // pieces
        for piece in range(pieces):
            part = pl.ds(piece * depth, depth)
            copies.append(
                pltpu.make_async_copy(source.at[:, part], target.at[:, part], done.at[len(copies)])
            )
    for copy in copies:
        copy.start()
    for copy in copies:
        copy.wait()


def load_weights(weights):
    pieces = math.gcd(weights[0].shape[1] // 16, 4)
    return pl.pallas_call(
        functools.partial(load_kernel, pieces),
        out_shape=[pltpu.VMEM(w.shape, w.dtype) for w in weights],
        in_specs=[pl.BlockSpec(memory_space=pltpu.HBM)] * len(weights),
        out_specs=[pl.BlockSpec(memory_space=pltpu.VMEM)] * len(weights),
        scratch_shapes=[pltpu.SemaphoreType.DMA((len(weights) * pieces,))],
        compiler_params=pltpu.CompilerParams(vmem_limit_bytes=16 << 20),
        cost_estimate=pl.CostEstimate(flops=0, bytes_accessed=1024, transcendentals=0),
        name="load",
    )(*[pltpu.with_memory_space_constraint(w, pltpu.HBM) for w in weights])


def pack_kernel(experts, tokens_ref, ids_ref, weights_ref, out_ref, own_ids, own_weights, done):
    count, width = tokens_ref.shape
    copies = [
        pltpu.make_async_copy(source, target, done.at[number])
        for number, (source, target) in enumerate(
            ((ids_ref, own_ids), (weights_ref, own_weights), (tokens_ref, out_ref.at[:, :width]))
        )
    ]
    for copy in copies:
        copy.start()
    copies[0].wait()
    copies[1].wait()
    ids = own_ids[...]
    scale = own_weights[...]
    number = lax.broadcasted_iota(jnp.int32, (experts, count), 0)
    weight = jnp.zeros((experts, count), jnp.float32)
    for choice in range(ids.shape[0]):
        weight += jnp.where(ids[choice : choice + 1] == number, scale[choice : choice + 1], 0.0)
    high = weight.astype(jnp.bfloat16).astype(jnp.float32)
    low = weight - high
    rest = jnp.zeros((128 - 2 * experts, count), jnp.float32)
    columns = jnp.concatenate([high, low, rest], 0)
    columns = jnp.concatenate([columns, jnp.zeros((128, 128 - count), jnp.float32)], 1)
    out_ref[:, width:] = columns.T[:count].astype(jnp.bfloat16)
    copies[2].wait()


def pack(tokens, expert_ids, router_weights, experts):
    count, width = tokens.shape
    ids, scale = expert_ids.T, router_weights.T
    return pl.pallas_call(
        functools.partial(pack_kernel, experts),
        out_shape=jax.ShapeDtypeStruct((count, width + 128), jnp.bfloat16),
        in_specs=[pl.BlockSpec(memory_space=pltpu.HBM)] * 3,
        out_specs=pl.BlockSpec(memory_space=pltpu.VMEM),
        scratch_shapes=[
            pltpu.VMEM(ids.shape, ids.dtype),
            pltpu.VMEM(scale.shape, scale.dtype),
            pltpu.SemaphoreType.DMA((3,)),
        ],
        cost_estimate=pl.CostEstimate(flops=0, bytes_accessed=1024, transcendentals=0),
        name="pack",
    )(*[pltpu.with_memory_space_constraint(array, pltpu.HBM) for array in (tokens, ids, scale)])


def added(*terms, kind=jnp.bfloat16):
    total = terms[0].astype(jnp.float32)
    for term in terms[1:]:
        total = total + term.astype(jnp.float32)
    return total.astype(kind)


def after(value, *others):
    return lax.optimization_barrier((value, *others))[0]


def dense_body(tokens, expert_ids, router_weights, w_gate, w_up, w_down):
    experts = lax.axis_size("expert")
    count = tokens.shape[0]
    rounds = experts // 4
    swap = functools.partial(lax.ppermute, axis_name="expert", perm=swap_pairs(experts))
    ring = functools.partial(lax.ppermute, axis_name="expert", perm=ring_pairs(experts, 1))
    home = functools.partial(lax.ppermute, axis_name="expert", perm=ring_pairs(experts, 1, 1))
    leap = functools.partial(lax.ppermute, axis_name="expert", perm=ring_pairs(experts, 2))
    own = lax.axis_index("expert").reshape(1)

    mine = pack(after(tokens, own), expert_ids, router_weights, experts)
    sibling = swap(mine)
    first, second = ring(mine), ring(sibling)
    gate_w, up_w = load_weights((after(w_gate, sibling), w_up))
    first = after(first, gate_w)
    down_w, = load_weights((after(w_down, first),))
    weights = [gate_w, up_w, down_w]
    run = lambda *blocks: run_expert(own, blocks, weights, experts, count)
    blocks = {}
    for step in range(1, rounds - 1):
        if step > 1:
            first, second = ring(first), ring(second)
        if step == 2:
            first = after(first, down_w)
        blocks[step] = (swap(first), swap(second), first, second)
    far = leap(first)
    both = ring(jnp.concatenate([first, second], 0))
    turned = lambda keep, keep_trail, send, send_trail: (keep_trail, keep, swap(send_trail), swap(send))
    sums = {2: run(after(blocks[2][0], *blocks[1][:2]), *blocks[2][1:])}
    far = after(far, sums[2][0])
    sums[2] = turned(*sums[2])
    send, = run(far)
    keep, = run(after(swap(far), send))
    lead, trail = [added(keep, swap(send))], []
    sent = run(after(both, lead[0]))
    sums[3] = turned(*run(after(swap(both), sent[0])), *sent)
    lead = [ring(lead[0])]
    for step in range(rounds - 1, 0, -1):
        if step == 2:
            lead = [after(lead[0], sums[1][0])]
        if step == 1:
            lead = [after(lead[0], kept)]
        keep_trail, keep, send_trail, send = sums[step]
        if step == 3:
            keep, lead = lax.optimization_barrier(added(keep, *lead, kind=jnp.float32)), []
        lead = [added(keep, send, *lead)]
        trail = [added(after(keep_trail, lead[0]), send_trail, *trail)]
        if step == 3:
            sums[1] = turned(*run(after(blocks[1][0], trail[0]), *blocks[1][1:]))
        if step == 2:
            kept, other = run(after(mine, trail[0]), sibling)
        lead, trail = [(ring if step > 1 else home)(lead[0])], [ring(trail[0])]
    near = lax.optimization_barrier(added(lead[0], kept, swap(other), kind=jnp.float32))
    return added(near, trail[0])


def solution(mesh):
    in_specs = (
        P(("parts", "expert", "dp"), None),
        P(("parts", "expert", "dp"), None),
        P(("parts", "expert", "dp"), None),
        P("expert", None, "dp"),
        P("expert", None, "dp"),
        P("expert", None, "dp"),
    )
    out_specs = P(("parts", "expert", "dp"), None)

    def whole(tokens, expert_ids, router_weights, w_gate, w_up, w_down):
        few = mesh.shape["dp"] == 1 and 2 * expert_ids.shape[1] >= mesh.shape["expert"]
        body = dense_body if few else routed_body
        return jax.shard_map(
            body, mesh=mesh, in_specs=in_specs, out_specs=out_specs, check_vma=False
        )(tokens, expert_ids, router_weights, w_gate, w_up, w_down)

    return whole
```

```python
import functools
import math

import jax
import jax.numpy as jnp
from jax import lax
from jax.experimental import pallas as pl
from jax.experimental.pallas import tpu as pltpu
from jax.sharding import PartitionSpec as P


def expert_rows(rows, gate_w, up_w, down_w):
    total = rows.shape[0]
    block = math.gcd(total, 128)
    pieces = []
    for index in range(total // block):
        block_rows = rows[index * block : (index + 1) * block]
        gate_val = jnp.dot(block_rows, gate_w, preferred_element_type=jnp.float32)
        up_val = jnp.dot(block_rows, up_w, preferred_element_type=jnp.float32)
        hidden = (jax.nn.silu(gate_val) * up_val).astype(jnp.bfloat16)
        pieces.append(
            lax.dot_general(
                hidden, down_w, (((1,), (1,)), ((), ())), preferred_element_type=jnp.float32
            )
        )
    return jnp.concatenate(pieces, 0)


def routed_body(tokens, expert_ids, router_weights, w_gate, w_up, w_down):
    tok_count, top = expert_ids.shape
    width = tokens.shape[1]
    experts = lax.axis_size("expert")
    cap = max(2, min(tok_count, 2 * tok_count * top // experts))
    slots_all = experts * cap
    flat_ids = expert_ids.reshape(-1)
    onehot = (flat_ids[:, None] == jnp.arange(experts, dtype=jnp.int32)[None, :]).astype(jnp.int32)
    before = jnp.cumsum(onehot, 0) - onehot
    position = jnp.sum(before * onehot, 1)
    slot = flat_ids * cap + position
    send = jnp.zeros((slots_all, width), jnp.bfloat16).at[slot].set(jnp.repeat(tokens, top, 0))
    send = send.reshape(experts, cap, width)
    arrived = lax.all_to_all(send, "expert", split_axis=0, concat_axis=0, tiled=True)
    packed = arrived.reshape(slots_all, width)
    result = expert_rows(
        packed,
        lax.all_gather(w_gate, "dp", axis=2, tiled=True)[0],
        lax.all_gather(w_up, "dp", axis=2, tiled=True)[0],
        lax.all_gather(w_down, "dp", axis=2, tiled=True)[0],
    )
    expert_out = result.astype(jnp.bfloat16)
    back = lax.all_to_all(
        expert_out.reshape(experts, cap, width), "expert", split_axis=0, concat_axis=0, tiled=True
    )
    picked = back.reshape(slots_all, width)[slot].reshape(tok_count, top, width)
    mixed = jnp.einsum("tk,tkd->td", router_weights, picked.astype(jnp.float32))
    return mixed.astype(jnp.bfloat16)


def ring_order(chips):
    half = chips // 2
    return [2 * row for row in range(half)] + [2 * row + 1 for row in reversed(range(half))]


def swap_pairs(experts):
    return [(index, index ^ 1) for index in range(experts)]


def ring_pairs(experts, places, cross=0):
    order = ring_order(experts // 2)
    count = len(order)
    pairs = []
    for place, chip in enumerate(order):
        pairs.append((2 * chip, 2 * order[(place + places) % count] + cross))
        pairs.append((2 * chip + 1, 2 * order[(place - places) % count] + 1 - cross))
    return pairs


def expert_kernel(experts, blocks, own_ref, *refs):
    gate_ref, up_ref, down_ref, *outs = refs[blocks:-2]
    rows_ref, hidden_ref = refs[-2:]
    width, ff = gate_ref.shape[1:]
    each = outs[0].shape[0]
    at = 0
    for block in refs[:blocks]:
        rows_ref[at : at + block.shape[0], :] = block[...]
        at += block.shape[0]
    step = math.gcd(ff, 256)
    for at in range(0, ff, step):
        part = slice(at, at + step)
        rows = rows_ref[:, :width]
        gate = jnp.dot(rows, gate_ref[0, :, part], preferred_element_type=jnp.float32)
        up = jnp.dot(rows, up_ref[0, :, part], preferred_element_type=jnp.float32)
        hidden_ref[:, part] = (gate / (1.0 + jnp.exp(-gate)) * up).astype(jnp.bfloat16)
    tail = rows_ref[:, width:].astype(jnp.float32)
    lane = lax.broadcasted_iota(jnp.int32, tail.shape, 1)
    own = own_ref[0]
    mine = (lane == own) | (lane == own + experts)
    weight = jnp.sum(jnp.where(mine, tail, 0.0), axis=1, keepdims=True)
    step = math.gcd(width, 512)
    for at in range(0, width, step):
        part = slice(at, at + step)
        out = lax.dot_general(
            hidden_ref[...], down_ref[0, part, :], (((1,), (1,)), ((), ())),
            preferred_element_type=jnp.float32,
        )
        out = (out * weight).astype(jnp.bfloat16)
        for number, target in enumerate(outs):
            target[:, part] = out[number * each : (number + 1) * each]


def run_expert(own, blocks, weights, experts, each):
    rows = sum(block.shape[0] for block in blocks)
    wide = blocks[0].shape[1]
    width, ff = weights[0].shape[1:]
    vmem = pl.BlockSpec(memory_space=pltpu.VMEM)
    return pl.pallas_call(
        functools.partial(expert_kernel, experts, len(blocks)),
        out_shape=[jax.ShapeDtypeStruct((each, width), jnp.bfloat16)] * (rows // each),
        in_specs=[pl.BlockSpec(memory_space=pltpu.SMEM)] + [vmem] * (len(blocks) + 3),
        out_specs=[vmem] * (rows // each),
        scratch_shapes=[pltpu.VMEM((rows, wide), jnp.bfloat16), pltpu.VMEM((rows, ff), jnp.bfloat16)],
        compiler_params=pltpu.CompilerParams(vmem_limit_bytes=16 << 20),
        cost_estimate=pl.CostEstimate(
            flops=rows * width, bytes_accessed=rows * width, transcendentals=0
        ),
        name="expert",
    )(own, *blocks, *weights)


def load_kernel(pieces, *refs):
    *arrays, done = refs
    count = len(arrays) // 2
    copies = []
    for source, target in zip(arrays[:count], arrays[count:]):
        depth = source.shape[1] // pieces
        for piece in range(pieces):
            part = pl.ds(piece * depth, depth)
            copies.append(
                pltpu.make_async_copy(source.at[:, part], target.at[:, part], done.at[len(copies)])
            )
    for copy in copies:
        copy.start()
    for copy in copies:
        copy.wait()


def load_weights(weights):
    pieces = math.gcd(weights[0].shape[1] // 16, 4)
    return pl.pallas_call(
        functools.partial(load_kernel, pieces),
        out_shape=[pltpu.VMEM(w.shape, w.dtype) for w in weights],
        in_specs=[pl.BlockSpec(memory_space=pltpu.HBM)] * len(weights),
        out_specs=[pl.BlockSpec(memory_space=pltpu.VMEM)] * len(weights),
        scratch_shapes=[pltpu.SemaphoreType.DMA((len(weights) * pieces,))],
        compiler_params=pltpu.CompilerParams(vmem_limit_bytes=16 << 20),
        cost_estimate=pl.CostEstimate(flops=0, bytes_accessed=1024, transcendentals=0),
        name="load",
    )(*[pltpu.with_memory_space_constraint(w, pltpu.HBM) for w in weights])


def pack_kernel(experts, tokens_ref, ids_ref, weights_ref, out_ref, own_ids, own_weights, done):
    count, width = tokens_ref.shape
    copies = [
        pltpu.make_async_copy(source, target, done.at[number])
        for number, (source, target) in enumerate(
            ((ids_ref, own_ids), (weights_ref, own_weights), (tokens_ref, out_ref.at[:, :width]))
        )
    ]
    for copy in copies:
        copy.start()
    copies[0].wait()
    copies[1].wait()
    ids = own_ids[...]
    scale = own_weights[...]
    number = lax.broadcasted_iota(jnp.int32, (experts, count), 0)
    weight = jnp.zeros((experts, count), jnp.float32)
    for choice in range(ids.shape[0]):
        weight += jnp.where(ids[choice : choice + 1] == number, scale[choice : choice + 1], 0.0)
    high = weight.astype(jnp.bfloat16).astype(jnp.float32)
    low = weight - high
    rest = jnp.zeros((128 - 2 * experts, count), jnp.float32)
    columns = jnp.concatenate([high, low, rest], 0)
    columns = jnp.concatenate([columns, jnp.zeros((128, 128 - count), jnp.float32)], 1)
    out_ref[:, width:] = columns.T[:count].astype(jnp.bfloat16)
    copies[2].wait()


def pack(tokens, expert_ids, router_weights, experts):
    count, width = tokens.shape
    ids, scale = expert_ids.T, router_weights.T
    return pl.pallas_call(
        functools.partial(pack_kernel, experts),
        out_shape=jax.ShapeDtypeStruct((count, width + 128), jnp.bfloat16),
        in_specs=[pl.BlockSpec(memory_space=pltpu.HBM)] * 3,
        out_specs=pl.BlockSpec(memory_space=pltpu.VMEM),
        scratch_shapes=[
            pltpu.VMEM(ids.shape, ids.dtype),
            pltpu.VMEM(scale.shape, scale.dtype),
            pltpu.SemaphoreType.DMA((3,)),
        ],
        cost_estimate=pl.CostEstimate(flops=0, bytes_accessed=1024, transcendentals=0),
        name="pack",
    )(*[pltpu.with_memory_space_constraint(array, pltpu.HBM) for array in (tokens, ids, scale)])


def added(*terms, kind=jnp.bfloat16):
    total = terms[0].astype(jnp.float32)
    for term in terms[1:]:
        total = total + term.astype(jnp.float32)
    return total.astype(kind)


def after(value, *others):
    return lax.optimization_barrier((value, *others))[0]


def dense_body(tokens, expert_ids, router_weights, w_gate, w_up, w_down):
    experts = lax.axis_size("expert")
    count = tokens.shape[0]
    rounds = experts // 4
    swap = functools.partial(lax.ppermute, axis_name="expert", perm=swap_pairs(experts))
    ring = functools.partial(lax.ppermute, axis_name="expert", perm=ring_pairs(experts, 1))
    pass_on = functools.partial(lax.ppermute, axis_name="expert", perm=ring_pairs(experts, -1, 1))
    home = functools.partial(lax.ppermute, axis_name="expert", perm=ring_pairs(experts, 1, 1))
    leap = functools.partial(lax.ppermute, axis_name="expert", perm=ring_pairs(experts, 2))
    own = lax.axis_index("expert").reshape(1)

    mine = pack(after(tokens, own), expert_ids, router_weights, experts)
    first, second = ring(mine), pass_on(mine)
    gate_w, up_w = load_weights((after(w_gate, mine), w_up))
    sibling = swap(mine)
    first = after(first, gate_w)
    down_w, = load_weights((after(w_down, first),))
    weights = [gate_w, up_w, down_w]
    run = lambda *blocks: run_expert(own, blocks, weights, experts, count)
    blocks = {}
    for step in range(1, rounds - 1):
        if step > 1:
            first, second = ring(first), ring(second)
        if step == 2:
            first = after(first, down_w, sibling)
        blocks[step] = (swap(after(first, second) if step == 2 else first), swap(second), first, second)
    far = leap(first)
    both = ring(jnp.concatenate([first, second], 0))
    turned = lambda keep, keep_trail, send, send_trail: (keep_trail, keep, swap(send_trail), swap(send))
    sums = {2: run(after(blocks[2][0], *blocks[1][:2]), *blocks[2][1:])}
    sums[1] = run(after(blocks[1][0], sums[2][0]), *blocks[1][1:])
    far = after(far, sums[1][0])
    sums[2], sums[1] = turned(*sums[2]), turned(*sums[1])
    keep, send = run(after(swap(far), *sums[2][2:]), far)
    lead, trail = [added(keep, swap(send))], []
    sums[3] = turned(*run(after(swap(both), lead[0]), both))
    lead = [ring(lead[0])]
    for step in range(rounds - 1, 0, -1):
        if step == 2:
            lead = [after(lead[0], kept)]
        keep_trail, keep, send_trail, send = sums[step]
        lead = [added(keep, send, *lead)]
        trail = [added(after(keep_trail, lead[0]), send_trail, *trail)]
        if step == 3:
            kept, other = run(after(mine, trail[0]), sibling)
        lead, trail = [(ring if step > 1 else home)(lead[0])], [ring(trail[0])]
    near = lax.optimization_barrier(added(lead[0], kept, swap(other), kind=jnp.float32))
    return added(near, trail[0])


def solution(mesh):
    in_specs = (
        P(("parts", "expert", "dp"), None),
        P(("parts", "expert", "dp"), None),
        P(("parts", "expert", "dp"), None),
        P("expert", None, "dp"),
        P("expert", None, "dp"),
        P("expert", None, "dp"),
    )
    out_specs = P(("parts", "expert", "dp"), None)

    def whole(tokens, expert_ids, router_weights, w_gate, w_up, w_down):
        few = mesh.shape["dp"] == 1 and 2 * expert_ids.shape[1] >= mesh.shape["expert"]
        body = dense_body if few else routed_body
        return jax.shard_map(
            body, mesh=mesh, in_specs=in_specs, out_specs=out_specs, check_vma=False
        )(tokens, expert_ids, router_weights, w_gate, w_up, w_down)

    return whole
```

```python
import functools
import math

import jax
import jax.numpy as jnp
from jax import lax
from jax.experimental import pallas as pl
from jax.experimental.pallas import tpu as pltpu
from jax.sharding import PartitionSpec as P


def expert_rows(rows, gate_w, up_w, down_w):
    total = rows.shape[0]
    block = math.gcd(total, 128)
    pieces = []
    for index in range(total // block):
        block_rows = rows[index * block : (index + 1) * block]
        gate_val = jnp.dot(block_rows, gate_w, preferred_element_type=jnp.float32)
        up_val = jnp.dot(block_rows, up_w, preferred_element_type=jnp.float32)
        hidden = (jax.nn.silu(gate_val) * up_val).astype(jnp.bfloat16)
        pieces.append(
            lax.dot_general(
                hidden, down_w, (((1,), (1,)), ((), ())), preferred_element_type=jnp.float32
            )
        )
    return jnp.concatenate(pieces, 0)


def routed_body(tokens, expert_ids, router_weights, w_gate, w_up, w_down):
    tok_count, top = expert_ids.shape
    width = tokens.shape[1]
    experts = lax.axis_size("expert")
    cap = max(2, min(tok_count, 2 * tok_count * top // experts))
    slots_all = experts * cap
    flat_ids = expert_ids.reshape(-1)
    onehot = (flat_ids[:, None] == jnp.arange(experts, dtype=jnp.int32)[None, :]).astype(jnp.int32)
    before = jnp.cumsum(onehot, 0) - onehot
    position = jnp.sum(before * onehot, 1)
    slot = flat_ids * cap + position
    send = jnp.zeros((slots_all, width), jnp.bfloat16).at[slot].set(jnp.repeat(tokens, top, 0))
    send = send.reshape(experts, cap, width)
    arrived = lax.all_to_all(send, "expert", split_axis=0, concat_axis=0, tiled=True)
    packed = arrived.reshape(slots_all, width)
    result = expert_rows(
        packed,
        lax.all_gather(w_gate, "dp", axis=2, tiled=True)[0],
        lax.all_gather(w_up, "dp", axis=2, tiled=True)[0],
        lax.all_gather(w_down, "dp", axis=2, tiled=True)[0],
    )
    expert_out = result.astype(jnp.bfloat16)
    back = lax.all_to_all(
        expert_out.reshape(experts, cap, width), "expert", split_axis=0, concat_axis=0, tiled=True
    )
    picked = back.reshape(slots_all, width)[slot].reshape(tok_count, top, width)
    mixed = jnp.einsum("tk,tkd->td", router_weights, picked.astype(jnp.float32))
    return mixed.astype(jnp.bfloat16)


def ring_order(chips):
    half = chips // 2
    return [2 * row for row in range(half)] + [2 * row + 1 for row in reversed(range(half))]


def swap_pairs(experts):
    return [(index, index ^ 1) for index in range(experts)]


def ring_pairs(experts, places, cross=0):
    order = ring_order(experts // 2)
    count = len(order)
    pairs = []
    for place, chip in enumerate(order):
        pairs.append((2 * chip, 2 * order[(place + places) % count] + cross))
        pairs.append((2 * chip + 1, 2 * order[(place - places) % count] + 1 - cross))
    return pairs


def expert_kernel(experts, blocks, own_ref, *refs):
    gate_ref, up_ref, down_ref, *outs = refs[blocks:-2]
    rows_ref, hidden_ref = refs[-2:]
    width, ff = gate_ref.shape[1:]
    each = outs[0].shape[0]
    at = 0
    for block in refs[:blocks]:
        rows_ref[at : at + block.shape[0], :] = block[...]
        at += block.shape[0]
    step = math.gcd(ff, 256)
    for at in range(0, ff, step):
        part = slice(at, at + step)
        rows = rows_ref[:, :width]
        gate = jnp.dot(rows, gate_ref[0, :, part], preferred_element_type=jnp.float32)
        up = jnp.dot(rows, up_ref[0, :, part], preferred_element_type=jnp.float32)
        hidden_ref[:, part] = (gate / (1.0 + jnp.exp(-gate)) * up).astype(jnp.bfloat16)
    tail = rows_ref[:, width:].astype(jnp.float32)
    lane = lax.broadcasted_iota(jnp.int32, tail.shape, 1)
    own = own_ref[0]
    mine = (lane == own) | (lane == own + experts)
    weight = jnp.sum(jnp.where(mine, tail, 0.0), axis=1, keepdims=True)
    step = math.gcd(width, 512)
    for at in range(0, width, step):
        part = slice(at, at + step)
        out = lax.dot_general(
            hidden_ref[...], down_ref[0, part, :], (((1,), (1,)), ((), ())),
            preferred_element_type=jnp.float32,
        )
        out = (out * weight).astype(jnp.bfloat16)
        for number, target in enumerate(outs):
            target[:, part] = out[number * each : (number + 1) * each]


def run_expert(own, blocks, weights, experts, each):
    rows = sum(block.shape[0] for block in blocks)
    wide = blocks[0].shape[1]
    width, ff = weights[0].shape[1:]
    vmem = pl.BlockSpec(memory_space=pltpu.VMEM)
    return pl.pallas_call(
        functools.partial(expert_kernel, experts, len(blocks)),
        out_shape=[jax.ShapeDtypeStruct((each, width), jnp.bfloat16)] * (rows // each),
        in_specs=[pl.BlockSpec(memory_space=pltpu.SMEM)] + [vmem] * (len(blocks) + 3),
        out_specs=[vmem] * (rows // each),
        scratch_shapes=[pltpu.VMEM((rows, wide), jnp.bfloat16), pltpu.VMEM((rows, ff), jnp.bfloat16)],
        compiler_params=pltpu.CompilerParams(vmem_limit_bytes=16 << 20),
        cost_estimate=pl.CostEstimate(
            flops=rows * width, bytes_accessed=rows * width, transcendentals=0
        ),
        name="expert",
    )(own, *blocks, *weights)


def load_kernel(pieces, *refs):
    *arrays, done = refs
    count = len(arrays) // 2
    copies = []
    for source, target in zip(arrays[:count], arrays[count:]):
        depth = source.shape[1] // pieces
        for piece in range(pieces):
            part = pl.ds(piece * depth, depth)
            copies.append(
                pltpu.make_async_copy(source.at[:, part], target.at[:, part], done.at[len(copies)])
            )
    for copy in copies:
        copy.start()
    for copy in copies:
        copy.wait()


def load_weights(weights):
    pieces = math.gcd(weights[0].shape[1] // 16, 4)
    return pl.pallas_call(
        functools.partial(load_kernel, pieces),
        out_shape=[pltpu.VMEM(w.shape, w.dtype) for w in weights],
        in_specs=[pl.BlockSpec(memory_space=pltpu.HBM)] * len(weights),
        out_specs=[pl.BlockSpec(memory_space=pltpu.VMEM)] * len(weights),
        scratch_shapes=[pltpu.SemaphoreType.DMA((len(weights) * pieces,))],
        compiler_params=pltpu.CompilerParams(vmem_limit_bytes=16 << 20),
        cost_estimate=pl.CostEstimate(flops=0, bytes_accessed=1024, transcendentals=0),
        name="load",
    )(*[pltpu.with_memory_space_constraint(w, pltpu.HBM) for w in weights])


def pack_kernel(experts, tokens_ref, ids_ref, weights_ref, out_ref, own_ids, own_weights, done):
    count, width = tokens_ref.shape
    copies = [
        pltpu.make_async_copy(source, target, done.at[number])
        for number, (source, target) in enumerate(
            ((ids_ref, own_ids), (weights_ref, own_weights), (tokens_ref, out_ref.at[:, :width]))
        )
    ]
    for copy in copies:
        copy.start()
    copies[0].wait()
    copies[1].wait()
    ids = own_ids[...]
    scale = own_weights[...]
    number = lax.broadcasted_iota(jnp.int32, (experts, count), 0)
    weight = jnp.zeros((experts, count), jnp.float32)
    for choice in range(ids.shape[0]):
        weight += jnp.where(ids[choice : choice + 1] == number, scale[choice : choice + 1], 0.0)
    high = weight.astype(jnp.bfloat16).astype(jnp.float32)
    low = weight - high
    rest = jnp.zeros((128 - 2 * experts, count), jnp.float32)
    columns = jnp.concatenate([high, low, rest], 0)
    columns = jnp.concatenate([columns, jnp.zeros((128, 128 - count), jnp.float32)], 1)
    out_ref[:, width:] = columns.T[:count].astype(jnp.bfloat16)
    copies[2].wait()


def pack(tokens, expert_ids, router_weights, experts):
    count, width = tokens.shape
    ids, scale = expert_ids.T, router_weights.T
    return pl.pallas_call(
        functools.partial(pack_kernel, experts),
        out_shape=jax.ShapeDtypeStruct((count, width + 128), jnp.bfloat16),
        in_specs=[pl.BlockSpec(memory_space=pltpu.HBM)] * 3,
        out_specs=pl.BlockSpec(memory_space=pltpu.VMEM),
        scratch_shapes=[
            pltpu.VMEM(ids.shape, ids.dtype),
            pltpu.VMEM(scale.shape, scale.dtype),
            pltpu.SemaphoreType.DMA((3,)),
        ],
        cost_estimate=pl.CostEstimate(flops=0, bytes_accessed=1024, transcendentals=0),
        name="pack",
    )(*[pltpu.with_memory_space_constraint(array, pltpu.HBM) for array in (tokens, ids, scale)])


def added(*terms, kind=jnp.bfloat16):
    total = terms[0].astype(jnp.float32)
    for term in terms[1:]:
        total = total + term.astype(jnp.float32)
    return total.astype(kind)


def after(value, *others):
    return lax.optimization_barrier((value, *others))[0]


def dense_body(tokens, expert_ids, router_weights, w_gate, w_up, w_down):
    experts = lax.axis_size("expert")
    count = tokens.shape[0]
    rounds = experts // 4
    swap = functools.partial(lax.ppermute, axis_name="expert", perm=swap_pairs(experts))
    ring = functools.partial(lax.ppermute, axis_name="expert", perm=ring_pairs(experts, 1))
    home = functools.partial(lax.ppermute, axis_name="expert", perm=ring_pairs(experts, 1, 1))
    leap = functools.partial(lax.ppermute, axis_name="expert", perm=ring_pairs(experts, 2))
    own = lax.axis_index("expert").reshape(1)

    mine = pack(after(tokens, own), expert_ids, router_weights, experts)
    sibling = swap(mine)
    first, second = ring(mine), ring(sibling)
    gate_w, up_w = load_weights((after(w_gate, sibling), w_up))
    first = after(first, gate_w)
    down_w, = load_weights((after(w_down, first),))
    weights = [gate_w, up_w, down_w]
    run = lambda *blocks: run_expert(own, blocks, weights, experts, count)
    blocks = {}
    for step in range(1, rounds - 1):
        if step > 1:
            first, second = ring(first), ring(second)
        if step == 2:
            first = after(first, down_w)
        blocks[step] = (swap(first), swap(second), first, second)
    far = leap(first)
    both = ring(jnp.concatenate([first, second], 0))
    turned = lambda keep, keep_trail, send, send_trail: (keep_trail, keep, swap(send_trail), swap(send))
    sums = {2: run(after(blocks[2][0], *blocks[1][:2]), *blocks[2][1:])}
    sums[1] = run(after(blocks[1][0], sums[2][0]), *blocks[1][1:])
    far = after(far, sums[1][0])
    sums[2], sums[1] = turned(*sums[2]), turned(*sums[1])
    keep, send = run(after(swap(far), *sums[2][2:]), far)
    lead, trail = [added(keep, swap(send))], []
    sums[3] = turned(*run(after(swap(both), lead[0]), both))
    lead = [ring(lead[0])]
    for step in range(rounds - 1, 0, -1):
        if step == 2:
            lead = [after(lead[0], kept)]
        keep_trail, keep, send_trail, send = sums[step]
        lead = [added(keep, send, *lead)]
        trail = [added(after(keep_trail, lead[0]), send_trail, *trail)]
        if step == 3:
            kept, other = run(after(mine, trail[0]), sibling)
        lead, trail = [(ring if step > 1 else home)(lead[0])], [ring(trail[0])]
    near = lax.optimization_barrier(added(lead[0], kept, swap(other), kind=jnp.float32))
    return added(near, trail[0])


def solution(mesh):
    in_specs = (
        P(("parts", "expert", "dp"), None),
        P(("parts", "expert", "dp"), None),
        P(("parts", "expert", "dp"), None),
        P("expert", None, "dp"),
        P("expert", None, "dp"),
        P("expert", None, "dp"),
    )
    out_specs = P(("parts", "expert", "dp"), None)

    def whole(tokens, expert_ids, router_weights, w_gate, w_up, w_down):
        few = mesh.shape["dp"] == 1 and 2 * expert_ids.shape[1] >= mesh.shape["expert"]
        body = dense_body if few else routed_body
        return jax.shard_map(
            body, mesh=mesh, in_specs=in_specs, out_specs=out_specs, check_vma=False
        )(tokens, expert_ids, router_weights, w_gate, w_up, w_down)

    return whole
```

```python
import functools
import math

import jax
import jax.numpy as jnp
from jax import lax
from jax.experimental import pallas as pl
from jax.experimental.pallas import tpu as pltpu
from jax.sharding import PartitionSpec as P


def expert_rows(rows, gate_w, up_w, down_w):
    total = rows.shape[0]
    block = math.gcd(total, 128)
    pieces = []
    for index in range(total // block):
        block_rows = rows[index * block : (index + 1) * block]
        gate_val = jnp.dot(block_rows, gate_w, preferred_element_type=jnp.float32)
        up_val = jnp.dot(block_rows, up_w, preferred_element_type=jnp.float32)
        hidden = (jax.nn.silu(gate_val) * up_val).astype(jnp.bfloat16)
        pieces.append(
            lax.dot_general(
                hidden, down_w, (((1,), (1,)), ((), ())), preferred_element_type=jnp.float32
            )
        )
    return jnp.concatenate(pieces, 0)


def routed_body(tokens, expert_ids, router_weights, w_gate, w_up, w_down):
    tok_count, top = expert_ids.shape
    width = tokens.shape[1]
    experts = lax.axis_size("expert")
    cap = max(2, min(tok_count, 2 * tok_count * top // experts))
    slots_all = experts * cap
    flat_ids = expert_ids.reshape(-1)
    onehot = (flat_ids[:, None] == jnp.arange(experts, dtype=jnp.int32)[None, :]).astype(jnp.int32)
    before = jnp.cumsum(onehot, 0) - onehot
    position = jnp.sum(before * onehot, 1)
    slot = flat_ids * cap + position
    send = jnp.zeros((slots_all, width), jnp.bfloat16).at[slot].set(jnp.repeat(tokens, top, 0))
    send = send.reshape(experts, cap, width)
    arrived = lax.all_to_all(send, "expert", split_axis=0, concat_axis=0, tiled=True)
    packed = arrived.reshape(slots_all, width)
    result = expert_rows(
        packed,
        lax.all_gather(w_gate, "dp", axis=2, tiled=True)[0],
        lax.all_gather(w_up, "dp", axis=2, tiled=True)[0],
        lax.all_gather(w_down, "dp", axis=2, tiled=True)[0],
    )
    expert_out = result.astype(jnp.bfloat16)
    back = lax.all_to_all(
        expert_out.reshape(experts, cap, width), "expert", split_axis=0, concat_axis=0, tiled=True
    )
    picked = back.reshape(slots_all, width)[slot].reshape(tok_count, top, width)
    mixed = jnp.einsum("tk,tkd->td", router_weights, picked.astype(jnp.float32))
    return mixed.astype(jnp.bfloat16)


def ring_order(chips):
    half = chips // 2
    return [2 * row for row in range(half)] + [2 * row + 1 for row in reversed(range(half))]


def swap_pairs(experts):
    return [(index, index ^ 1) for index in range(experts)]


def ring_pairs(experts, places, cross=0):
    order = ring_order(experts // 2)
    count = len(order)
    pairs = []
    for place, chip in enumerate(order):
        pairs.append((2 * chip, 2 * order[(place + places) % count] + cross))
        pairs.append((2 * chip + 1, 2 * order[(place - places) % count] + 1 - cross))
    return pairs


def expert_kernel(experts, blocks, own_ref, *refs):
    gate_ref, up_ref, down_ref, *outs = refs[blocks:-2]
    rows_ref, hidden_ref = refs[-2:]
    width, ff = gate_ref.shape[1:]
    each = outs[0].shape[0]
    at = 0
    for block in refs[:blocks]:
        rows_ref[at : at + block.shape[0], :] = block[...]
        at += block.shape[0]
    step = math.gcd(ff, 256)
    for at in range(0, ff, step):
        part = slice(at, at + step)
        rows = rows_ref[:, :width]
        gate = jnp.dot(rows, gate_ref[0, :, part], preferred_element_type=jnp.float32)
        up = jnp.dot(rows, up_ref[0, :, part], preferred_element_type=jnp.float32)
        hidden_ref[:, part] = (gate / (1.0 + jnp.exp(-gate)) * up).astype(jnp.bfloat16)
    tail = rows_ref[:, width:].astype(jnp.float32)
    lane = lax.broadcasted_iota(jnp.int32, tail.shape, 1)
    own = own_ref[0]
    mine = (lane == own) | (lane == own + experts)
    weight = jnp.sum(jnp.where(mine, tail, 0.0), axis=1, keepdims=True)
    step = math.gcd(width, 512)
    for at in range(0, width, step):
        part = slice(at, at + step)
        out = lax.dot_general(
            hidden_ref[...], down_ref[0, part, :], (((1,), (1,)), ((), ())),
            preferred_element_type=jnp.float32,
        )
        out = (out * weight).astype(jnp.bfloat16)
        for number, target in enumerate(outs):
            target[:, part] = out[number * each : (number + 1) * each]


def run_expert(own, blocks, weights, experts, each):
    rows = sum(block.shape[0] for block in blocks)
    wide = blocks[0].shape[1]
    width, ff = weights[0].shape[1:]
    vmem = pl.BlockSpec(memory_space=pltpu.VMEM)
    return pl.pallas_call(
        functools.partial(expert_kernel, experts, len(blocks)),
        out_shape=[jax.ShapeDtypeStruct((each, width), jnp.bfloat16)] * (rows // each),
        in_specs=[pl.BlockSpec(memory_space=pltpu.SMEM)] + [vmem] * (len(blocks) + 3),
        out_specs=[vmem] * (rows // each),
        scratch_shapes=[pltpu.VMEM((rows, wide), jnp.bfloat16), pltpu.VMEM((rows, ff), jnp.bfloat16)],
        compiler_params=pltpu.CompilerParams(vmem_limit_bytes=16 << 20),
        cost_estimate=pl.CostEstimate(
            flops=rows * width, bytes_accessed=rows * width, transcendentals=0
        ),
        name="expert",
    )(own, *blocks, *weights)


def load_kernel(pieces, *refs):
    *arrays, done = refs
    count = len(arrays) // 2
    copies = []
    for source, target in zip(arrays[:count], arrays[count:]):
        depth = source.shape[1] // pieces
        for piece in range(pieces):
            part = pl.ds(piece * depth, depth)
            copies.append(
                pltpu.make_async_copy(source.at[:, part], target.at[:, part], done.at[len(copies)])
            )
    for copy in copies:
        copy.start()
    for copy in copies:
        copy.wait()


def load_weights(weights):
    pieces = math.gcd(weights[0].shape[1] // 16, 16)
    return pl.pallas_call(
        functools.partial(load_kernel, pieces),
        out_shape=[pltpu.VMEM(w.shape, w.dtype) for w in weights],
        in_specs=[pl.BlockSpec(memory_space=pltpu.HBM)] * len(weights),
        out_specs=[pl.BlockSpec(memory_space=pltpu.VMEM)] * len(weights),
        scratch_shapes=[pltpu.SemaphoreType.DMA((len(weights) * pieces,))],
        compiler_params=pltpu.CompilerParams(vmem_limit_bytes=16 << 20),
        cost_estimate=pl.CostEstimate(flops=0, bytes_accessed=1024, transcendentals=0),
        name="load",
    )(*[pltpu.with_memory_space_constraint(w, pltpu.HBM) for w in weights])


def pack_kernel(experts, tokens_ref, ids_ref, weights_ref, out_ref, own_ids, own_weights, done):
    count, width = tokens_ref.shape
    copies = [
        pltpu.make_async_copy(source, target, done.at[number])
        for number, (source, target) in enumerate(
            ((ids_ref, own_ids), (weights_ref, own_weights), (tokens_ref, out_ref.at[:, :width]))
        )
    ]
    for copy in copies:
        copy.start()
    copies[0].wait()
    copies[1].wait()
    ids = own_ids[...]
    scale = own_weights[...]
    number = lax.broadcasted_iota(jnp.int32, (experts, count), 0)
    weight = jnp.zeros((experts, count), jnp.float32)
    for choice in range(ids.shape[0]):
        weight += jnp.where(ids[choice : choice + 1] == number, scale[choice : choice + 1], 0.0)
    high = weight.astype(jnp.bfloat16).astype(jnp.float32)
    low = weight - high
    rest = jnp.zeros((128 - 2 * experts, count), jnp.float32)
    columns = jnp.concatenate([high, low, rest], 0)
    columns = jnp.concatenate([columns, jnp.zeros((128, 128 - count), jnp.float32)], 1)
    out_ref[:, width:] = columns.T[:count].astype(jnp.bfloat16)
    copies[2].wait()


def pack(tokens, expert_ids, router_weights, experts):
    count, width = tokens.shape
    ids, scale = expert_ids.T, router_weights.T
    return pl.pallas_call(
        functools.partial(pack_kernel, experts),
        out_shape=jax.ShapeDtypeStruct((count, width + 128), jnp.bfloat16),
        in_specs=[pl.BlockSpec(memory_space=pltpu.HBM)] * 3,
        out_specs=pl.BlockSpec(memory_space=pltpu.VMEM),
        scratch_shapes=[
            pltpu.VMEM(ids.shape, ids.dtype),
            pltpu.VMEM(scale.shape, scale.dtype),
            pltpu.SemaphoreType.DMA((3,)),
        ],
        cost_estimate=pl.CostEstimate(flops=0, bytes_accessed=1024, transcendentals=0),
        name="pack",
    )(*[pltpu.with_memory_space_constraint(array, pltpu.HBM) for array in (tokens, ids, scale)])


def added(*terms, kind=jnp.bfloat16):
    total = terms[0].astype(jnp.float32)
    for term in terms[1:]:
        total = total + term.astype(jnp.float32)
    return total.astype(kind)


def after(value, *others):
    return lax.optimization_barrier((value, *others))[0]


def dense_body(tokens, expert_ids, router_weights, w_gate, w_up, w_down):
    experts = lax.axis_size("expert")
    count = tokens.shape[0]
    rounds = experts // 4
    swap = functools.partial(lax.ppermute, axis_name="expert", perm=swap_pairs(experts))
    ring = functools.partial(lax.ppermute, axis_name="expert", perm=ring_pairs(experts, 1))
    home = functools.partial(lax.ppermute, axis_name="expert", perm=ring_pairs(experts, 1, 1))
    leap = functools.partial(lax.ppermute, axis_name="expert", perm=ring_pairs(experts, 2))
    own = lax.axis_index("expert").reshape(1)

    mine = pack(after(tokens, own), expert_ids, router_weights, experts)
    sibling = swap(mine)
    first, second = ring(mine), ring(sibling)
    gate_w, up_w = load_weights((after(w_gate, sibling), w_up))
    first = after(first, gate_w)
    down_w, = load_weights((after(w_down, first),))
    weights = [gate_w, up_w, down_w]
    run = lambda *blocks: run_expert(own, blocks, weights, experts, count)
    blocks = {}
    for step in range(1, rounds - 1):
        if step > 1:
            first, second = ring(first), ring(second)
        if step == 2:
            first = after(first, down_w)
        blocks[step] = (swap(first), swap(second), first, second)
    far = leap(first)
    both = ring(jnp.concatenate([first, second], 0))
    turned = lambda keep, keep_trail, send, send_trail: (keep_trail, keep, swap(send_trail), swap(send))
    sums = {2: run(after(blocks[2][0], *blocks[1][:2]), *blocks[2][1:])}
    sums[1] = run(after(blocks[1][0], sums[2][0]), *blocks[1][1:])
    far = after(far, sums[1][0])
    sums[2], sums[1] = turned(*sums[2]), turned(*sums[1])
    keep, send = run(swap(far), far)
    lead, trail = [added(keep, swap(send))], []
    sums[3] = turned(*run(after(swap(both), lead[0], *sums[2][2:]), both))
    lead = [ring(lead[0])]
    for step in range(rounds - 1, 0, -1):
        if step == 2:
            lead = [after(lead[0], kept)]
        keep_trail, keep, send_trail, send = sums[step]
        lead = [added(keep, send, *lead)]
        trail = [added(after(keep_trail, lead[0]), send_trail, *trail)]
        if step == 3:
            kept, other = run(after(mine, trail[0]), sibling)
        lead, trail = [(ring if step > 1 else home)(lead[0])], [ring(trail[0])]
    near = lax.optimization_barrier(added(lead[0], kept, swap(other), kind=jnp.float32))
    return added(near, trail[0])


def solution(mesh):
    in_specs = (
        P(("parts", "expert", "dp"), None),
        P(("parts", "expert", "dp"), None),
        P(("parts", "expert", "dp"), None),
        P("expert", None, "dp"),
        P("expert", None, "dp"),
        P("expert", None, "dp"),
    )
    out_specs = P(("parts", "expert", "dp"), None)

    def whole(tokens, expert_ids, router_weights, w_gate, w_up, w_down):
        few = mesh.shape["dp"] == 1 and 2 * expert_ids.shape[1] >= mesh.shape["expert"]
        body = dense_body if few else routed_body
        return jax.shard_map(
            body, mesh=mesh, in_specs=in_specs, out_specs=out_specs, check_vma=False
        )(tokens, expert_ids, router_weights, w_gate, w_up, w_down)

    return whole
```

```python
import functools
import math

import jax
import jax.numpy as jnp
from jax import lax
from jax.experimental import pallas as pl
from jax.experimental.pallas import tpu as pltpu
from jax.sharding import PartitionSpec as P


def expert_rows(rows, gate_w, up_w, down_w):
    total = rows.shape[0]
    block = math.gcd(total, 128)
    pieces = []
    for index in range(total // block):
        block_rows = rows[index * block : (index + 1) * block]
        gate_val = jnp.dot(block_rows, gate_w, preferred_element_type=jnp.float32)
        up_val = jnp.dot(block_rows, up_w, preferred_element_type=jnp.float32)
        hidden = (jax.nn.silu(gate_val) * up_val).astype(jnp.bfloat16)
        pieces.append(
            lax.dot_general(
                hidden, down_w, (((1,), (1,)), ((), ())), preferred_element_type=jnp.float32
            )
        )
    return jnp.concatenate(pieces, 0)


def routed_body(tokens, expert_ids, router_weights, w_gate, w_up, w_down):
    tok_count, top = expert_ids.shape
    width = tokens.shape[1]
    experts = lax.axis_size("expert")
    cap = max(2, min(tok_count, 2 * tok_count * top // experts))
    slots_all = experts * cap
    flat_ids = expert_ids.reshape(-1)
    onehot = (flat_ids[:, None] == jnp.arange(experts, dtype=jnp.int32)[None, :]).astype(jnp.int32)
    before = jnp.cumsum(onehot, 0) - onehot
    position = jnp.sum(before * onehot, 1)
    slot = flat_ids * cap + position
    send = jnp.zeros((slots_all, width), jnp.bfloat16).at[slot].set(jnp.repeat(tokens, top, 0))
    send = send.reshape(experts, cap, width)
    arrived = lax.all_to_all(send, "expert", split_axis=0, concat_axis=0, tiled=True)
    packed = arrived.reshape(slots_all, width)
    result = expert_rows(
        packed,
        lax.all_gather(w_gate, "dp", axis=2, tiled=True)[0],
        lax.all_gather(w_up, "dp", axis=2, tiled=True)[0],
        lax.all_gather(w_down, "dp", axis=2, tiled=True)[0],
    )
    expert_out = result.astype(jnp.bfloat16)
    back = lax.all_to_all(
        expert_out.reshape(experts, cap, width), "expert", split_axis=0, concat_axis=0, tiled=True
    )
    picked = back.reshape(slots_all, width)[slot].reshape(tok_count, top, width)
    mixed = jnp.einsum("tk,tkd->td", router_weights, picked.astype(jnp.float32))
    return mixed.astype(jnp.bfloat16)


def ring_order(chips):
    half = chips // 2
    return [2 * row for row in range(half)] + [2 * row + 1 for row in reversed(range(half))]


def swap_pairs(experts):
    return [(index, index ^ 1) for index in range(experts)]


def ring_pairs(experts, places, cross=0):
    order = ring_order(experts // 2)
    count = len(order)
    pairs = []
    for place, chip in enumerate(order):
        pairs.append((2 * chip, 2 * order[(place + places) % count] + cross))
        pairs.append((2 * chip + 1, 2 * order[(place - places) % count] + 1 - cross))
    return pairs


def expert_kernel(experts, blocks, load, own_ref, *refs):
    copies = []
    if load:
        gate_ref, up_ref, source, *outs, down_ref = refs[blocks:-3]
        rows_ref, hidden_ref, done = refs[-3:]
        depth = source.shape[1] // load
        for piece in range(load):
            part = pl.ds(piece * depth, depth)
            copies.append(
                pltpu.make_async_copy(source.at[:, part], down_ref.at[:, part], done.at[piece])
            )
    else:
        gate_ref, up_ref, down_ref, *outs = refs[blocks:-2]
        rows_ref, hidden_ref = refs[-2:]
    for copy in copies:
        copy.start()
    width, ff = gate_ref.shape[1:]
    each = outs[0].shape[0]
    at = 0
    for block in refs[:blocks]:
        rows_ref[at : at + block.shape[0], :] = block[...]
        at += block.shape[0]
    step = math.gcd(ff, 256)
    for at in range(0, ff, step):
        part = slice(at, at + step)
        rows = rows_ref[:, :width]
        gate = jnp.dot(rows, gate_ref[0, :, part], preferred_element_type=jnp.float32)
        up = jnp.dot(rows, up_ref[0, :, part], preferred_element_type=jnp.float32)
        hidden_ref[:, part] = (gate / (1.0 + jnp.exp(-gate)) * up).astype(jnp.bfloat16)
    tail = rows_ref[:, width:].astype(jnp.float32)
    lane = lax.broadcasted_iota(jnp.int32, tail.shape, 1)
    own = own_ref[0]
    mine = (lane == own) | (lane == own + experts)
    weight = jnp.sum(jnp.where(mine, tail, 0.0), axis=1, keepdims=True)
    for copy in copies:
        copy.wait()
    step = math.gcd(width, 512)
    for at in range(0, width, step):
        part = slice(at, at + step)
        out = lax.dot_general(
            hidden_ref[...], down_ref[0, part, :], (((1,), (1,)), ((), ())),
            preferred_element_type=jnp.float32,
        )
        out = (out * weight).astype(jnp.bfloat16)
        for number, target in enumerate(outs):
            target[:, part] = out[number * each : (number + 1) * each]


def run_expert(own, blocks, weights, experts, each, load=False):
    rows = sum(block.shape[0] for block in blocks)
    wide = blocks[0].shape[1]
    width, ff = weights[0].shape[1:]
    vmem = pl.BlockSpec(memory_space=pltpu.VMEM)
    pieces = math.gcd(width // 16, 4) if load else 0
    gate_w, up_w, down_w = weights
    out_shape = [jax.ShapeDtypeStruct((each, width), jnp.bfloat16)] * (rows // each)
    scratch = [pltpu.VMEM((rows, wide), jnp.bfloat16), pltpu.VMEM((rows, ff), jnp.bfloat16)]
    place = vmem
    if load:
        out_shape.append(pltpu.VMEM(down_w.shape, down_w.dtype))
        scratch.append(pltpu.SemaphoreType.DMA((pieces,)))
        place = pl.BlockSpec(memory_space=pltpu.HBM)
        down_w = pltpu.with_memory_space_constraint(down_w, pltpu.HBM)
    return pl.pallas_call(
        functools.partial(expert_kernel, experts, len(blocks), pieces),
        out_shape=out_shape,
        in_specs=[pl.BlockSpec(memory_space=pltpu.SMEM)] + [vmem] * (len(blocks) + 2) + [place],
        out_specs=[vmem] * len(out_shape),
        scratch_shapes=scratch,
        compiler_params=pltpu.CompilerParams(vmem_limit_bytes=16 << 20),
        cost_estimate=pl.CostEstimate(
            flops=rows * width, bytes_accessed=rows * width, transcendentals=0
        ),
        name="expert",
    )(own, *blocks, gate_w, up_w, down_w)


def load_kernel(pieces, *refs):
    *arrays, done = refs
    count = len(arrays) // 2
    copies = []
    for source, target in zip(arrays[:count], arrays[count:]):
        depth = source.shape[1] // pieces
        for piece in range(pieces):
            part = pl.ds(piece * depth, depth)
            copies.append(
                pltpu.make_async_copy(source.at[:, part], target.at[:, part], done.at[len(copies)])
            )
    for copy in copies:
        copy.start()
    for copy in copies:
        copy.wait()


def load_weights(weights):
    pieces = math.gcd(weights[0].shape[1] // 16, 4)
    return pl.pallas_call(
        functools.partial(load_kernel, pieces),
        out_shape=[pltpu.VMEM(w.shape, w.dtype) for w in weights],
        in_specs=[pl.BlockSpec(memory_space=pltpu.HBM)] * len(weights),
        out_specs=[pl.BlockSpec(memory_space=pltpu.VMEM)] * len(weights),
        scratch_shapes=[pltpu.SemaphoreType.DMA((len(weights) * pieces,))],
        compiler_params=pltpu.CompilerParams(vmem_limit_bytes=16 << 20),
        cost_estimate=pl.CostEstimate(flops=0, bytes_accessed=1024, transcendentals=0),
        name="load",
    )(*[pltpu.with_memory_space_constraint(w, pltpu.HBM) for w in weights])


def pack_kernel(experts, tokens_ref, ids_ref, weights_ref, out_ref, own_ids, own_weights, done):
    count, width = tokens_ref.shape
    copies = [
        pltpu.make_async_copy(source, target, done.at[number])
        for number, (source, target) in enumerate(
            ((ids_ref, own_ids), (weights_ref, own_weights), (tokens_ref, out_ref.at[:, :width]))
        )
    ]
    for copy in copies:
        copy.start()
    copies[0].wait()
    copies[1].wait()
    ids = own_ids[...]
    scale = own_weights[...]
    number = lax.broadcasted_iota(jnp.int32, (experts, count), 0)
    weight = jnp.zeros((experts, count), jnp.float32)
    for choice in range(ids.shape[0]):
        weight += jnp.where(ids[choice : choice + 1] == number, scale[choice : choice + 1], 0.0)
    high = weight.astype(jnp.bfloat16).astype(jnp.float32)
    low = weight - high
    rest = jnp.zeros((128 - 2 * experts, count), jnp.float32)
    columns = jnp.concatenate([high, low, rest], 0)
    columns = jnp.concatenate([columns, jnp.zeros((128, 128 - count), jnp.float32)], 1)
    out_ref[:, width:] = columns.T[:count].astype(jnp.bfloat16)
    copies[2].wait()


def pack(tokens, expert_ids, router_weights, experts):
    count, width = tokens.shape
    ids, scale = expert_ids.T, router_weights.T
    return pl.pallas_call(
        functools.partial(pack_kernel, experts),
        out_shape=jax.ShapeDtypeStruct((count, width + 128), jnp.bfloat16),
        in_specs=[pl.BlockSpec(memory_space=pltpu.HBM)] * 3,
        out_specs=pl.BlockSpec(memory_space=pltpu.VMEM),
        scratch_shapes=[
            pltpu.VMEM(ids.shape, ids.dtype),
            pltpu.VMEM(scale.shape, scale.dtype),
            pltpu.SemaphoreType.DMA((3,)),
        ],
        cost_estimate=pl.CostEstimate(flops=0, bytes_accessed=1024, transcendentals=0),
        name="pack",
    )(*[pltpu.with_memory_space_constraint(array, pltpu.HBM) for array in (tokens, ids, scale)])


def added(*terms, kind=jnp.bfloat16):
    total = terms[0].astype(jnp.float32)
    for term in terms[1:]:
        total = total + term.astype(jnp.float32)
    return total.astype(kind)


def after(value, *others):
    return lax.optimization_barrier((value, *others))[0]


def dense_body(tokens, expert_ids, router_weights, w_gate, w_up, w_down):
    experts = lax.axis_size("expert")
    count = tokens.shape[0]
    rounds = experts // 4
    swap = functools.partial(lax.ppermute, axis_name="expert", perm=swap_pairs(experts))
    ring = functools.partial(lax.ppermute, axis_name="expert", perm=ring_pairs(experts, 1))
    home = functools.partial(lax.ppermute, axis_name="expert", perm=ring_pairs(experts, 1, 1))
    leap = functools.partial(lax.ppermute, axis_name="expert", perm=ring_pairs(experts, 2))
    own = lax.axis_index("expert").reshape(1)

    mine = pack(after(tokens, own), expert_ids, router_weights, experts)
    sibling = swap(mine)
    first, second = ring(mine), ring(sibling)
    gate_w, up_w = load_weights((after(w_gate, sibling), w_up))
    first = after(first, gate_w)
    weights = [gate_w, up_w, w_down]
    run = lambda *blocks: run_expert(own, blocks, weights, experts, count)
    blocks = {}
    for step in range(1, rounds - 1):
        if step > 1:
            first, second = ring(first), ring(second)
        blocks[step] = (swap(first), swap(second), first, second)
    far = leap(first)
    both = ring(jnp.concatenate([first, second], 0))
    turned = lambda keep, keep_trail, send, send_trail: (keep_trail, keep, swap(send_trail), swap(send))
    blocks[2] = (after(blocks[2][0], *blocks[1][:2]), *blocks[2][1:])
    *sums, down_w = run_expert(own, blocks[2], weights, experts, count, True)
    weights = [gate_w, up_w, down_w]
    sums = {2: sums}
    sums[1] = run(after(blocks[1][0], sums[2][0]), *blocks[1][1:])
    far = after(far, sums[1][0])
    sums[2], sums[1] = turned(*sums[2]), turned(*sums[1])
    keep, send = run(swap(far), far)
    lead, trail = [added(keep, swap(send))], []
    sums[3] = turned(*run(after(swap(both), lead[0], *sums[2][2:]), both))
    lead = [ring(lead[0])]
    for step in range(rounds - 1, 0, -1):
        if step == 2:
            lead = [after(lead[0], kept)]
        keep_trail, keep, send_trail, send = sums[step]
        lead = [added(keep, send, *lead)]
        trail = [added(after(keep_trail, lead[0]), send_trail, *trail)]
        if step == 3:
            kept, other = run(after(mine, trail[0]), sibling)
        lead, trail = [(ring if step > 1 else home)(lead[0])], [ring(trail[0])]
    near = lax.optimization_barrier(added(lead[0], kept, swap(other), kind=jnp.float32))
    return added(near, trail[0])


def solution(mesh):
    in_specs = (
        P(("parts", "expert", "dp"), None),
        P(("parts", "expert", "dp"), None),
        P(("parts", "expert", "dp"), None),
        P("expert", None, "dp"),
        P("expert", None, "dp"),
        P("expert", None, "dp"),
    )
    out_specs = P(("parts", "expert", "dp"), None)

    def whole(tokens, expert_ids, router_weights, w_gate, w_up, w_down):
        few = mesh.shape["dp"] == 1 and 2 * expert_ids.shape[1] >= mesh.shape["expert"]
        body = dense_body if few else routed_body
        return jax.shard_map(
            body, mesh=mesh, in_specs=in_specs, out_specs=out_specs, check_vma=False
        )(tokens, expert_ids, router_weights, w_gate, w_up, w_down)

    return whole
```

```python
import functools
import math

import jax
import jax.numpy as jnp
from jax import lax
from jax.experimental import pallas as pl
from jax.experimental.pallas import tpu as pltpu
from jax.sharding import PartitionSpec as P


def expert_rows(rows, gate_w, up_w, down_w):
    total = rows.shape[0]
    block = math.gcd(total, 128)
    pieces = []
    for index in range(total // block):
        block_rows = rows[index * block : (index + 1) * block]
        gate_val = jnp.dot(block_rows, gate_w, preferred_element_type=jnp.float32)
        up_val = jnp.dot(block_rows, up_w, preferred_element_type=jnp.float32)
        hidden = (jax.nn.silu(gate_val) * up_val).astype(jnp.bfloat16)
        pieces.append(
            lax.dot_general(
                hidden, down_w, (((1,), (1,)), ((), ())), preferred_element_type=jnp.float32
            )
        )
    return jnp.concatenate(pieces, 0)


def routed_body(tokens, expert_ids, router_weights, w_gate, w_up, w_down):
    tok_count, top = expert_ids.shape
    width = tokens.shape[1]
    experts = lax.axis_size("expert")
    cap = max(2, min(tok_count, 2 * tok_count * top // experts))
    slots_all = experts * cap
    flat_ids = expert_ids.reshape(-1)
    onehot = (flat_ids[:, None] == jnp.arange(experts, dtype=jnp.int32)[None, :]).astype(jnp.int32)
    before = jnp.cumsum(onehot, 0) - onehot
    position = jnp.sum(before * onehot, 1)
    slot = flat_ids * cap + position
    send = jnp.zeros((slots_all, width), jnp.bfloat16).at[slot].set(jnp.repeat(tokens, top, 0))
    send = send.reshape(experts, cap, width)
    arrived = lax.all_to_all(send, "expert", split_axis=0, concat_axis=0, tiled=True)
    packed = arrived.reshape(slots_all, width)
    result = expert_rows(
        packed,
        lax.all_gather(w_gate, "dp", axis=2, tiled=True)[0],
        lax.all_gather(w_up, "dp", axis=2, tiled=True)[0],
        lax.all_gather(w_down, "dp", axis=2, tiled=True)[0],
    )
    expert_out = result.astype(jnp.bfloat16)
    back = lax.all_to_all(
        expert_out.reshape(experts, cap, width), "expert", split_axis=0, concat_axis=0, tiled=True
    )
    picked = back.reshape(slots_all, width)[slot].reshape(tok_count, top, width)
    mixed = jnp.einsum("tk,tkd->td", router_weights, picked.astype(jnp.float32))
    return mixed.astype(jnp.bfloat16)


def ring_order(chips):
    half = chips // 2
    return [2 * row for row in range(half)] + [2 * row + 1 for row in reversed(range(half))]


def swap_pairs(experts):
    return [(index, index ^ 1) for index in range(experts)]


def ring_pairs(experts, places, cross=0):
    order = ring_order(experts // 2)
    count = len(order)
    pairs = []
    for place, chip in enumerate(order):
        pairs.append((2 * chip, 2 * order[(place + places) % count] + cross))
        pairs.append((2 * chip + 1, 2 * order[(place - places) % count] + 1 - cross))
    return pairs


def expert_kernel(experts, blocks, load, own_ref, *refs):
    copies = []
    if load:
        gate_ref, up_ref, source, *outs, down_ref = refs[blocks:-3]
        rows_ref, hidden_ref, done = refs[-3:]
        depth = source.shape[1] // load
        for piece in range(load):
            part = pl.ds(piece * depth, depth)
            copies.append(
                pltpu.make_async_copy(source.at[:, part], down_ref.at[:, part], done.at[piece])
            )
    else:
        gate_ref, up_ref, down_ref, *outs = refs[blocks:-2]
        rows_ref, hidden_ref = refs[-2:]
    for copy in copies:
        copy.start()
    width, ff = gate_ref.shape[1:]
    each = outs[0].shape[0]
    at = 0
    for block in refs[:blocks]:
        rows_ref[at : at + block.shape[0], :] = block[...]
        at += block.shape[0]
    step = math.gcd(ff, 256)
    for at in range(0, ff, step):
        part = slice(at, at + step)
        rows = rows_ref[:, :width]
        gate = jnp.dot(rows, gate_ref[0, :, part], preferred_element_type=jnp.float32)
        up = jnp.dot(rows, up_ref[0, :, part], preferred_element_type=jnp.float32)
        hidden_ref[:, part] = (gate / (1.0 + jnp.exp(-gate)) * up).astype(jnp.bfloat16)
    tail = rows_ref[:, width:].astype(jnp.float32)
    lane = lax.broadcasted_iota(jnp.int32, tail.shape, 1)
    own = own_ref[0]
    mine = (lane == own) | (lane == own + experts)
    weight = jnp.sum(jnp.where(mine, tail, 0.0), axis=1, keepdims=True)
    for copy in copies:
        copy.wait()
    step = math.gcd(width, 512)
    for at in range(0, width, step):
        part = slice(at, at + step)
        out = lax.dot_general(
            hidden_ref[...], down_ref[0, part, :], (((1,), (1,)), ((), ())),
            preferred_element_type=jnp.float32,
        )
        out = (out * weight).astype(jnp.bfloat16)
        for number, target in enumerate(outs):
            target[:, part] = out[number * each : (number + 1) * each]


def run_expert(own, blocks, weights, experts, each, load=False):
    rows = sum(block.shape[0] for block in blocks)
    wide = blocks[0].shape[1]
    width, ff = weights[0].shape[1:]
    vmem = pl.BlockSpec(memory_space=pltpu.VMEM)
    pieces = math.gcd(width // 16, 4) if load else 0
    gate_w, up_w, down_w = weights
    out_shape = [jax.ShapeDtypeStruct((each, width), jnp.bfloat16)] * (rows // each)
    scratch = [pltpu.VMEM((rows, wide), jnp.bfloat16), pltpu.VMEM((rows, ff), jnp.bfloat16)]
    place = vmem
    if load:
        out_shape.append(pltpu.VMEM(down_w.shape, down_w.dtype))
        scratch.append(pltpu.SemaphoreType.DMA((pieces,)))
        place = pl.BlockSpec(memory_space=pltpu.HBM)
        down_w = pltpu.with_memory_space_constraint(down_w, pltpu.HBM)
    return pl.pallas_call(
        functools.partial(expert_kernel, experts, len(blocks), pieces),
        out_shape=out_shape,
        in_specs=[pl.BlockSpec(memory_space=pltpu.SMEM)] + [vmem] * (len(blocks) + 2) + [place],
        out_specs=[vmem] * len(out_shape),
        scratch_shapes=scratch,
        compiler_params=pltpu.CompilerParams(vmem_limit_bytes=16 << 20),
        cost_estimate=pl.CostEstimate(
            flops=rows * width, bytes_accessed=rows * width, transcendentals=0
        ),
        name="expert",
    )(own, *blocks, gate_w, up_w, down_w)


def load_kernel(pieces, *refs):
    *arrays, done = refs
    count = len(arrays) // 2
    copies = []
    for source, target in zip(arrays[:count], arrays[count:]):
        depth = source.shape[1] // pieces
        for piece in range(pieces):
            part = pl.ds(piece * depth, depth)
            copies.append(
                pltpu.make_async_copy(source.at[:, part], target.at[:, part], done.at[len(copies)])
            )
    for copy in copies:
        copy.start()
    for copy in copies:
        copy.wait()


def load_weights(weights):
    pieces = math.gcd(weights[0].shape[1] // 16, 4)
    return pl.pallas_call(
        functools.partial(load_kernel, pieces),
        out_shape=[pltpu.VMEM(w.shape, w.dtype) for w in weights],
        in_specs=[pl.BlockSpec(memory_space=pltpu.HBM)] * len(weights),
        out_specs=[pl.BlockSpec(memory_space=pltpu.VMEM)] * len(weights),
        scratch_shapes=[pltpu.SemaphoreType.DMA((len(weights) * pieces,))],
        compiler_params=pltpu.CompilerParams(vmem_limit_bytes=16 << 20),
        cost_estimate=pl.CostEstimate(flops=0, bytes_accessed=1024, transcendentals=0),
        name="load",
    )(*[pltpu.with_memory_space_constraint(w, pltpu.HBM) for w in weights])


def pack_kernel(experts, tokens_ref, ids_ref, weights_ref, out_ref, own_ids, own_weights, done):
    count, width = tokens_ref.shape
    copies = [
        pltpu.make_async_copy(source, target, done.at[number])
        for number, (source, target) in enumerate(
            ((ids_ref, own_ids), (weights_ref, own_weights), (tokens_ref, out_ref.at[:, :width]))
        )
    ]
    for copy in copies:
        copy.start()
    copies[0].wait()
    copies[1].wait()
    ids = own_ids[...]
    scale = own_weights[...]
    number = lax.broadcasted_iota(jnp.int32, (experts, count), 0)
    weight = jnp.zeros((experts, count), jnp.float32)
    for choice in range(ids.shape[0]):
        weight += jnp.where(ids[choice : choice + 1] == number, scale[choice : choice + 1], 0.0)
    high = weight.astype(jnp.bfloat16).astype(jnp.float32)
    low = weight - high
    rest = jnp.zeros((128 - 2 * experts, count), jnp.float32)
    columns = jnp.concatenate([high, low, rest], 0)
    columns = jnp.concatenate([columns, jnp.zeros((128, 128 - count), jnp.float32)], 1)
    out_ref[:, width:] = columns.T[:count].astype(jnp.bfloat16)
    copies[2].wait()


def pack(tokens, expert_ids, router_weights, experts):
    count, width = tokens.shape
    ids, scale = expert_ids.T, router_weights.T
    return pl.pallas_call(
        functools.partial(pack_kernel, experts),
        out_shape=jax.ShapeDtypeStruct((count, width + 128), jnp.bfloat16),
        in_specs=[pl.BlockSpec(memory_space=pltpu.HBM)] * 3,
        out_specs=pl.BlockSpec(memory_space=pltpu.VMEM),
        scratch_shapes=[
            pltpu.VMEM(ids.shape, ids.dtype),
            pltpu.VMEM(scale.shape, scale.dtype),
            pltpu.SemaphoreType.DMA((3,)),
        ],
        cost_estimate=pl.CostEstimate(flops=0, bytes_accessed=1024, transcendentals=0),
        name="pack",
    )(*[pltpu.with_memory_space_constraint(array, pltpu.HBM) for array in (tokens, ids, scale)])


def added(*terms, kind=jnp.bfloat16):
    total = terms[0].astype(jnp.float32)
    for term in terms[1:]:
        total = total + term.astype(jnp.float32)
    return total.astype(kind)


def after(value, *others):
    return lax.optimization_barrier((value, *others))[0]


def dense_body(tokens, expert_ids, router_weights, w_gate, w_up, w_down):
    experts = lax.axis_size("expert")
    count = tokens.shape[0]
    rounds = experts // 4
    swap = functools.partial(lax.ppermute, axis_name="expert", perm=swap_pairs(experts))
    ring = functools.partial(lax.ppermute, axis_name="expert", perm=ring_pairs(experts, 1))
    home = functools.partial(lax.ppermute, axis_name="expert", perm=ring_pairs(experts, 1, 1))
    leap = functools.partial(lax.ppermute, axis_name="expert", perm=ring_pairs(experts, 2))
    own = lax.axis_index("expert").reshape(1)

    mine = pack(after(tokens, own), expert_ids, router_weights, experts)
    sibling = swap(mine)
    first, second = ring(mine), ring(sibling)
    gate_w, up_w = load_weights((after(w_gate, sibling), w_up))
    first = after(first, gate_w)
    weights = [gate_w, up_w, w_down]
    run = lambda *blocks: run_expert(own, blocks, weights, experts, count)
    blocks = {}
    for step in range(1, rounds - 1):
        if step > 1:
            first, second = ring(first), ring(second)
        blocks[step] = (swap(first), swap(second), first, second)
    far = leap(first)
    both = ring(jnp.concatenate([first, second], 0))
    turned = lambda keep, keep_trail, send, send_trail: (keep_trail, keep, swap(send_trail), swap(send))
    blocks[2] = (after(blocks[2][0], *blocks[1][:2]), *blocks[2][1:])
    *sums, down_w = run_expert(own, blocks[2], weights, experts, count, True)
    weights = [gate_w, up_w, down_w]
    sums = {2: sums}
    far = after(far, sums[2][0])
    sums[2] = turned(*sums[2])
    keep, send = run(swap(far), far)
    lead, trail = [added(keep, swap(send))], []
    sums[3] = turned(*run(after(swap(both), lead[0], *sums[2][2:]), both))
    lead = [ring(lead[0])]
    for step in range(rounds - 1, 0, -1):
        if step == 2:
            lead = [after(lead[0], sums[1][0])]
        keep_trail, keep, send_trail, send = sums[step]
        lead = [added(keep, send, *lead)]
        trail = [added(after(keep_trail, lead[0]), send_trail, *trail)]
        if step == 3:
            sums[1] = turned(*run(after(blocks[1][0], trail[0]), *blocks[1][1:]))
        if step == 1:
            kept, other = run(after(mine, lead[0]), sibling)
        lead, trail = [(ring if step > 1 else home)(lead[0])], [ring(trail[0])]
    near = lax.optimization_barrier(added(lead[0], kept, swap(other), kind=jnp.float32))
    return added(near, trail[0])


def solution(mesh):
    in_specs = (
        P(("parts", "expert", "dp"), None),
        P(("parts", "expert", "dp"), None),
        P(("parts", "expert", "dp"), None),
        P("expert", None, "dp"),
        P("expert", None, "dp"),
        P("expert", None, "dp"),
    )
    out_specs = P(("parts", "expert", "dp"), None)

    def whole(tokens, expert_ids, router_weights, w_gate, w_up, w_down):
        few = mesh.shape["dp"] == 1 and 2 * expert_ids.shape[1] >= mesh.shape["expert"]
        body = dense_body if few else routed_body
        return jax.shard_map(
            body, mesh=mesh, in_specs=in_specs, out_specs=out_specs, check_vma=False
        )(tokens, expert_ids, router_weights, w_gate, w_up, w_down)

    return whole
```

```python
import functools
import math

import jax
import jax.numpy as jnp
from jax import lax
from jax.experimental import pallas as pl
from jax.experimental.pallas import tpu as pltpu
from jax.sharding import PartitionSpec as P


def expert_rows(rows, gate_w, up_w, down_w):
    total = rows.shape[0]
    block = math.gcd(total, 128)
    pieces = []
    for index in range(total // block):
        block_rows = rows[index * block : (index + 1) * block]
        gate_val = jnp.dot(block_rows, gate_w, preferred_element_type=jnp.float32)
        up_val = jnp.dot(block_rows, up_w, preferred_element_type=jnp.float32)
        hidden = (jax.nn.silu(gate_val) * up_val).astype(jnp.bfloat16)
        pieces.append(
            lax.dot_general(
                hidden, down_w, (((1,), (1,)), ((), ())), preferred_element_type=jnp.float32
            )
        )
    return jnp.concatenate(pieces, 0)


def routed_body(tokens, expert_ids, router_weights, w_gate, w_up, w_down):
    tok_count, top = expert_ids.shape
    width = tokens.shape[1]
    experts = lax.axis_size("expert")
    cap = max(2, min(tok_count, 2 * tok_count * top // experts))
    slots_all = experts * cap
    flat_ids = expert_ids.reshape(-1)
    onehot = (flat_ids[:, None] == jnp.arange(experts, dtype=jnp.int32)[None, :]).astype(jnp.int32)
    before = jnp.cumsum(onehot, 0) - onehot
    position = jnp.sum(before * onehot, 1)
    slot = flat_ids * cap + position
    send = jnp.zeros((slots_all, width), jnp.bfloat16).at[slot].set(jnp.repeat(tokens, top, 0))
    send = send.reshape(experts, cap, width)
    arrived = lax.all_to_all(send, "expert", split_axis=0, concat_axis=0, tiled=True)
    packed = arrived.reshape(slots_all, width)
    result = expert_rows(
        packed,
        lax.all_gather(w_gate, "dp", axis=2, tiled=True)[0],
        lax.all_gather(w_up, "dp", axis=2, tiled=True)[0],
        lax.all_gather(w_down, "dp", axis=2, tiled=True)[0],
    )
    expert_out = result.astype(jnp.bfloat16)
    back = lax.all_to_all(
        expert_out.reshape(experts, cap, width), "expert", split_axis=0, concat_axis=0, tiled=True
    )
    picked = back.reshape(slots_all, width)[slot].reshape(tok_count, top, width)
    mixed = jnp.einsum("tk,tkd->td", router_weights, picked.astype(jnp.float32))
    return mixed.astype(jnp.bfloat16)


def ring_order(chips):
    half = chips // 2
    return [2 * row for row in range(half)] + [2 * row + 1 for row in reversed(range(half))]


def swap_pairs(experts):
    return [(index, index ^ 1) for index in range(experts)]


def ring_pairs(experts, places, cross=0):
    order = ring_order(experts // 2)
    count = len(order)
    pairs = []
    for place, chip in enumerate(order):
        pairs.append((2 * chip, 2 * order[(place + places) % count] + cross))
        pairs.append((2 * chip + 1, 2 * order[(place - places) % count] + 1 - cross))
    return pairs


def expert_kernel(experts, blocks, own_ref, *refs):
    gate_ref, up_ref, down_ref, *outs = refs[blocks:-2]
    rows_ref, hidden_ref = refs[-2:]
    width, ff = gate_ref.shape[1:]
    each = outs[0].shape[0]
    at = 0
    for block in refs[:blocks]:
        rows_ref[at : at + block.shape[0], :] = block[...]
        at += block.shape[0]
    step = math.gcd(ff, 256)
    for at in range(0, ff, step):
        part = slice(at, at + step)
        rows = rows_ref[:, :width]
        gate = jnp.dot(rows, gate_ref[0, :, part], preferred_element_type=jnp.float32)
        up = jnp.dot(rows, up_ref[0, :, part], preferred_element_type=jnp.float32)
        hidden_ref[:, part] = (gate / (1.0 + jnp.exp(-gate)) * up).astype(jnp.bfloat16)
    tail = rows_ref[:, width:].astype(jnp.float32)
    lane = lax.broadcasted_iota(jnp.int32, tail.shape, 1)
    own = own_ref[0]
    mine = (lane == own) | (lane == own + experts)
    weight = jnp.sum(jnp.where(mine, tail, 0.0), axis=1, keepdims=True)
    step = math.gcd(width, 512)
    for at in range(0, width, step):
        part = slice(at, at + step)
        out = lax.dot_general(
            hidden_ref[...], down_ref[0, part, :], (((1,), (1,)), ((), ())),
            preferred_element_type=jnp.float32,
        )
        out = (out * weight).astype(jnp.bfloat16)
        for number, target in enumerate(outs):
            target[:, part] = out[number * each : (number + 1) * each]


def run_expert(own, blocks, weights, experts, each):
    rows = sum(block.shape[0] for block in blocks)
    wide = blocks[0].shape[1]
    width, ff = weights[0].shape[1:]
    vmem = pl.BlockSpec(memory_space=pltpu.VMEM)
    return pl.pallas_call(
        functools.partial(expert_kernel, experts, len(blocks)),
        out_shape=[jax.ShapeDtypeStruct((each, width), jnp.bfloat16)] * (rows // each),
        in_specs=[pl.BlockSpec(memory_space=pltpu.SMEM)] + [vmem] * (len(blocks) + 3),
        out_specs=[vmem] * (rows // each),
        scratch_shapes=[pltpu.VMEM((rows, wide), jnp.bfloat16), pltpu.VMEM((rows, ff), jnp.bfloat16)],
        compiler_params=pltpu.CompilerParams(vmem_limit_bytes=16 << 20),
        cost_estimate=pl.CostEstimate(
            flops=rows * width, bytes_accessed=rows * width, transcendentals=0
        ),
        name="expert",
    )(own, *blocks, *weights)


def load_kernel(pieces, *refs):
    *arrays, done = refs
    count = len(arrays) // 2
    copies = []
    for source, target in zip(arrays[:count], arrays[count:]):
        depth = source.shape[1] // pieces
        for piece in range(pieces):
            part = pl.ds(piece * depth, depth)
            copies.append(
                pltpu.make_async_copy(source.at[:, part], target.at[:, part], done.at[len(copies)])
            )
    for copy in copies:
        copy.start()
    for copy in copies:
        copy.wait()


def load_weights(weights):
    pieces = math.gcd(weights[0].shape[1] // 16, 4)
    return pl.pallas_call(
        functools.partial(load_kernel, pieces),
        out_shape=[pltpu.VMEM(w.shape, w.dtype) for w in weights],
        in_specs=[pl.BlockSpec(memory_space=pltpu.HBM)] * len(weights),
        out_specs=[pl.BlockSpec(memory_space=pltpu.VMEM)] * len(weights),
        scratch_shapes=[pltpu.SemaphoreType.DMA((len(weights) * pieces,))],
        compiler_params=pltpu.CompilerParams(vmem_limit_bytes=16 << 20),
        cost_estimate=pl.CostEstimate(flops=0, bytes_accessed=1024, transcendentals=0),
        name="load",
    )(*[pltpu.with_memory_space_constraint(w, pltpu.HBM) for w in weights])


def pack_kernel(experts, tokens_ref, ids_ref, weights_ref, out_ref, own_ids, own_weights, done):
    count, width = tokens_ref.shape
    copies = [
        pltpu.make_async_copy(source, target, done.at[number])
        for number, (source, target) in enumerate(
            ((ids_ref, own_ids), (weights_ref, own_weights), (tokens_ref, out_ref.at[:, :width]))
        )
    ]
    for copy in copies:
        copy.start()
    copies[0].wait()
    copies[1].wait()
    ids = own_ids[...]
    scale = own_weights[...]
    number = lax.broadcasted_iota(jnp.int32, (experts, count), 0)
    weight = jnp.zeros((experts, count), jnp.float32)
    for choice in range(ids.shape[0]):
        weight += jnp.where(ids[choice : choice + 1] == number, scale[choice : choice + 1], 0.0)
    high = weight.astype(jnp.bfloat16).astype(jnp.float32)
    low = weight - high
    rest = jnp.zeros((128 - 2 * experts, count), jnp.float32)
    columns = jnp.concatenate([high, low, rest], 0)
    columns = jnp.concatenate([columns, jnp.zeros((128, 128 - count), jnp.float32)], 1)
    out_ref[:, width:] = columns.T[:count].astype(jnp.bfloat16)
    copies[2].wait()


def pack(tokens, expert_ids, router_weights, experts):
    count, width = tokens.shape
    ids, scale = expert_ids.T, router_weights.T
    return pl.pallas_call(
        functools.partial(pack_kernel, experts),
        out_shape=jax.ShapeDtypeStruct((count, width + 128), jnp.bfloat16),
        in_specs=[pl.BlockSpec(memory_space=pltpu.HBM)] * 3,
        out_specs=pl.BlockSpec(memory_space=pltpu.VMEM),
        scratch_shapes=[
            pltpu.VMEM(ids.shape, ids.dtype),
            pltpu.VMEM(scale.shape, scale.dtype),
            pltpu.SemaphoreType.DMA((3,)),
        ],
        cost_estimate=pl.CostEstimate(flops=0, bytes_accessed=1024, transcendentals=0),
        name="pack",
    )(*[pltpu.with_memory_space_constraint(array, pltpu.HBM) for array in (tokens, ids, scale)])


def added(*terms, kind=jnp.bfloat16):
    total = terms[0].astype(jnp.float32)
    for term in terms[1:]:
        total = total + term.astype(jnp.float32)
    return total.astype(kind)


def after(value, *others):
    return lax.optimization_barrier((value, *others))[0]


def dense_body(tokens, expert_ids, router_weights, w_gate, w_up, w_down):
    experts = lax.axis_size("expert")
    count = tokens.shape[0]
    rounds = experts // 4
    swap = functools.partial(lax.ppermute, axis_name="expert", perm=swap_pairs(experts))
    ring = functools.partial(lax.ppermute, axis_name="expert", perm=ring_pairs(experts, 1))
    home = functools.partial(lax.ppermute, axis_name="expert", perm=ring_pairs(experts, 1, 1))
    leap = functools.partial(lax.ppermute, axis_name="expert", perm=ring_pairs(experts, 2))
    own = lax.axis_index("expert").reshape(1)

    mine = pack(after(tokens, own), expert_ids, router_weights, experts)
    sibling = swap(mine)
    first, second = ring(mine), ring(sibling)
    gate_w, up_w = load_weights((after(w_gate, sibling), w_up))
    first = after(first, gate_w)
    down_w, = load_weights((after(w_down, first),))
    weights = [gate_w, up_w, down_w]
    run = lambda *blocks: run_expert(own, blocks, weights, experts, count)
    blocks = {}
    for step in range(1, rounds - 1):
        if step > 1:
            first, second = ring(first), ring(second)
        if step == 2:
            first = after(first, down_w)
        blocks[step] = (swap(first), swap(second), first, second)
    far = leap(first)
    both = ring(jnp.concatenate([first, second], 0))
    turned = lambda keep, keep_trail, send, send_trail: (keep_trail, keep, swap(send_trail), swap(send))
    sums = {2: run(after(blocks[2][0], *blocks[1][:2]), *blocks[2][1:])}
    sums[1] = run(after(blocks[1][0], sums[2][0]), *blocks[1][1:])
    far = after(far, sums[1][0])
    sums[2], sums[1] = turned(*sums[2]), turned(*sums[1])
    keep, send = run(swap(far), far)
    lead, trail = [added(keep, swap(send))], []
    sums[3] = turned(*run(after(swap(both), lead[0], *sums[2][2:]), both))
    lead = [ring(lead[0])]
    for step in range(rounds - 1, 0, -1):
        if step == 2:
            lead = [after(lead[0], kept)]
        keep_trail, keep, send_trail, send = sums[step]
        lead = [added(keep, send, *lead)]
        trail = [added(after(keep_trail, lead[0]), send_trail, *trail)]
        if step == 3:
            kept, other = run(after(mine, trail[0]), sibling)
        lead, trail = [(ring if step > 1 else home)(lead[0])], [ring(trail[0])]
    near = lax.optimization_barrier(added(lead[0], kept, swap(other), kind=jnp.float32))
    return added(near, trail[0])


def solution(mesh):
    in_specs = (
        P(("parts", "expert", "dp"), None),
        P(("parts", "expert", "dp"), None),
        P(("parts", "expert", "dp"), None),
        P("expert", None, "dp"),
        P("expert", None, "dp"),
        P("expert", None, "dp"),
    )
    out_specs = P(("parts", "expert", "dp"), None)

    def whole(tokens, expert_ids, router_weights, w_gate, w_up, w_down):
        few = mesh.shape["dp"] == 1 and 2 * expert_ids.shape[1] >= mesh.shape["expert"]
        body = dense_body if few else routed_body
        return jax.shard_map(
            body, mesh=mesh, in_specs=in_specs, out_specs=out_specs, check_vma=False
        )(tokens, expert_ids, router_weights, w_gate, w_up, w_down)

    return whole
```

```python
import functools
import math

import jax
import jax.numpy as jnp
from jax import lax
from jax.experimental import pallas as pl
from jax.experimental.pallas import tpu as pltpu
from jax.sharding import PartitionSpec as P


def expert_rows(rows, gate_w, up_w, down_w):
    total = rows.shape[0]
    block = math.gcd(total, 128)
    pieces = []
    for index in range(total // block):
        block_rows = rows[index * block : (index + 1) * block]
        gate_val = jnp.dot(block_rows, gate_w, preferred_element_type=jnp.float32)
        up_val = jnp.dot(block_rows, up_w, preferred_element_type=jnp.float32)
        hidden = (jax.nn.silu(gate_val) * up_val).astype(jnp.bfloat16)
        pieces.append(
            lax.dot_general(
                hidden, down_w, (((1,), (1,)), ((), ())), preferred_element_type=jnp.float32
            )
        )
    return jnp.concatenate(pieces, 0)


def routed_body(tokens, expert_ids, router_weights, w_gate, w_up, w_down):
    tok_count, top = expert_ids.shape
    width = tokens.shape[1]
    experts = lax.axis_size("expert")
    cap = max(2, min(tok_count, 2 * tok_count * top // experts))
    slots_all = experts * cap
    flat_ids = expert_ids.reshape(-1)
    onehot = (flat_ids[:, None] == jnp.arange(experts, dtype=jnp.int32)[None, :]).astype(jnp.int32)
    before = jnp.cumsum(onehot, 0) - onehot
    position = jnp.sum(before * onehot, 1)
    slot = flat_ids * cap + position
    send = jnp.zeros((slots_all, width), jnp.bfloat16).at[slot].set(jnp.repeat(tokens, top, 0))
    send = send.reshape(experts, cap, width)
    arrived = lax.all_to_all(send, "expert", split_axis=0, concat_axis=0, tiled=True)
    packed = arrived.reshape(slots_all, width)
    result = expert_rows(
        packed,
        lax.all_gather(w_gate, "dp", axis=2, tiled=True)[0],
        lax.all_gather(w_up, "dp", axis=2, tiled=True)[0],
        lax.all_gather(w_down, "dp", axis=2, tiled=True)[0],
    )
    expert_out = result.astype(jnp.bfloat16)
    back = lax.all_to_all(
        expert_out.reshape(experts, cap, width), "expert", split_axis=0, concat_axis=0, tiled=True
    )
    picked = back.reshape(slots_all, width)[slot].reshape(tok_count, top, width)
    mixed = jnp.einsum("tk,tkd->td", router_weights, picked.astype(jnp.float32))
    return mixed.astype(jnp.bfloat16)


def ring_order(chips):
    half = chips // 2
    return [2 * row for row in range(half)] + [2 * row + 1 for row in reversed(range(half))]


def swap_pairs(experts):
    return [(index, index ^ 1) for index in range(experts)]


def ring_pairs(experts, places, cross=0):
    order = ring_order(experts // 2)
    count = len(order)
    pairs = []
    for place, chip in enumerate(order):
        pairs.append((2 * chip, 2 * order[(place + places) % count] + cross))
        pairs.append((2 * chip + 1, 2 * order[(place - places) % count] + 1 - cross))
    return pairs


def expert_kernel(experts, blocks, own_ref, *refs):
    gate_ref, up_ref, down_ref, *outs = refs[blocks:-2]
    rows_ref, hidden_ref = refs[-2:]
    width, ff = gate_ref.shape[1:]
    each = outs[0].shape[0]
    at = 0
    for block in refs[:blocks]:
        rows_ref[at : at + block.shape[0], :] = block[...]
        at += block.shape[0]
    step = math.gcd(ff, 256)
    for at in range(0, ff, step):
        part = slice(at, at + step)
        rows = rows_ref[:, :width]
        gate = jnp.dot(rows, gate_ref[0, :, part], preferred_element_type=jnp.float32)
        up = jnp.dot(rows, up_ref[0, :, part], preferred_element_type=jnp.float32)
        hidden_ref[:, part] = (gate / (1.0 + jnp.exp(-gate)) * up).astype(jnp.bfloat16)
    tail = rows_ref[:, width:].astype(jnp.float32)
    lane = lax.broadcasted_iota(jnp.int32, tail.shape, 1)
    own = own_ref[0]
    mine = (lane == own) | (lane == own + experts)
    weight = jnp.sum(jnp.where(mine, tail, 0.0), axis=1, keepdims=True)
    step = math.gcd(width, 512)
    for at in range(0, width, step):
        part = slice(at, at + step)
        out = lax.dot_general(
            hidden_ref[...], down_ref[0, part, :], (((1,), (1,)), ((), ())),
            preferred_element_type=jnp.float32,
        )
        out = (out * weight).astype(jnp.bfloat16)
        for number, target in enumerate(outs):
            target[:, part] = out[number * each : (number + 1) * each]


def run_expert(own, blocks, weights, experts, each):
    rows = sum(block.shape[0] for block in blocks)
    wide = blocks[0].shape[1]
    width, ff = weights[0].shape[1:]
    vmem = pl.BlockSpec(memory_space=pltpu.VMEM)
    return pl.pallas_call(
        functools.partial(expert_kernel, experts, len(blocks)),
        out_shape=[jax.ShapeDtypeStruct((each, width), jnp.bfloat16)] * (rows // each),
        in_specs=[pl.BlockSpec(memory_space=pltpu.SMEM)] + [vmem] * (len(blocks) + 3),
        out_specs=[vmem] * (rows // each),
        scratch_shapes=[pltpu.VMEM((rows, wide), jnp.bfloat16), pltpu.VMEM((rows, ff), jnp.bfloat16)],
        compiler_params=pltpu.CompilerParams(vmem_limit_bytes=16 << 20),
        cost_estimate=pl.CostEstimate(
            flops=rows * width, bytes_accessed=rows * width, transcendentals=0
        ),
        name="expert",
    )(own, *blocks, *weights)


def load_kernel(pieces, *refs):
    *arrays, done = refs
    count = len(arrays) // 2
    copies = []
    for source, target in zip(arrays[:count], arrays[count:]):
        depth = source.shape[1] // pieces
        for piece in range(pieces):
            part = pl.ds(piece * depth, depth)
            copies.append(
                pltpu.make_async_copy(source.at[:, part], target.at[:, part], done.at[len(copies)])
            )
    for copy in copies:
        copy.start()
    for copy in copies:
        copy.wait()


def load_weights(weights):
    pieces = math.gcd(weights[0].shape[1] // 16, 4)
    return pl.pallas_call(
        functools.partial(load_kernel, pieces),
        out_shape=[pltpu.VMEM(w.shape, w.dtype) for w in weights],
        in_specs=[pl.BlockSpec(memory_space=pltpu.HBM)] * len(weights),
        out_specs=[pl.BlockSpec(memory_space=pltpu.VMEM)] * len(weights),
        scratch_shapes=[pltpu.SemaphoreType.DMA((len(weights) * pieces,))],
        compiler_params=pltpu.CompilerParams(vmem_limit_bytes=16 << 20),
        cost_estimate=pl.CostEstimate(flops=0, bytes_accessed=1024, transcendentals=0),
        name="load",
    )(*[pltpu.with_memory_space_constraint(w, pltpu.HBM) for w in weights])


def pack_kernel(experts, tokens_ref, ids_ref, weights_ref, out_ref, own_ids, own_weights, done):
    count, width = tokens_ref.shape
    copies = [
        pltpu.make_async_copy(source, target, done.at[number])
        for number, (source, target) in enumerate(
            ((ids_ref, own_ids), (weights_ref, own_weights), (tokens_ref, out_ref.at[:, :width]))
        )
    ]
    for copy in copies:
        copy.start()
    copies[0].wait()
    copies[1].wait()
    ids = own_ids[...]
    scale = own_weights[...]
    number = lax.broadcasted_iota(jnp.int32, (experts, count), 0)
    weight = jnp.zeros((experts, count), jnp.float32)
    for choice in range(ids.shape[0]):
        weight += jnp.where(ids[choice : choice + 1] == number, scale[choice : choice + 1], 0.0)
    high = weight.astype(jnp.bfloat16).astype(jnp.float32)
    low = weight - high
    rest = jnp.zeros((128 - 2 * experts, count), jnp.float32)
    columns = jnp.concatenate([high, low, rest], 0)
    columns = jnp.concatenate([columns, jnp.zeros((128, 128 - count), jnp.float32)], 1)
    out_ref[:, width:] = columns.T[:count].astype(jnp.bfloat16)
    copies[2].wait()


def pack(tokens, expert_ids, router_weights, experts):
    count, width = tokens.shape
    ids, scale = expert_ids.T, router_weights.T
    return pl.pallas_call(
        functools.partial(pack_kernel, experts),
        out_shape=jax.ShapeDtypeStruct((count, width + 128), jnp.bfloat16),
        in_specs=[pl.BlockSpec(memory_space=pltpu.HBM)] * 3,
        out_specs=pl.BlockSpec(memory_space=pltpu.VMEM),
        scratch_shapes=[
            pltpu.VMEM(ids.shape, ids.dtype),
            pltpu.VMEM(scale.shape, scale.dtype),
            pltpu.SemaphoreType.DMA((3,)),
        ],
        cost_estimate=pl.CostEstimate(flops=0, bytes_accessed=1024, transcendentals=0),
        name="pack",
    )(*[pltpu.with_memory_space_constraint(array, pltpu.HBM) for array in (tokens, ids, scale)])


def added(*terms, kind=jnp.bfloat16):
    total = terms[0].astype(jnp.float32)
    for term in terms[1:]:
        total = total + term.astype(jnp.float32)
    return total.astype(kind)


def after(value, *others):
    return lax.optimization_barrier((value, *others))[0]


def dense_body(tokens, expert_ids, router_weights, w_gate, w_up, w_down):
    experts = lax.axis_size("expert")
    count = tokens.shape[0]
    rounds = experts // 4
    swap = functools.partial(lax.ppermute, axis_name="expert", perm=swap_pairs(experts))
    ring = functools.partial(lax.ppermute, axis_name="expert", perm=ring_pairs(experts, 1))
    home = functools.partial(lax.ppermute, axis_name="expert", perm=ring_pairs(experts, 1, 1))
    leap = functools.partial(lax.ppermute, axis_name="expert", perm=ring_pairs(experts, 2))
    own = lax.axis_index("expert").reshape(1)

    mine = pack(after(tokens, own), expert_ids, router_weights, experts)
    sibling = swap(mine)
    first, second = ring(mine), ring(sibling)
    gate_w, up_w = load_weights((after(w_gate, sibling), w_up))
    first = after(first, gate_w)
    down_w, = load_weights((after(w_down, first),))
    weights = [gate_w, up_w, down_w]
    run = lambda *blocks: run_expert(own, blocks, weights, experts, count)
    blocks = {}
    for step in range(1, rounds - 1):
        if step > 1:
            first, second = ring(first), ring(second)
        if step == 2:
            first = after(first, down_w)
        blocks[step] = (swap(first), swap(second), first, second)
    far = leap(first)
    both = ring(jnp.concatenate([first, second], 0))
    turned = lambda keep, keep_trail, send, send_trail: (keep_trail, keep, swap(send_trail), swap(send))
    sums = {2: run(after(blocks[2][0], *blocks[1][:2]), *blocks[2][1:])}
    sums[1] = run(after(blocks[1][0], sums[2][0]), *blocks[1][1:])
    far = after(far, sums[1][0])
    sums[2] = turned(*sums[2])
    keep, send = run(swap(far), far)
    lead, trail = [added(keep, swap(send))], []
    sums[3] = turned(*run(after(swap(both), lead[0], *sums[2][2:]), both))
    lead = [ring(lead[0])]
    for step in range(rounds - 1, 0, -1):
        if step == 2:
            lead = [after(lead[0], kept)]
        keep_trail, keep, send_trail, send = sums[step]
        lead = [added(keep, send, *lead)]
        trail = [added(after(keep_trail, lead[0]), send_trail, *trail)]
        if step == 3:
            kept, other = run(after(mine, trail[0]), sibling)
            sums[1] = turned(*sums[1][:2], *[after(sent, trail[0]) for sent in sums[1][2:]])
        lead, trail = [(ring if step > 1 else home)(lead[0])], [ring(trail[0])]
    near = lax.optimization_barrier(added(lead[0], kept, swap(other), kind=jnp.float32))
    return added(near, trail[0])


def solution(mesh):
    in_specs = (
        P(("parts", "expert", "dp"), None),
        P(("parts", "expert", "dp"), None),
        P(("parts", "expert", "dp"), None),
        P("expert", None, "dp"),
        P("expert", None, "dp"),
        P("expert", None, "dp"),
    )
    out_specs = P(("parts", "expert", "dp"), None)

    def whole(tokens, expert_ids, router_weights, w_gate, w_up, w_down):
        few = mesh.shape["dp"] == 1 and 2 * expert_ids.shape[1] >= mesh.shape["expert"]
        body = dense_body if few else routed_body
        return jax.shard_map(
            body, mesh=mesh, in_specs=in_specs, out_specs=out_specs, check_vma=False
        )(tokens, expert_ids, router_weights, w_gate, w_up, w_down)

    return whole
```
